32 devices in a mesh: rows: 4 (over y, core), batch: 8 (over z, x).
Axes of the slice: x: 2, y: 2, z: 4, core: 2. Of those that a mesh axis runs over, the one named last changes fastest.
Arguments:
- tokens: bfloat16 [64, 16, 64, 128], P('batch', 'rows'), may hold values from -6 to 6
- valid_rows: int32 [64], P('batch'), may hold values from 8 to 16, as said below
- valid_cols: int32 [64], P('batch'), may hold values from 32 to 64, as said below
- ln1_gain: float32 [128], replicated, may hold values from 0.25 to 1.75
- q_weight: bfloat16 [128, 128], replicated, may hold values from -0.5 to 0.5
- sr_weight: bfloat16 [2048, 128], replicated, may hold values from -0.125 to 0.125
- sr_gain: float32 [128], replicated, may hold values from 0.25 to 1.75
- kv_weight: bfloat16 [128, 256], replicated, may hold values from -0.5 to 0.5
- out_weight: bfloat16 [128, 128], replicated, may hold values from -1 to 1
- ln2_gain: float32 [128], replicated, may hold values from 0.25 to 1.75
- fc1_weight: bfloat16 [128, 1024], replicated, may hold values from -0.5 to 0.5
- dw_weight: bfloat16 [3, 3, 1024], replicated, may hold values from -2 to 2
- fc2_weight: bfloat16 [1024, 128], replicated, may hold values from -0.1875 to 0.1875
- cotangent: bfloat16 [64, 16, 64, 128], P('batch', 'rows'), may hold values from -6 to 6
Outputs:
- block_out: bfloat16 [64, 16, 64, 128], P('batch', 'rows')
- input_grad: bfloat16 [64, 16, 64, 128], P('batch', 'rows')
- ln1_gain_grad: float32 [128], replicated
- q_weight_grad: float32 [128, 128], replicated
- sr_weight_grad: float32 [2048, 128], replicated
- sr_gain_grad: float32 [128], replicated
- kv_weight_grad: float32 [128, 256], replicated
- out_weight_grad: float32 [128, 128], replicated
- ln2_gain_grad: float32 [128], replicated
- fc1_weight_grad: float32 [128, 1024], replicated
- dw_weight_grad: float32 [3, 3, 1024], replicated
- fc2_weight_grad: float32 [1024, 128], replicated
The draws below stay inside these ranges and needn't reach their ends.
Inputs may be any that keep to these rules, and one draw needn't show every extreme that they name: `valid_rows`: a multiple of 4; on each index b of batch one of the images 8 * b to 8 * b + 7, drawn from the seed, has all rows and all columns valid. `valid_cols`: a multiple of 4.
All inputs are finite; a program needn't handle non-finite values.
Results may differ from the reference program's by a relative error of at most 0.017.
Values may be sent and summed in bfloat16 or wider, within the bound.
No kernel may reach another device: no remote copies, remote signals or barrier semaphores. Data moves between devices by JAX's collectives and lax.ppermute only.
A program may use at most 128 MiB of HBM per device.

```python
import jax
import jax.numpy as jnp
from jax import lax

D = 128
FF = 1024
HEADS = 2
POOL = 4
W = 64
IMG_DEV = 8
HEAD_DIM = 64
HEIGHT = 16
IMAGES = 64
KEYS = 64
N_ROWS = 4
N_BATCH = 8


def full_slot(key):
    return jax.random.randint(jax.random.fold_in(key, 11), (N_BATCH,), 0, IMG_DEV)


def full_images(key):
    slots = full_slot(key)
    return jnp.arange(IMAGES) % IMG_DEV == jnp.repeat(slots, IMG_DEV)


def draw_valid_rows(key, part):
    chosen = full_images(key)
    key = jax.random.fold_in(key, 1)
    blocks = jax.random.randint(key, (IMAGES,), (N_ROWS + 1) // 2, N_ROWS + 1)
    return (jnp.where(chosen, N_ROWS, blocks) * POOL).astype(jnp.int32)


def draw_valid_cols(key, part):
    chosen = full_images(key)
    key = jax.random.fold_in(key, 2)
    blocks = jax.random.randint(key, (IMAGES,), (W // POOL + 1) // 2, W // POOL + 1)
    return (jnp.where(chosen, W // POOL, blocks) * POOL).astype(jnp.int32)


def block_scale(stream_key, dims, pieces, least, top_value):
    level = 1.0
    for position, blocks in pieces:
        draws = jax.random.uniform(jax.random.fold_in(jax.random.fold_in(stream_key, 6), position), (blocks,), jnp.float32, least / len(pieces), top_value / len(pieces))
        level = level * jnp.repeat(jnp.exp(draws), dims[position] // blocks).reshape((-1,) + (1,) * (len(dims) - 1 - position))
    return level


def centred(own_key, shape, scale, bound, pieces=(), kind=jnp.bfloat16):
    loudness = block_scale(own_key, shape, pieces, -0.22, 0.18) if pieces else 1.0
    drawn = jax.random.normal(own_key, shape, jnp.float32) * scale * loudness
    return jnp.minimum(jnp.maximum(drawn, -bound), bound).astype(kind)


def setup_inputs(seed: int = 0) -> dict:
    splits = jax.random.split(jax.random.key(seed), 15)
    tokens = centred(splits[0], (IMAGES, HEIGHT, W, D), 1.0, 6.0, ((0, 8), (1, 4)))
    valid_rows = draw_valid_rows(jax.random.fold_in(splits[14], 71), 0)
    valid_cols = draw_valid_cols(jax.random.fold_in(splits[14], 71), 0)
    ln1_gain = jnp.clip(1.0 + 0.15 * jax.random.normal(splits[3], (D,), jnp.float32), 0.25, 1.75)
    q_weight = centred(splits[4], (D, D), D ** -0.5, 0.5)
    sr_weight = centred(splits[5], (POOL * POOL * D, D), (POOL * POOL * D) ** -0.5, 0.125)
    sr_gain = jnp.clip(1.0 + 0.15 * jax.random.normal(splits[6], (D,), jnp.float32), 0.25, 1.75)
    kv_weight = centred(splits[7], (D, 2 * D), D ** -0.5, 0.5)
    out_weight = centred(splits[8], (D, D), (max(D * 16 // KEYS, 1)) ** -0.5, 1.0)
    ln2_gain = jnp.clip(1.0 + 0.15 * jax.random.normal(splits[9], (D,), jnp.float32), 0.25, 1.75)
    fc1_weight = centred(splits[10], (D, FF), D ** -0.5, 0.5)
    dw_weight = centred(splits[11], (3, 3, FF), 9 ** -0.5, 2.0)
    fc2_weight = centred(splits[12], (FF, D), FF ** -0.5, 0.1875)
    cotangent = centred(splits[13], (IMAGES, HEIGHT, W, D), 1.0, 6.0, ((0, 8), (1, 4)))
    return dict(tokens=tokens, valid_rows=valid_rows, valid_cols=valid_cols, ln1_gain=ln1_gain, q_weight=q_weight, sr_weight=sr_weight, sr_gain=sr_gain, kv_weight=kv_weight, out_weight=out_weight, ln2_gain=ln2_gain, fc1_weight=fc1_weight, dw_weight=dw_weight, fc2_weight=fc2_weight, cotangent=cotangent)


EPS = 1e-06
NEG = -1e+30

@jax.custom_vjp
def low(v):
    return lax.optimization_barrier(v.astype(jnp.bfloat16)).astype(jnp.float32)

@jax.custom_vjp
def low_back(v):
    return v

def low_keep(v):
    return (low(v), None)

def low_pass(kept, grad):
    return (grad,)

def back_keep(v):
    return (v, None)

def back_low(kept, grad):
    return (low(grad),)
low.defvjp(low_keep, low_pass)
low_back.defvjp(back_keep, back_low)

def layer_norm(source, gain):
    centered = source - lax.optimization_barrier(jnp.mean(source, axis=-1, keepdims=True))
    spread = lax.optimization_barrier(jnp.mean(centered * centered, axis=-1, keepdims=True))
    return centered * lax.rsqrt(spread + EPS) * gain

def matmul(left, right):
    return jnp.dot(left, right, precision=lax.Precision.HIGHEST, preferred_element_type=jnp.float32)

def depthwise(source, kernel):
    height, columns = (source.shape[0], source.shape[1])
    padded = jnp.pad(source, ((1, 1), (1, 1), (0, 0)))
    summed = jnp.zeros_like(source)
    for offset_row in range(3):
        for offset_col in range(3):
            summed = summed + padded[offset_row:offset_row + height, offset_col:offset_col + columns] * kernel[offset_row, offset_col]
    return summed

def forward(picture, row_count, col_count, params):
    ln1g, wq, wsr, srg, wkv, wout, ln2g, wfc1, wdw, wfc2 = params
    height, columns = (picture.shape[0], picture.shape[1])
    inside = ((jnp.arange(height)[:, None] < row_count) & (jnp.arange(columns)[None, :] < col_count)).astype(jnp.float32)[..., None]
    normed = low(layer_norm(picture, ln1g))
    queries = low_back(low(matmul(normed, wq)))
    masked = normed * inside
    patches = masked.reshape(height // POOL, POOL, columns // POOL, POOL, D).transpose(0, 2, 1, 3, 4).reshape(height // POOL, columns // POOL, POOL * POOL * D)
    pooled = low_back(matmul(patches, wsr))
    reduced = low(layer_norm(pooled, srg))
    key_value = low_back(low(matmul(reduced, wkv))).reshape(-1, 2 * D)
    key_live = ((jnp.arange(height // POOL)[:, None] * POOL < row_count) & (jnp.arange(columns // POOL)[None, :] * POOL < col_count)).reshape(-1)
    key_part = key_value[:, :D].reshape(-1, HEADS, HEAD_DIM)
    values = key_value[:, D:].reshape(-1, HEADS, HEAD_DIM)
    head_queries = queries.reshape(-1, HEADS, HEAD_DIM)
    scores = low_back(jnp.einsum('nhe,phe->hnp', head_queries, key_part, precision=lax.Precision.HIGHEST)) * HEAD_DIM ** (-0.5)
    scores = jnp.where(key_live[None, None, :], scores, NEG)
    probabilities = low(jax.nn.softmax(scores, axis=-1))
    attended = jnp.einsum('hnp,phe->nhe', probabilities, values, precision=lax.Precision.HIGHEST).reshape(height, columns, D)
    attended = low_back(low(attended * inside))
    middle = picture + low_back(matmul(attended, wout))
    normed2 = low(layer_norm(middle, ln2g))
    hidden = low(low_back(matmul(normed2, wfc1))) * inside
    convolved = low_back(depthwise(hidden, wdw))
    active = low(jax.nn.gelu(convolved, approximate=False))
    return middle + low_back(matmul(active, wfc2)) * inside

def reference(tokens, valid_rows, valid_cols, ln1_gain, q_weight, sr_weight, sr_gain, kv_weight, out_weight, ln2_gain, fc1_weight, dw_weight, fc2_weight, cotangent):
    params = tuple((weight.astype(jnp.float32) for weight in (ln1_gain, q_weight, sr_weight, sr_gain, kv_weight, out_weight, ln2_gain, fc1_weight, dw_weight, fc2_weight)))

    def one_image(running, record):
        picture, cotangent_one, row_count, col_count = record

        def apply_block(source, *weights):
            return forward(source, row_count, col_count, weights)
        result, pullback = jax.vjp(apply_block, picture, *params)
        gradients = pullback(cotangent_one)
        running = tuple((total + grad for total, grad in zip(running, gradients[1:])))
        return (running, (result, gradients[0]))
    zeros_all = tuple((jnp.zeros_like(weight) for weight in params))
    totals, (results, input_grads) = lax.scan(one_image, zeros_all, (tokens.astype(jnp.float32), cotangent.astype(jnp.float32), valid_rows, valid_cols))
    return (results.astype(jnp.bfloat16), input_grads.astype(jnp.bfloat16), totals[0], totals[1], totals[2], totals[3], totals[4], totals[5], totals[6], totals[7], totals[8], totals[9])
```

```python
import jax
import jax.numpy as jnp
from jax import lax
from jax.experimental import pallas as pl
from jax.experimental.pallas import tpu as pltpu
from jax.sharding import PartitionSpec as P

D = 128
FF = 1024
HEADS = 2
POOL = 4
HEAD_DIM = 64


EPS = 1e-06
NEG = -1e30


def padded_2(value, sides, width):
    for axis, dim in sides:
        size, length = (lax.axis_size(axis), value.shape[dim])
        up = [(i, (i + 1) % size) for i in range(size - 1)]
        down = [(j, i) for i, j in up]
        last = lax.slice_in_dim(value, length - width, length, axis=dim)
        first = lax.slice_in_dim(value, 0, width, axis=dim)
        before = lax.ppermute(last, axis, up)
        after = lax.ppermute(first, axis, down)
        value = jnp.concatenate([before, value, after], axis=dim)
    return value


def layer_norm(source, gain):
    centered = source - jnp.mean(source, axis=-1, keepdims=True)
    spread = jnp.mean(centered * centered, axis=-1, keepdims=True)
    return centered * lax.rsqrt(spread + EPS) * gain


def activate(source):
    return jax.nn.gelu(source, approximate=False)


def outer_product(left, right):
    return lax.dot_general(
        left.reshape(-1, left.shape[-1]),
        right.reshape(-1, right.shape[-1]),
        (((0,), (0,)), ((), ())),
        preferred_element_type=jnp.float32,
    )


def back_product(grad, weight):
    return lax.dot_general(
        grad, weight, (((grad.ndim - 1,), (1,)), ((), ())), preferred_element_type=jnp.float32
    )


def pad_columns(source):
    return jnp.pad(source, ((0, 0), (0, 0), (1, 1), (0, 0)))


def depth_conv(padded, kernel, count, columns):
    summed = jnp.zeros((padded.shape[0], count, columns, padded.shape[3]), jnp.float32)
    for offset_row in range(3):
        for offset_col in range(3):
            summed = (
                summed
                + padded[:, offset_row : offset_row + count, offset_col : offset_col + columns]
                * kernel[offset_row, offset_col]
            )
    return summed


def row_shards(
    tokens,
    valid_rows,
    valid_cols,
    ln1_gain,
    q_weight,
    sr_weight,
    sr_gain,
    kv_weight,
    out_weight,
    ln2_gain,
    fc1_weight,
    dw_weight,
    fc2_weight,
    cotangent,
):
    images = tokens.shape[0]
    columns = tokens.shape[2]
    groups = lax.axis_size("rows")
    score_scale = HEAD_DIM ** (-0.5)
    first_row = lax.axis_index("rows") * POOL
    ids = first_row + jnp.arange(POOL, dtype=jnp.int32)
    inside = (
        (ids[None, :, None] >= 0)
        & (ids[None, :, None] < valid_rows[:, None, None])
        & (jnp.arange(columns)[None, None, :] < valid_cols[:, None, None])
    )
    inside_float = inside.astype(jnp.float32)[..., None]
    key_live = (
        (jnp.arange(groups)[None, :, None] * POOL < valid_rows[:, None, None])
        & (jnp.arange(columns // POOL)[None, None, :] * POOL < valid_cols[:, None, None])
    ).reshape(images, -1)
    picture = tokens.astype(jnp.float32)
    normed, ln1_back = jax.vjp(layer_norm, picture, ln1_gain)
    normed_low = normed.astype(jnp.bfloat16)
    queries = jnp.dot(normed_low, q_weight, preferred_element_type=jnp.float32).astype(jnp.bfloat16)
    masked = jnp.where(inside[..., None], normed_low, 0)
    patches = (
        masked.reshape(images, POOL, columns // POOL, POOL, D)
        .transpose(0, 2, 1, 3, 4)
        .reshape(images, columns // POOL, POOL * POOL * D)
    )
    pooled = jnp.dot(patches, sr_weight, preferred_element_type=jnp.float32)
    reduced, sr_back = jax.vjp(layer_norm, pooled, sr_gain)
    reduced_low = reduced.astype(jnp.bfloat16)
    key_value = jnp.dot(reduced_low, kv_weight, preferred_element_type=jnp.float32).astype(
        jnp.bfloat16
    )
    gathered = lax.all_gather(key_value[:, None], "rows", axis=1, tiled=True).reshape(
        images, -1, 2 * D
    )
    key_part = gathered[..., :D].reshape(images, -1, HEADS, HEAD_DIM)
    value_part = gathered[..., D:].reshape(images, -1, HEADS, HEAD_DIM)
    head_queries = queries.reshape(images, -1, HEADS, HEAD_DIM)
    scores = (
        jnp.einsum("inhe,iphe->ihnp", head_queries, key_part, preferred_element_type=jnp.float32)
        * score_scale
    )
    scores = jnp.where(key_live[:, None, None, :], scores, NEG)
    probabilities = jax.nn.softmax(scores, axis=-1)
    probs_low = probabilities.astype(jnp.bfloat16)
    attended = jnp.einsum(
        "ihnp,iphe->inhe", probs_low, value_part, preferred_element_type=jnp.float32
    ).reshape(images, POOL, columns, D)
    attended_low = (attended * inside_float).astype(jnp.bfloat16)
    middle = picture + jnp.dot(attended_low, out_weight, preferred_element_type=jnp.float32)
    normed2, ln2_back = jax.vjp(layer_norm, middle, ln2_gain)
    normed2_low = normed2.astype(jnp.bfloat16)
    kernel = dw_weight.astype(jnp.float32)
    hidden_shape = (images, POOL, columns, FF)
    hidden = jnp.where(
        inside[..., None],
        jnp.dot(normed2_low, fc1_weight, preferred_element_type=jnp.float32).astype(jnp.bfloat16),
        0,
    )
    padded = pad_columns(padded_2(hidden, (("rows", 1),), 1))
    convolved = depth_conv(padded, kernel, POOL, columns)
    active, gelu_back = jax.vjp(activate, convolved)
    active_low = active.astype(jnp.bfloat16)
    block_out = (
        middle + jnp.dot(active_low, fc2_weight, preferred_element_type=jnp.float32) * inside_float
    ).astype(jnp.bfloat16)
    branch_grad = jnp.where(inside[..., None], cotangent, 0)
    fc2_grad = outer_product(active_low, branch_grad)
    active_grad = back_product(branch_grad, fc2_weight)
    (conv_grad,) = gelu_back(active_grad)
    conv_low = conv_grad.astype(jnp.bfloat16)
    grad_padded = pad_columns(padded_2(conv_low, (("rows", 1),), 1))
    hidden_grad = jnp.zeros(hidden_shape, jnp.float32)
    for offset_row in range(3):
        for offset_col in range(3):
            hidden_grad = (
                hidden_grad
                + grad_padded[
                    :,
                    2 - offset_row : 2 - offset_row + POOL,
                    2 - offset_col : 2 - offset_col + columns,
                ]
                * kernel[offset_row, offset_col]
            )
    dw_grad = jnp.stack(
        [
            jnp.stack(
                [
                    jnp.sum(
                        padded[:, offset_row : offset_row + POOL, offset_col : offset_col + columns]
                        * conv_low.astype(jnp.float32),
                        axis=(0, 1, 2),
                    )
                    for offset_col in range(3)
                ]
            )
            for offset_row in range(3)
        ]
    )
    hidden_low_grad = jnp.where(inside[..., None], hidden_grad, 0.0).astype(jnp.bfloat16)
    fc1_grad = outer_product(normed2_low, hidden_low_grad)
    normed2_grad = back_product(hidden_low_grad, fc1_weight)
    middle_back, ln2_gain_grad = ln2_back(normed2_grad)
    middle_grad = cotangent.astype(jnp.float32) + middle_back
    branch_low = middle_grad.astype(jnp.bfloat16)
    out_grad = outer_product(attended_low, branch_low)
    attended_grad = (
        jnp.where(inside[..., None], back_product(branch_low, out_weight), 0.0)
        .astype(jnp.bfloat16)
        .reshape(images, -1, HEADS, HEAD_DIM)
    )
    value_grad = jnp.einsum(
        "ihnp,inhe->iphe", probs_low, attended_grad, preferred_element_type=jnp.float32
    )
    prob_grad = jnp.einsum(
        "inhe,iphe->ihnp", attended_grad, value_part, preferred_element_type=jnp.float32
    )
    score_grad = (
        probabilities
        * (prob_grad - jnp.sum(probabilities * prob_grad, axis=-1, keepdims=True))
        * score_scale
    ).astype(jnp.bfloat16)
    query_grad = (
        jnp.einsum("ihnp,iphe->inhe", score_grad, key_part, preferred_element_type=jnp.float32)
        .astype(jnp.bfloat16)
        .reshape(images, POOL, columns, D)
    )
    key_grad = jnp.einsum(
        "ihnp,inhe->iphe", score_grad, head_queries, preferred_element_type=jnp.float32
    )
    pair_partial = jnp.concatenate(
        [key_grad.reshape(images, -1, D), value_grad.reshape(images, -1, D)], axis=-1
    ).reshape(images, groups, columns // POOL, 2 * D)
    pair_owned = lax.psum_scatter(pair_partial, "rows", scatter_dimension=1, tiled=True)
    pair_low = pair_owned[:, 0].astype(jnp.bfloat16)
    pair_weight_grad = outer_product(reduced_low, pair_low)
    reduced_grad = back_product(pair_low, kv_weight)
    pooled_grad, sr_gain_grad = sr_back(reduced_grad)
    pooled_low = pooled_grad.astype(jnp.bfloat16)
    sr_grad = outer_product(patches, pooled_low)
    patch_grad = (
        back_product(pooled_low, sr_weight)
        .reshape(images, columns // POOL, POOL, POOL, D)
        .transpose(0, 2, 1, 3, 4)
        .reshape(images, POOL, columns, D)
    )
    normed_grad = back_product(query_grad, q_weight) + jnp.where(inside[..., None], patch_grad, 0.0)
    q_grad = outer_product(normed_low, query_grad)
    picture_back, ln1_gain_grad = ln1_back(normed_grad)
    input_grad = (middle_grad + picture_back).astype(jnp.bfloat16)
    ln1_sum, q_sum, sr_sum, srg_sum, pair_sum, out_sum, ln2_sum, fc1_sum, dw_sum, fc2_sum = (
        lax.psum(
            (
                ln1_gain_grad,
                q_grad,
                sr_grad,
                sr_gain_grad,
                pair_weight_grad,
                out_grad,
                ln2_gain_grad,
                fc1_grad,
                dw_grad,
                fc2_grad,
            ),
            ("rows", "batch"),
        )
    )
    return (
        block_out,
        input_grad,
        ln1_sum,
        q_sum,
        sr_sum,
        srg_sum,
        pair_sum,
        out_sum,
        ln2_sum,
        fc1_sum,
        dw_sum,
        fc2_sum,
    )


VMEM = pltpu.VMEM
NT = (((1,), (1,)), ((), ()))
TN = (((0,), (0,)), ((), ()))


def mm(left, right):
    return jnp.dot(left, right, preferred_element_type=jnp.float32)


def mm_nt(left, right):
    return lax.dot_general(left, right, NT, preferred_element_type=jnp.float32)


def mm_tn(left, right):
    return lax.dot_general(left, right, TN, preferred_element_type=jnp.float32)


def norm_parts(source):
    centered = source - jnp.mean(source, axis=-1, keepdims=True)
    scale = lax.rsqrt(jnp.mean(centered * centered, axis=-1, keepdims=True) + EPS)
    return centered * scale, scale


def norm_back(grad, gain, unit, scale):
    scaled = grad * gain
    inner = jnp.mean(scaled * unit, axis=-1, keepdims=True)
    return scale * (scaled - jnp.mean(scaled, axis=-1, keepdims=True) - unit * inner)


def block_inside(first_row, rows, cols):
    row = first_row + lax.broadcasted_iota(jnp.int32, (4, 64, D), 0)
    col = lax.broadcasted_iota(jnp.int32, (4, 64, D), 1)
    return ((row < rows) & (col < cols)).reshape(256, D)


def halves(shape):
    return lax.broadcasted_iota(jnp.int32, shape, len(shape) - 1) < HEAD_DIM


def block_pair(source):
    left = halves(source.shape)
    zero = jnp.zeros_like(source)
    return jnp.concatenate([jnp.where(left, source, zero), jnp.where(left, zero, source)], axis=0)


def half_reduce(reducer, value, empty):
    left = halves(value.shape)
    first = reducer(jnp.where(left, value, empty), axis=-1, keepdims=True)
    second = reducer(jnp.where(left, empty, value), axis=-1, keepdims=True)
    return jnp.where(left, first, second)


def attend_kernel(
    place, vrows, vcols, own, near1, near2, near3, ln1, wq, wsr, srg, wkv, wout,
    x_out, normed_out, q_out, prob_out, att_out, mid_out, pat_out, pooled_out, kv_out, masked,
):
    me = place[0]
    for k, chunk in enumerate((own, near1, near2, near3)):
        block = me ^ k
        for i in range(2):
            raw = own[2 * me + i] if k == 0 else chunk[i]
            x_out[pl.ds(block * 4, 4), i] = raw
            unit, _ = norm_parts(raw.astype(jnp.float32).reshape(256, D))
            normed = (unit * ln1[...]).astype(jnp.bfloat16)
            normed_out[pl.ds(block * 4, 4), i] = normed.reshape(4, 64, D)
            inside = block_inside(block * 4, vrows[2 * me + i], vcols[2 * me + i])
            start = pl.multiple_of(i * 1024 + block * 256, 256)
            masked[pl.ds(start, 256), :] = jnp.where(inside, normed.astype(jnp.float32), 0.0)
    for i in range(2):
        for a in range(4):
            for u in range(4):
                for t in range(4):
                    piece = masked[pl.ds(i * 1024 + (4 * a + u) * 64 + t, 16, stride=4), :]
                    pat_out[pl.ds(i * 64 + a * 16, 16), pl.ds((u * 4 + t) * D, D)] = piece.astype(
                        jnp.bfloat16
                    )
    pooled = mm(pat_out[...], wsr[...])
    pooled_out[...] = pooled
    unit, _ = norm_parts(pooled)
    pairs = mm((unit * srg[...]).astype(jnp.bfloat16), wkv[...]).astype(jnp.bfloat16)
    kv_out[...] = pairs
    lane = lax.broadcasted_iota(jnp.int32, (1, D), 1) % 64
    for i in range(2):
        rows, cols = vrows[2 * me + i], vcols[2 * me + i]
        live = ((lane // 16) * 4 < rows) & ((lane % 16) * 4 < cols)
        keys = block_pair(pairs[i * 64 : i * 64 + 64, :D].astype(jnp.float32)).astype(jnp.bfloat16)
        values = block_pair(pairs[i * 64 : i * 64 + 64, D:].astype(jnp.float32)).astype(jnp.bfloat16)
        for b in range(4):
            part = pl.ds(b * 4, 4)
            query = mm(normed_out[part, i].reshape(256, D), wq[...]).astype(jnp.bfloat16)
            q_out[part, i] = query.reshape(4, 64, D)
            scores = jnp.where(live, mm_nt(query, keys) * SCORE_SCALE, NEG)
            weights = jnp.exp(scores - half_reduce(jnp.max, scores, -jnp.inf))
            probs = weights / half_reduce(jnp.sum, weights, 0.0)
            prob_out[part, i] = probs.reshape(4, 64, D)
            mixed = mm(probs.astype(jnp.bfloat16), values)
            mixed = jnp.where(block_inside(b * 4, rows, cols), mixed, 0.0).astype(jnp.bfloat16)
            att_out[part, i] = mixed.reshape(4, 64, D)
            middle = x_out[part, i].astype(jnp.float32).reshape(256, D) + mm(mixed, wout[...])
            mid_out[part, i] = middle.reshape(4, 64, D)


def gelu_parts(x):
    density = jnp.exp(x * x * -0.5) * 0.3989422804014327
    phi = 0.5 + 0.5 * lax.erf(x * 0.7071067811865476)
    return x * phi, phi + x * density


def feed_kernel(
    place, vrows, vcols, mid, cot, cot1, cot2, cot3, ln2, wfc1, wdw, wfc2,
    bo0, bo1, bo2, bo3, mg_out, send_out, keep_out,
    cj, br, br_t, wide, x_t, xcol, w9, cg, act, acc, stage, mask,
):
    me = place[0]
    zeros = jnp.zeros((128, 3 * D), jnp.bfloat16)
    wide[pl.ds(0, 128), :] = zeros
    wide[pl.ds(2176, 128), :] = zeros
    x_t[:, pl.ds(0, 128)] = jnp.zeros((3 * D, 128), jnp.bfloat16)
    x_t[:, pl.ds(2176, 128)] = jnp.zeros((3 * D, 128), jnp.bfloat16)
    cg[pl.ds(0, 128), :] = jnp.zeros((128, FF), jnp.bfloat16)
    cg[pl.ds(2176, 128), :] = jnp.zeros((128, FF), jnp.bfloat16)
    col = lax.broadcasted_iota(jnp.int32, (512, D), 0) % 64
    for k, chunk in enumerate((cot, cot1, cot2, cot3)):
        block = me ^ k
        for i in range(2):
            raw = cot[2 * me + i] if k == 0 else chunk[i]
            inside = block_inside(block * 4, vrows[2 * me + i], vcols[2 * me + i]).reshape(4, 64, D)
            for r in range(4):
                at = pl.ds(pl.multiple_of(block * 512 + r * 128 + i * 64, 64), 64)
                cj[at, :] = raw[r]
                mask[at, :] = jnp.where(inside[r], 1.0, 0.0)
    fc1_wide = wfc1[...].astype(jnp.float32)
    for tap in range(9):
        w9[pl.ds(tap * D, D), :] = (fc1_wide * wdw[pl.ds(tap, 1), :]).astype(jnp.bfloat16)
    for b in range(4):
        part = pl.ds(b * 512, 512)
        inside = mask[part, :]
        branch = cj[part, :].astype(jnp.float32) * inside
        br[part, :] = branch.astype(jnp.bfloat16)
        br_t[:, part] = branch.T.astype(jnp.bfloat16)
        unit, _ = norm_parts(mid[part, :])
        normed = ((unit * ln2[...]).astype(jnp.bfloat16)).astype(jnp.float32) * inside
        before = jnp.where(col == 0, 0.0, pltpu.roll(normed, 1, 0))
        after = jnp.where(col == 63, 0.0, pltpu.roll(normed, 511, 0))
        for s, value in enumerate((before, normed, after)):
            wide[pl.ds(b * 512 + 128, 512), pl.ds(s * D, D)] = value.astype(jnp.bfloat16)
            x_t[pl.ds(s * D, D), pl.ds(b * 512 + 128, 512)] = value.T.astype(jnp.bfloat16)
    for p in range(3):
        xcol[:, pl.ds(p * 3 * D, 3 * D)] = wide[pl.ds(p * 128, 2048), :]
    for f in range(FF // FC):
        chan = pl.ds(f * FC, FC)
        for b in range(2048 // TB):
            part = pl.ds(b * TB, TB)
            conv = mm(xcol[part, :], w9[:, chan])
            value, slope = gelu_parts(conv)
            low = value.astype(jnp.bfloat16)
            act[part, :] = low
            grad = mm_nt(br[part, :], wfc2[chan, :]) * slope
            cg[pl.ds(b * TB + 128, TB), chan] = grad.astype(jnp.bfloat16)
            if f == 0:
                acc[part, :] = mm(low, wfc2[chan, :])
            else:
                acc[part, :] += mm(low, wfc2[chan, :])
        fc2_grad = mm(br_t[...], act[...])
        stage[pl.ds(FF + f * FC, FC), :] = fc2_grad.T
        fc1_grad = jnp.zeros((D, FC), jnp.float32)
        grads = cg[pl.ds(128, 2048), chan]
        for p in range(3):
            outer = mm(x_t[:, pl.ds(p * 128, 2048)], grads)
            for s in range(3):
                tap = p * 3 + s
                here = outer[s * D : (s + 1) * D]
                fc1_grad += here * wdw[pl.ds(tap, 1), chan]
                dw_grad = jnp.sum(here * wfc1[:, chan].astype(jnp.float32), axis=0, keepdims=True)
                for j in range(FC // D):
                    stage[pl.ds(2 * FF + tap * 8 + f * (FC // D) + j, 1), :] = dw_grad[:, j * D : (j + 1) * D]
        for j in range(FC // D):
            stage[pl.ds((f * (FC // D) + j) * D, D), :] = fc1_grad[:, j * D : (j + 1) * D]
    gain_grad = jnp.zeros((1, D), jnp.float32)
    for k, bo in enumerate((bo0, bo1, bo2, bo3)):
        base = pl.multiple_of((me ^ k) * 512, 512)
        part = pl.ds(base, 512)
        inside = mask[part, :]
        middle = mid[part, :]
        result = (middle + acc[part, :] * inside).astype(jnp.bfloat16).reshape(4, 2, 64, D)
        for i in range(2):
            bo[i] = result[:, i]
        spread = jnp.zeros((512, 3 * D), jnp.float32)
        for p in range(3):
            rows = pl.ds(pl.multiple_of(base + (2 - p) * 128, 128), 512)
            spread += mm_nt(cg[rows, :], w9[pl.ds(p * 3 * D, 3 * D), :])
        after = jnp.where(col == 63, 0.0, pltpu.roll(spread[:, :D], 511, 0))
        before = jnp.where(col == 0, 0.0, pltpu.roll(spread[:, 2 * D :], 1, 0))
        normed_grad = (spread[:, D : 2 * D] + before + after) * inside
        unit, scale = norm_parts(middle)
        gain_grad += jnp.sum(normed_grad * unit, axis=0, keepdims=True)
        mg_out[part, :] = cj[part, :].astype(jnp.float32) + norm_back(normed_grad, ln2[...], unit, scale)
    stage[pl.ds(2 * FF + 72, 1), :] = gain_grad
    stage[pl.ds(2 * FF + 73, 55), :] = jnp.zeros((55, D), jnp.float32)
    split_pack(place, stage, send_out, keep_out)


def split_pack(place, stage, send_out, keep_out):
    rows = stage.shape[0] // 8
    for k in range(4):
        at = pl.ds(k * rows, rows)
        for out, core in ((send_out, 1 - place[1]), (keep_out, place[1])):
            start = pl.multiple_of((core * 4 + (place[2] ^ k)) * rows, 16)
            out[at, :] = stage[pl.ds(start, rows), :].astype(jnp.bfloat16)


def back_kernel(
    place, vrows, vcols, x, normed, query, prob, att, mgrad, pat, pooled, kv,
    ln1, wq, wsr, srg, wkv, wout,
    ig0, ig1, ig2, ig3, send_out, keep_out,
    stage, probs_low, att_grad, score_grad, query_grad, unfold,
):
    me = place[0]
    zero = jnp.zeros((D, D), jnp.float32)
    out_grad = zero
    key_rows = []
    for i in range(2):
        rows, cols = vrows[2 * me + i], vcols[2 * me + i]
        keys = block_pair(kv[pl.ds(i * 64, 64), pl.ds(0, D)].astype(jnp.float32)).astype(jnp.bfloat16)
        values = block_pair(kv[pl.ds(i * 64, 64), pl.ds(D, D)].astype(jnp.float32)).astype(jnp.bfloat16)
        for b in range(4):
            part = pl.ds(b * 4, 4)
            at = pl.ds(b * 256, 256)
            low = mgrad[part, i].reshape(256, D).astype(jnp.bfloat16)
            out_grad += mm_tn(att[part, i].reshape(256, D), low)
            mixed = jnp.where(block_inside(b * 4, rows, cols), mm_nt(low, wout[...]), 0.0).astype(jnp.bfloat16)
            att_grad[at, :] = mixed
            weights = prob[part, i].reshape(256, D)
            probs_low[at, :] = weights.astype(jnp.bfloat16)
            back = mm_nt(mixed, values)
            back = weights * (back - half_reduce(jnp.sum, weights * back, 0.0)) * SCORE_SCALE
            back = back.astype(jnp.bfloat16)
            score_grad[at, :] = back
            query_grad[pl.ds(i * 1024 + b * 256, 256), :] = mm(back, keys).astype(jnp.bfloat16)
        value_full = mm_tn(probs_low[...], att_grad[...])
        key_full = mm_tn(score_grad[...], query[:, i].reshape(1024, D))
        left = halves((64, D))
        key_rows.append(
            jnp.concatenate(
                [
                    jnp.where(left, key_full[:64], key_full[64:]),
                    jnp.where(left, value_full[:64], value_full[64:]),
                ],
                axis=1,
            )
        )
    pair = jnp.concatenate(key_rows, axis=0).astype(jnp.bfloat16)
    unit, scale = norm_parts(pooled[...])
    reduced = (unit * srg[...]).astype(jnp.bfloat16)
    kv_grad = mm_tn(reduced, pair)
    reduced_grad = mm_nt(pair, wkv[...])
    srg_grad = jnp.sum(reduced_grad * unit, axis=0, keepdims=True)
    pooled_low = norm_back(reduced_grad, srg[...], unit, scale).astype(jnp.bfloat16)
    stage[pl.ds(0, 2048), :] = mm_tn(pat[...], pooled_low)
    patch_grad = mm_nt(pooled_low, wsr[...])
    for i in range(2):
        for a in range(4):
            for u in range(4):
                for t in range(4):
                    unfold[pl.ds(i * 1024 + (4 * a + u) * 64 + t, 16, stride=4), :] = patch_grad[
                        i * 64 + a * 16 : i * 64 + a * 16 + 16, (u * 4 + t) * D : (u * 4 + t + 1) * D
                    ]
    stage[pl.ds(2048, D), :] = kv_grad[:, :D]
    stage[pl.ds(2176, D), :] = kv_grad[:, D:]
    stage[pl.ds(2432, D), :] = out_grad
    q_grad = zero
    gain_grad = jnp.zeros((1, D), jnp.float32)
    for k, ig in enumerate((ig0, ig1, ig2, ig3)):
        block = me ^ k
        part = pl.ds(block * 4, 4)
        for i in range(2):
            at = pl.ds(pl.multiple_of(i * 1024 + block * 256, 256), 256)
            inside = block_inside(block * 4, vrows[2 * me + i], vcols[2 * me + i])
            back = query_grad[at, :]
            q_grad += mm_tn(normed[part, i].reshape(256, D), back)
            grad = mm_nt(back, wq[...]) + jnp.where(inside, unfold[at, :], 0.0)
            unit, scale = norm_parts(x[part, i].astype(jnp.float32).reshape(256, D))
            gain_grad += jnp.sum(grad * unit, axis=0, keepdims=True)
            total = mgrad[part, i].reshape(256, D) + norm_back(grad, ln1[...], unit, scale)
            ig[i] = total.astype(jnp.bfloat16).reshape(4, 64, D)
    stage[pl.ds(2304, D), :] = q_grad
    stage[pl.ds(2560, 1), :] = gain_grad
    stage[pl.ds(2561, 1), :] = srg_grad
    stage[pl.ds(2562, 126), :] = jnp.zeros((126, D), jnp.float32)
    split_pack(place, stage, send_out, keep_out)


def call(kernel, scalars, arrays, outs, scratch, flops=0, name=None):
    spec = pl.BlockSpec(memory_space=VMEM)
    return pl.pallas_call(
        kernel,
        out_shape=[jax.ShapeDtypeStruct(shape, kind) for shape, kind in outs],
        in_specs=[pl.BlockSpec(memory_space=pltpu.SMEM)] * len(scalars) + [spec] * len(arrays),
        out_specs=[spec] * len(outs),
        scratch_shapes=scratch,
        compiler_params=pltpu.CompilerParams(vmem_limit_bytes=56 * 2**20),
        cost_estimate=pl.CostEstimate(flops=flops, bytes_accessed=4 * 2**20, transcendentals=0),
        name=name,
    )(*scalars, *arrays)


BF, F32 = jnp.bfloat16, jnp.float32
JOINT = (16, 2, 64, D)
CHUNK = (2, 4, 64, D)
PACK1, PACK2 = 2176, 2688
FC, TB = 256, 512
SCORE_SCALE = HEAD_DIM ** (-0.5)


def attend(place, vrows, vcols, chunks, ln1, wq, wsr, srg, wkv, wout):
    return call(
        attend_kernel,
        (place, vrows, vcols),
        (*chunks, ln1, wq, wsr, srg, wkv, wout),
        [
            (JOINT, BF), (JOINT, BF), (JOINT, BF), (JOINT, F32), (JOINT, BF), (JOINT, F32),
            ((128, 2048), BF), ((128, D), F32), ((128, 2 * D), BF),
        ],
        [VMEM((2048, D), F32)],
        flops=10**9, name="attend",
    )


def feed(place, vrows, vcols, middle, chunks, ln2, wfc1, wdw, wfc2):
    return call(
        feed_kernel,
        (place, vrows, vcols),
        (middle, *chunks, ln2, wfc1, wdw, wfc2),
        [(CHUNK, BF)] * 4 + [((2048, D), F32), ((PACK1 // 2, D), BF), ((PACK1 // 2, D), BF)],
        [
            VMEM((2048, D), BF), VMEM((2048, D), BF), VMEM((D, 2048), BF),
            VMEM((2304, 3 * D), BF), VMEM((3 * D, 2304), BF), VMEM((2048, 9 * D), BF),
            VMEM((9 * D, FF), BF), VMEM((2304, FF), BF), VMEM((2048, FC), BF),
            VMEM((2048, D), F32), VMEM((PACK1, D), F32), VMEM((2048, D), F32),
        ],
        flops=16 * 10**9, name="feed",
    )


def back(place, vrows, vcols, kept, mgrad, ln1, wq, wsr, srg, wkv, wout):
    x, normed, query, prob, att, _, pat, pooled, kv = kept
    return call(
        back_kernel,
        (place, vrows, vcols),
        (x, normed, query, prob, att, mgrad, pat, pooled, kv, ln1, wq, wsr, srg, wkv, wout),
        [(CHUNK, BF)] * 4 + [((PACK2 // 2, D), BF), ((PACK2 // 2, D), BF)],
        [
            VMEM((PACK2, D), F32), VMEM((1024, D), BF), VMEM((1024, D), BF), VMEM((1024, D), BF),
            VMEM((2048, D), BF), VMEM((2048, D), F32),
        ],
        flops=2 * 10**9, name="back",
    )


def swap(value, axes, partner):
    size = lax.axis_size(axes)
    return lax.ppermute(value, axes, [(i, partner(i)) for i in range(size)])


def over_rows(value, k):
    return swap(value, "rows", lambda i: i ^ k)


def over_plane(value, k):
    size = lax.axis_size("batch")
    return swap(value, ("rows", "batch"), lambda i: i ^ ((k >> 1) * 2 * size) ^ (k & 1))


def over_line(value, k):
    return swap(value, "batch", lambda i: i ^ (2 * k))


def plus(*values):
    return sum(v.astype(F32) for v in values).astype(BF)


def summed(send, keep):
    rows = send.shape[0] // 4
    both = plus(keep, over_rows(send, 1))
    parts = [both[k * rows : (k + 1) * rows] for k in range(4)]
    mine = plus(parts[0], *(over_plane(parts[k], k) for k in (1, 2, 3)))
    near, far, last = (over_line(mine, k).astype(F32) for k in (1, 2, 3))
    total = ((mine.astype(F32) + near) + (far + last)).astype(BF)
    pieces = [total] + [over_plane(total, k) for k in (1, 2, 3)]
    return pieces + [over_rows(piece, 1) for piece in pieces]


def finish_kernel(place, *refs):
    first, second = refs[:8], refs[8:16]
    q, sr, kv, out, fc1, dw, fc2, gains, stage1, stage2 = refs[16:]
    for pieces, stage in ((first, stage1), (second, stage2)):
        rows = stage.shape[0] // 8
        for j, piece in enumerate(pieces):
            core = place[1] if j < 4 else 1 - place[1]
            start = pl.multiple_of((core * 4 + (place[2] ^ (j % 4))) * rows, 16)
            stage[pl.ds(start, rows), :] = piece[...].astype(F32)
    for j in range(8):
        fc1[:, pl.ds(j * D, D)] = stage1[pl.ds(j * D, D), :]
    fc2[...] = stage1[pl.ds(FF, FF), :]
    dw[...] = stage1[pl.ds(2 * FF, 72), :]
    sr[...] = stage2[pl.ds(0, 2048), :]
    for j in range(2):
        kv[:, pl.ds(j * D, D)] = stage2[pl.ds(2048 + j * D, D), :]
    q[...] = stage2[pl.ds(2304, D), :]
    out[...] = stage2[pl.ds(2432, D), :]
    gains[pl.ds(0, 1), :] = stage1[pl.ds(2 * FF + 72, 1), :]
    gains[pl.ds(1, 1), :] = stage2[pl.ds(2560, 1), :]
    gains[pl.ds(2, 1), :] = stage2[pl.ds(2561, 1), :]
    gains[pl.ds(3, 5), :] = jnp.zeros((5, D), F32)


def finish(place, first, second):
    return call(
        finish_kernel,
        (place,),
        (*first, *second),
        [
            ((D, D), F32), ((2048, D), F32), ((D, 2 * D), F32), ((D, D), F32),
            ((D, FF), F32), ((72, D), F32), ((FF, D), F32), ((8, D), F32),
        ],
        [VMEM((PACK1, D), F32), VMEM((PACK2, D), F32)],
        name="finish",
    )


def gather_kernel(place, part0, part1, part2, part3, out):
    for k, part in enumerate((part0, part1, part2, part3)):
        out[pl.ds(2 * (place[0] ^ k), 2)] = part[...]


def gather_rows(place, parts, shape):
    (out,) = call(gather_kernel, (place,), parts, [(shape, BF)], [], name="gather_rows")
    return out


def image_shards(
    tokens, valid_rows, valid_cols, ln1_gain, q_weight, sr_weight, sr_gain, kv_weight, out_weight,
    ln2_gain, fc1_weight, dw_weight, fc2_weight, cotangent,
):
    me, lane = lax.axis_index("rows"), lax.axis_index("batch")
    place = jnp.stack([me, me & 1, (me >> 1) * 2 + (lane & 1), lane >> 1]).astype(jnp.int32)

    def spread(source):
        near = [
            over_rows(lax.dynamic_slice_in_dim(source, 2 * (me ^ k), 2, 0), k) for k in (1, 2, 3)
        ]
        return (source, *near)

    def returned(parts):
        return gather_rows(place, (parts[0], *(over_rows(parts[k], k) for k in (1, 2, 3))), tokens.shape)

    ln1, ln2, srg = (g.reshape(1, D) for g in (ln1_gain, ln2_gain, sr_gain))
    taps = jnp.pad(dw_weight.astype(F32).reshape(9, FF), ((0, 7), (0, 0)))
    kept = attend(
        place, valid_rows, valid_cols, spread(tokens), ln1, q_weight, sr_weight, srg, kv_weight, out_weight
    )
    *block_parts, mgrad, send1, keep1 = feed(
        place, valid_rows, valid_cols, kept[5].reshape(2048, D), spread(cotangent), ln2, fc1_weight, taps, fc2_weight
    )
    *input_parts, send2, keep2 = back(
        place, valid_rows, valid_cols, kept, mgrad.reshape(JOINT), ln1, q_weight, sr_weight, srg, kv_weight, out_weight
    )
    block_out = returned(block_parts)
    input_grad = returned(input_parts)
    q, sr, kv, out, fc1, dw, fc2, gains = finish(place, summed(send1, keep1), summed(send2, keep2))
    return (
        block_out, input_grad, gains[1], q, sr, gains[2], kv, out, gains[0], fc1, dw.reshape(3, 3, FF), fc2,
    )


def shards(*arrays):
    tokens = arrays[0]
    fits = (
        lax.axis_size("rows") == 4
        and lax.axis_size("batch") == 8
        and tokens.shape == (8, 4, 64, D)
    )
    return image_shards(*arrays) if fits else row_shards(*arrays)


def solution(mesh):
    placed = (
        P("batch", "rows", None, None),
        P("batch"),
        P("batch"),
        P(),
        P(),
        P(),
        P(),
        P(),
        P(),
        P(),
        P(),
        P(),
        P(),
        P("batch", "rows", None, None),
    )
    return jax.shard_map(
        shards,
        mesh=mesh,
        in_specs=placed,
        out_specs=(
            P("batch", "rows", None, None),
            P("batch", "rows", None, None),
            P(),
            P(),
            P(),
            P(),
            P(),
            P(),
            P(),
            P(),
            P(),
            P(),
        ),
        check_vma=False,
    )
```

```python
import jax
import jax.numpy as jnp
from jax import lax
from jax.experimental import pallas as pl
from jax.experimental.pallas import tpu as pltpu
from jax.sharding import PartitionSpec as P

D = 128
FF = 1024
HEADS = 2
POOL = 4
HEAD_DIM = 64


EPS = 1e-06
NEG = -1e30


def padded_2(value, sides, width):
    for axis, dim in sides:
        size, length = (lax.axis_size(axis), value.shape[dim])
        up = [(i, (i + 1) % size) for i in range(size - 1)]
        down = [(j, i) for i, j in up]
        last = lax.slice_in_dim(value, length - width, length, axis=dim)
        first = lax.slice_in_dim(value, 0, width, axis=dim)
        before = lax.ppermute(last, axis, up)
        after = lax.ppermute(first, axis, down)
        value = jnp.concatenate([before, value, after], axis=dim)
    return value


def layer_norm(source, gain):
    centered = source - jnp.mean(source, axis=-1, keepdims=True)
    spread = jnp.mean(centered * centered, axis=-1, keepdims=True)
    return centered * lax.rsqrt(spread + EPS) * gain


def activate(source):
    return jax.nn.gelu(source, approximate=False)


def outer_product(left, right):
    return lax.dot_general(
        left.reshape(-1, left.shape[-1]),
        right.reshape(-1, right.shape[-1]),
        (((0,), (0,)), ((), ())),
        preferred_element_type=jnp.float32,
    )


def back_product(grad, weight):
    return lax.dot_general(
        grad, weight, (((grad.ndim - 1,), (1,)), ((), ())), preferred_element_type=jnp.float32
    )


def pad_columns(source):
    return jnp.pad(source, ((0, 0), (0, 0), (1, 1), (0, 0)))


def depth_conv(padded, kernel, count, columns):
    summed = jnp.zeros((padded.shape[0], count, columns, padded.shape[3]), jnp.float32)
    for offset_row in range(3):
        for offset_col in range(3):
            summed = (
                summed
                + padded[:, offset_row : offset_row + count, offset_col : offset_col + columns]
                * kernel[offset_row, offset_col]
            )
    return summed


def row_shards(
    tokens,
    valid_rows,
    valid_cols,
    ln1_gain,
    q_weight,
    sr_weight,
    sr_gain,
    kv_weight,
    out_weight,
    ln2_gain,
    fc1_weight,
    dw_weight,
    fc2_weight,
    cotangent,
):
    images = tokens.shape[0]
    columns = tokens.shape[2]
    groups = lax.axis_size("rows")
    score_scale = HEAD_DIM ** (-0.5)
    first_row = lax.axis_index("rows") * POOL
    ids = first_row + jnp.arange(POOL, dtype=jnp.int32)
    inside = (
        (ids[None, :, None] >= 0)
        & (ids[None, :, None] < valid_rows[:, None, None])
        & (jnp.arange(columns)[None, None, :] < valid_cols[:, None, None])
    )
    inside_float = inside.astype(jnp.float32)[..., None]
    key_live = (
        (jnp.arange(groups)[None, :, None] * POOL < valid_rows[:, None, None])
        & (jnp.arange(columns // POOL)[None, None, :] * POOL < valid_cols[:, None, None])
    ).reshape(images, -1)
    picture = tokens.astype(jnp.float32)
    normed, ln1_back = jax.vjp(layer_norm, picture, ln1_gain)
    normed_low = normed.astype(jnp.bfloat16)
    queries = jnp.dot(normed_low, q_weight, preferred_element_type=jnp.float32).astype(jnp.bfloat16)
    masked = jnp.where(inside[..., None], normed_low, 0)
    patches = (
        masked.reshape(images, POOL, columns // POOL, POOL, D)
        .transpose(0, 2, 1, 3, 4)
        .reshape(images, columns // POOL, POOL * POOL * D)
    )
    pooled = jnp.dot(patches, sr_weight, preferred_element_type=jnp.float32)
    reduced, sr_back = jax.vjp(layer_norm, pooled, sr_gain)
    reduced_low = reduced.astype(jnp.bfloat16)
    key_value = jnp.dot(reduced_low, kv_weight, preferred_element_type=jnp.float32).astype(
        jnp.bfloat16
    )
    gathered = lax.all_gather(key_value[:, None], "rows", axis=1, tiled=True).reshape(
        images, -1, 2 * D
    )
    key_part = gathered[..., :D].reshape(images, -1, HEADS, HEAD_DIM)
    value_part = gathered[..., D:].reshape(images, -1, HEADS, HEAD_DIM)
    head_queries = queries.reshape(images, -1, HEADS, HEAD_DIM)
    scores = (
        jnp.einsum("inhe,iphe->ihnp", head_queries, key_part, preferred_element_type=jnp.float32)
        * score_scale
    )
    scores = jnp.where(key_live[:, None, None, :], scores, NEG)
    probabilities = jax.nn.softmax(scores, axis=-1)
    probs_low = probabilities.astype(jnp.bfloat16)
    attended = jnp.einsum(
        "ihnp,iphe->inhe", probs_low, value_part, preferred_element_type=jnp.float32
    ).reshape(images, POOL, columns, D)
    attended_low = (attended * inside_float).astype(jnp.bfloat16)
    middle = picture + jnp.dot(attended_low, out_weight, preferred_element_type=jnp.float32)
    normed2, ln2_back = jax.vjp(layer_norm, middle, ln2_gain)
    normed2_low = normed2.astype(jnp.bfloat16)
    kernel = dw_weight.astype(jnp.float32)
    hidden_shape = (images, POOL, columns, FF)
    hidden = jnp.where(
        inside[..., None],
        jnp.dot(normed2_low, fc1_weight, preferred_element_type=jnp.float32).astype(jnp.bfloat16),
        0,
    )
    padded = pad_columns(padded_2(hidden, (("rows", 1),), 1))
    convolved = depth_conv(padded, kernel, POOL, columns)
    active, gelu_back = jax.vjp(activate, convolved)
    active_low = active.astype(jnp.bfloat16)
    block_out = (
        middle + jnp.dot(active_low, fc2_weight, preferred_element_type=jnp.float32) * inside_float
    ).astype(jnp.bfloat16)
    branch_grad = jnp.where(inside[..., None], cotangent, 0)
    fc2_grad = outer_product(active_low, branch_grad)
    active_grad = back_product(branch_grad, fc2_weight)
    (conv_grad,) = gelu_back(active_grad)
    conv_low = conv_grad.astype(jnp.bfloat16)
    grad_padded = pad_columns(padded_2(conv_low, (("rows", 1),), 1))
    hidden_grad = jnp.zeros(hidden_shape, jnp.float32)
    for offset_row in range(3):
        for offset_col in range(3):
            hidden_grad = (
                hidden_grad
                + grad_padded[
                    :,
                    2 - offset_row : 2 - offset_row + POOL,
                    2 - offset_col : 2 - offset_col + columns,
                ]
                * kernel[offset_row, offset_col]
            )
    dw_grad = jnp.stack(
        [
            jnp.stack(
                [
                    jnp.sum(
                        padded[:, offset_row : offset_row + POOL, offset_col : offset_col + columns]
                        * conv_low.astype(jnp.float32),
                        axis=(0, 1, 2),
                    )
                    for offset_col in range(3)
                ]
            )
            for offset_row in range(3)
        ]
    )
    hidden_low_grad = jnp.where(inside[..., None], hidden_grad, 0.0).astype(jnp.bfloat16)
    fc1_grad = outer_product(normed2_low, hidden_low_grad)
    normed2_grad = back_product(hidden_low_grad, fc1_weight)
    middle_back, ln2_gain_grad = ln2_back(normed2_grad)
    middle_grad = cotangent.astype(jnp.float32) + middle_back
    branch_low = middle_grad.astype(jnp.bfloat16)
    out_grad = outer_product(attended_low, branch_low)
    attended_grad = (
        jnp.where(inside[..., None], back_product(branch_low, out_weight), 0.0)
        .astype(jnp.bfloat16)
        .reshape(images, -1, HEADS, HEAD_DIM)
    )
    value_grad = jnp.einsum(
        "ihnp,inhe->iphe", probs_low, attended_grad, preferred_element_type=jnp.float32
    )
    prob_grad = jnp.einsum(
        "inhe,iphe->ihnp", attended_grad, value_part, preferred_element_type=jnp.float32
    )
    score_grad = (
        probabilities
        * (prob_grad - jnp.sum(probabilities * prob_grad, axis=-1, keepdims=True))
        * score_scale
    ).astype(jnp.bfloat16)
    query_grad = (
        jnp.einsum("ihnp,iphe->inhe", score_grad, key_part, preferred_element_type=jnp.float32)
        .astype(jnp.bfloat16)
        .reshape(images, POOL, columns, D)
    )
    key_grad = jnp.einsum(
        "ihnp,inhe->iphe", score_grad, head_queries, preferred_element_type=jnp.float32
    )
    pair_partial = jnp.concatenate(
        [key_grad.reshape(images, -1, D), value_grad.reshape(images, -1, D)], axis=-1
    ).reshape(images, groups, columns // POOL, 2 * D)
    pair_owned = lax.psum_scatter(pair_partial, "rows", scatter_dimension=1, tiled=True)
    pair_low = pair_owned[:, 0].astype(jnp.bfloat16)
    pair_weight_grad = outer_product(reduced_low, pair_low)
    reduced_grad = back_product(pair_low, kv_weight)
    pooled_grad, sr_gain_grad = sr_back(reduced_grad)
    pooled_low = pooled_grad.astype(jnp.bfloat16)
    sr_grad = outer_product(patches, pooled_low)
    patch_grad = (
        back_product(pooled_low, sr_weight)
        .reshape(images, columns // POOL, POOL, POOL, D)
        .transpose(0, 2, 1, 3, 4)
        .reshape(images, POOL, columns, D)
    )
    normed_grad = back_product(query_grad, q_weight) + jnp.where(inside[..., None], patch_grad, 0.0)
    q_grad = outer_product(normed_low, query_grad)
    picture_back, ln1_gain_grad = ln1_back(normed_grad)
    input_grad = (middle_grad + picture_back).astype(jnp.bfloat16)
    ln1_sum, q_sum, sr_sum, srg_sum, pair_sum, out_sum, ln2_sum, fc1_sum, dw_sum, fc2_sum = (
        lax.psum(
            (
                ln1_gain_grad,
                q_grad,
                sr_grad,
                sr_gain_grad,
                pair_weight_grad,
                out_grad,
                ln2_gain_grad,
                fc1_grad,
                dw_grad,
                fc2_grad,
            ),
            ("rows", "batch"),
        )
    )
    return (
        block_out,
        input_grad,
        ln1_sum,
        q_sum,
        sr_sum,
        srg_sum,
        pair_sum,
        out_sum,
        ln2_sum,
        fc1_sum,
        dw_sum,
        fc2_sum,
    )


VMEM = pltpu.VMEM
NT = (((1,), (1,)), ((), ()))
TN = (((0,), (0,)), ((), ()))


def mm(left, right):
    return jnp.dot(left, right, preferred_element_type=jnp.float32)


def mm_nt(left, right):
    return lax.dot_general(left, right, NT, preferred_element_type=jnp.float32)


def mm_tn(left, right):
    return lax.dot_general(left, right, TN, preferred_element_type=jnp.float32)


def norm_parts(source):
    centered = source - jnp.mean(source, axis=-1, keepdims=True)
    scale = lax.rsqrt(jnp.mean(centered * centered, axis=-1, keepdims=True) + EPS)
    return centered * scale, scale


def norm_back(grad, gain, unit, scale):
    scaled = grad * gain
    inner = jnp.mean(scaled * unit, axis=-1, keepdims=True)
    return scale * (scaled - jnp.mean(scaled, axis=-1, keepdims=True) - unit * inner)


def block_inside(first_row, rows, cols):
    row = first_row + lax.broadcasted_iota(jnp.int32, (4, 64, D), 0)
    col = lax.broadcasted_iota(jnp.int32, (4, 64, D), 1)
    return ((row < rows) & (col < cols)).reshape(256, D)


def halves(shape):
    return lax.broadcasted_iota(jnp.int32, shape, len(shape) - 1) < HEAD_DIM


def block_pair(source):
    left = halves(source.shape)
    zero = jnp.zeros_like(source)
    return jnp.concatenate([jnp.where(left, source, zero), jnp.where(left, zero, source)], axis=0)


def half_reduce(reducer, value, empty):
    left = halves(value.shape)
    first = reducer(jnp.where(left, value, empty), axis=-1, keepdims=True)
    second = reducer(jnp.where(left, empty, value), axis=-1, keepdims=True)
    return jnp.where(left, first, second)


def attend_kernel(
    place, own, near1, near2, near3, gains, wq, wsr, wkv, wout,
    x_out, normed_out, q_out, prob_out, att_out, mid_out, pat_out, pooled_out, kv_out, masked,
):
    me = place[0]
    for k, chunk in enumerate((own, near1, near2, near3)):
        block = me ^ k
        for i in range(2):
            raw = own[2 * me + i] if k == 0 else chunk[i]
            x_out[pl.ds(block * 4, 4), i] = raw
            unit, _ = norm_parts(raw.astype(jnp.float32).reshape(256, D))
            normed = (unit * gains[pl.ds(0, 1), :]).astype(jnp.bfloat16)
            normed_out[pl.ds(block * 4, 4), i] = normed.reshape(4, 64, D)
            inside = block_inside(block * 4, place[4 + i], place[6 + i])
            start = pl.multiple_of(i * 1024 + block * 256, 256)
            masked[pl.ds(start, 256), :] = jnp.where(inside, normed.astype(jnp.float32), 0.0)
    for i in range(2):
        for a in range(4):
            for u in range(4):
                for t in range(4):
                    piece = masked[pl.ds(i * 1024 + (4 * a + u) * 64 + t, 16, stride=4), :]
                    pat_out[pl.ds(i * 64 + a * 16, 16), pl.ds((u * 4 + t) * D, D)] = piece.astype(
                        jnp.bfloat16
                    )
    pooled = mm(pat_out[...], wsr[...])
    pooled_out[...] = pooled
    unit, _ = norm_parts(pooled)
    pairs = mm((unit * gains[pl.ds(1, 1), :]).astype(jnp.bfloat16), wkv[...]).astype(jnp.bfloat16)
    kv_out[...] = pairs
    lane = lax.broadcasted_iota(jnp.int32, (1, D), 1) % 64
    for i in range(2):
        rows, cols = place[4 + i], place[6 + i]
        live = ((lane // 16) * 4 < rows) & ((lane % 16) * 4 < cols)
        keys = block_pair(pairs[i * 64 : i * 64 + 64, :D].astype(jnp.float32)).astype(jnp.bfloat16)
        values = block_pair(pairs[i * 64 : i * 64 + 64, D:].astype(jnp.float32)).astype(jnp.bfloat16)
        for b in range(4):
            part = pl.ds(b * 4, 4)
            query = mm(normed_out[part, i].reshape(256, D), wq[...]).astype(jnp.bfloat16)
            q_out[part, i] = query.reshape(4, 64, D)
            scores = jnp.where(live, mm_nt(query, keys) * SCORE_SCALE, NEG)
            weights = jnp.exp(scores - half_reduce(jnp.max, scores, -jnp.inf))
            probs = weights / half_reduce(jnp.sum, weights, 0.0)
            prob_out[part, i] = probs.reshape(4, 64, D)
            mixed = mm(probs.astype(jnp.bfloat16), values)
            mixed = jnp.where(block_inside(b * 4, rows, cols), mixed, 0.0).astype(jnp.bfloat16)
            att_out[part, i] = mixed.reshape(4, 64, D)
            middle = x_out[part, i].astype(jnp.float32).reshape(256, D) + mm(mixed, wout[...])
            mid_out[part, i] = middle.reshape(4, 64, D)


def gelu_parts(x):
    density = jnp.exp(x * x * -0.5) * 0.3989422804014327
    phi = 0.5 + 0.5 * lax.erf(x * 0.7071067811865476)
    return x * phi, phi + x * density


def feed_kernel(
    place, mid, cot, cot1, cot2, cot3, gains, wfc1, taps, wfc2,
    bo0, bo1, bo2, bo3, mg_out, send_out, keep_out,
    cj, br, br_t, mask, even, odd, mix, pairs, pairs_t, cg, act, acc, back, stage,
):
    me = place[0]
    edge = jnp.zeros((128, 3 * D), jnp.bfloat16)
    even[pl.ds(1024, 128), :] = edge
    odd[pl.ds(0, 128), :] = edge
    col = lax.broadcasted_iota(jnp.int32, (256, D), 0) % 64
    for k, chunk in enumerate((cot, cot1, cot2, cot3)):
        block = me ^ k
        for i in range(2):
            raw = cot[2 * me + i] if k == 0 else chunk[i]
            inside = block_inside(block * 4, place[4 + i], place[6 + i]).reshape(4, 64, D)
            for r in range(4):
                at = pl.ds(pl.multiple_of((r % 2) * 1024 + block * 256 + (r // 2) * 128 + i * 64, 64), 64)
                cj[at, :] = raw[r]
                mask[at, :] = jnp.where(inside[r], 1.0, 0.0)
    fc1_wide = wfc1[...].astype(jnp.float32)
    for k in range(4):
        for s in range(3):
            mix[k, pl.ds(s * D, D), :] = (fc1_wide * taps[pl.ds(3 * k + s, 1), :]).astype(jnp.bfloat16)
    for e, side in enumerate((even, odd)):
        for j in range(0, 8, 2):
            part = pl.ds(e * 1024 + j * 128, 256)
            inside = mask[part, :]
            branch = cj[part, :].astype(jnp.float32) * inside
            br[part, :] = branch.astype(jnp.bfloat16)
            br_t[:, part] = branch.T.astype(jnp.bfloat16)
            source = jnp.concatenate([mid[pl.ds((2 * (j + h) + e) * 128, 128), :] for h in range(2)], axis=0)
            unit, _ = norm_parts(source)
            normed = ((unit * gains[pl.ds(2, 1), :]).astype(jnp.bfloat16)).astype(jnp.float32) * inside
            before = jnp.where(col == 0, 0.0, pltpu.roll(normed, 1, 0))
            after = jnp.where(col == 63, 0.0, pltpu.roll(normed, 255, 0))
            for s, value in enumerate((before, normed, after)):
                side[pl.ds((j + e) * 128, 256), pl.ds(s * D, D)] = value.astype(jnp.bfloat16)
    for k in range(4):
        for j in range(0, 8, 2):
            for s in range(3):
                lanes = pl.ds(s * D, D)
                ev, ev_next = (even[pl.ds((j + h) * 128, 256), lanes].astype(jnp.float32) for h in (0, 1))
                od_last, od = (odd[pl.ds((j + h) * 128, 256), lanes].astype(jnp.float32) for h in (0, 1))
                value = (od_last - od, ev + od, od - ev, ev - ev_next)[k]
                pairs[k, pl.ds(j * 128, 256), lanes] = value.astype(jnp.bfloat16)
                pairs_t[k, lanes, pl.ds(j * 128, 256)] = value.T.astype(jnp.bfloat16)
    for f in range(FF // FC):
        chan = pl.ds(f * FC, FC)
        for b in range(1024 // TB):
            part = pl.ds(b * TB, TB)
            m0, m1, m2, m3 = (mm(pairs[k, part, :], mix[k, :, chan]) for k in range(4))
            grads = []
            for e, conv in enumerate((m0 + (m1 + m2), (m1 - m2) - m3)):
                here = pl.ds(e * 1024 + b * TB, TB)
                value, slope = gelu_parts(conv)
                low = value.astype(jnp.bfloat16)
                act[here, :] = low
                grads.append(mm_nt(br[here, :], wfc2[chan, :]) * slope)
                if f == 0:
                    acc[here, :] = mm(low, wfc2[chan, :])
                else:
                    acc[here, :] += mm(low, wfc2[chan, :])
            for k, value in enumerate((grads[0], grads[0] + grads[1], grads[0] - grads[1], grads[1])):
                cg[k, part, chan] = value.astype(jnp.bfloat16)
        fc2_grad = mm(br_t[...], act[...])
        stage[pl.ds(FF + f * FC, FC), :] = fc2_grad.T
        fc1_grad = jnp.zeros((D, FC), jnp.float32)
        tap_grads = []
        for k in range(4):
            outer = mm(pairs_t[k], cg[k, :, chan])
            for s in range(3):
                here = outer[s * D : (s + 1) * D]
                if k == 3:
                    here = -here
                fc1_grad += here * taps[pl.ds(3 * k + s, 1), chan]
                tap_grads.append(jnp.sum(here * wfc1[:, chan].astype(jnp.float32), axis=0, keepdims=True))
        for s in range(3):
            half_sum = 0.5 * (tap_grads[3 + s] + tap_grads[6 + s])
            half_gap = 0.5 * (tap_grads[3 + s] - tap_grads[6 + s])
            for p, value in enumerate((tap_grads[s] + half_sum, half_gap, half_sum + tap_grads[9 + s])):
                for j in range(FC // D):
                    at = 2 * FF + (3 * p + s) * 8 + f * (FC // D) + j
                    stage[pl.ds(at, 1), :] = value[:, j * D : (j + 1) * D]
        for j in range(FC // D):
            stage[pl.ds((f * (FC // D) + j) * D, D), :] = fc1_grad[:, j * D : (j + 1) * D]
    back[0, pl.ds(1024, 128), :] = jnp.zeros((128, 3 * D), jnp.float32)
    back[3, pl.ds(0, 128), :] = jnp.zeros((128, 3 * D), jnp.float32)
    for k in range(4):
        for b in range(1024 // TB):
            here = pl.ds(b * TB + (128 if k == 3 else 0), TB)
            back[k, here, :] = mm_nt(cg[k, pl.ds(b * TB, TB), :], mix[k])
    gain_grad = jnp.zeros((1, D), jnp.float32)
    for k, bo in enumerate((bo0, bo1, bo2, bo3)):
        block = me ^ k
        for e in range(2):
            start = pl.multiple_of(block * 256, 256)
            here, later = pl.ds(start, 256), pl.ds(start + 128, 256)
            part = pl.ds(pl.multiple_of(e * 1024 + block * 256, 256), 256)
            rows = [pl.ds(pl.multiple_of(block * 512 + (2 * h + e) * 128, 128), 128) for h in range(2)]
            inside = mask[part, :]
            middle = jnp.concatenate([mid[row, :] for row in rows], axis=0)
            result = (middle + acc[part, :] * inside).astype(jnp.bfloat16).reshape(2, 2, 64, D)
            for i in range(2):
                for h in range(2):
                    bo[i, 2 * h + e] = result[h, i]
            if e == 0:
                spread = back[1, here, :] - back[2, here, :] + back[3, here, :] - back[3, later, :]
            else:
                spread = back[1, here, :] + back[2, here, :] - back[0, here, :] + back[0, later, :]
            after = jnp.where(col == 63, 0.0, pltpu.roll(spread[:, :D], 255, 0))
            before = jnp.where(col == 0, 0.0, pltpu.roll(spread[:, 2 * D :], 1, 0))
            normed_grad = (spread[:, D : 2 * D] + before + after) * inside
            unit, scale = norm_parts(middle)
            gain_grad += jnp.sum(normed_grad * unit, axis=0, keepdims=True)
            total = cj[part, :].astype(jnp.float32) + norm_back(normed_grad, gains[pl.ds(2, 1), :], unit, scale)
            for h in range(2):
                mg_out[rows[h], :] = total[h * 128 : (h + 1) * 128]
    stage[pl.ds(2 * FF + 72, 1), :] = gain_grad
    stage[pl.ds(2 * FF + 73, 55), :] = jnp.zeros((55, D), jnp.float32)
    split_pack(place, stage, send_out, keep_out)


def split_pack(place, stage, send_out, keep_out):
    rows = stage.shape[0] // 8
    for k in range(4):
        at = pl.ds(k * rows, rows)
        for out, core, first in ((send_out, 1 - place[1], place[3]), (keep_out, place[1], place[2])):
            start = pl.multiple_of((core * 4 + (first ^ k)) * rows, 16)
            out[at, :] = stage[pl.ds(start, rows), :].astype(jnp.bfloat16)


def back_kernel(
    place, x, normed, query, prob, att, mgrad, pat, pooled, kv,
    gains, wq, wsr, wkv, wout,
    ig0, ig1, ig2, ig3, send_out, keep_out,
    stage, probs_low, att_grad, score_grad, query_grad, unfold,
):
    me = place[0]
    zero = jnp.zeros((D, D), jnp.float32)
    out_grad = zero
    key_rows = []
    for i in range(2):
        rows, cols = place[4 + i], place[6 + i]
        keys = block_pair(kv[pl.ds(i * 64, 64), pl.ds(0, D)].astype(jnp.float32)).astype(jnp.bfloat16)
        values = block_pair(kv[pl.ds(i * 64, 64), pl.ds(D, D)].astype(jnp.float32)).astype(jnp.bfloat16)
        for b in range(4):
            part = pl.ds(b * 4, 4)
            at = pl.ds(b * 256, 256)
            low = mgrad[part, i].reshape(256, D).astype(jnp.bfloat16)
            out_grad += mm_tn(att[part, i].reshape(256, D), low)
            mixed = jnp.where(block_inside(b * 4, rows, cols), mm_nt(low, wout[...]), 0.0).astype(jnp.bfloat16)
            att_grad[at, :] = mixed
            weights = prob[part, i].reshape(256, D)
            probs_low[at, :] = weights.astype(jnp.bfloat16)
            back = mm_nt(mixed, values)
            back = weights * (back - half_reduce(jnp.sum, weights * back, 0.0)) * SCORE_SCALE
            back = back.astype(jnp.bfloat16)
            score_grad[at, :] = back
            query_grad[pl.ds(i * 1024 + b * 256, 256), :] = mm(back, keys).astype(jnp.bfloat16)
        value_full = mm_tn(probs_low[...], att_grad[...])
        key_full = mm_tn(score_grad[...], query[:, i].reshape(1024, D))
        left = halves((64, D))
        key_rows.append(
            jnp.concatenate(
                [
                    jnp.where(left, key_full[:64], key_full[64:]),
                    jnp.where(left, value_full[:64], value_full[64:]),
                ],
                axis=1,
            )
        )
    pair = jnp.concatenate(key_rows, axis=0).astype(jnp.bfloat16)
    unit, scale = norm_parts(pooled[...])
    reduced = (unit * gains[pl.ds(1, 1), :]).astype(jnp.bfloat16)
    kv_grad = mm_tn(reduced, pair)
    reduced_grad = mm_nt(pair, wkv[...])
    srg_grad = jnp.sum(reduced_grad * unit, axis=0, keepdims=True)
    pooled_low = norm_back(reduced_grad, gains[pl.ds(1, 1), :], unit, scale).astype(jnp.bfloat16)
    stage[pl.ds(0, 2048), :] = mm_tn(pat[...], pooled_low)
    patch_grad = mm_nt(pooled_low, wsr[...])
    for i in range(2):
        for a in range(4):
            for u in range(4):
                for t in range(4):
                    unfold[pl.ds(i * 1024 + (4 * a + u) * 64 + t, 16, stride=4), :] = patch_grad[
                        i * 64 + a * 16 : i * 64 + a * 16 + 16, (u * 4 + t) * D : (u * 4 + t + 1) * D
                    ]
    stage[pl.ds(2048, D), :] = kv_grad[:, :D]
    stage[pl.ds(2176, D), :] = kv_grad[:, D:]
    stage[pl.ds(2432, D), :] = out_grad
    q_grad = zero
    gain_grad = jnp.zeros((1, D), jnp.float32)
    for k, ig in enumerate((ig0, ig1, ig2, ig3)):
        block = me ^ k
        part = pl.ds(block * 4, 4)
        for i in range(2):
            at = pl.ds(pl.multiple_of(i * 1024 + block * 256, 256), 256)
            inside = block_inside(block * 4, place[4 + i], place[6 + i])
            back = query_grad[at, :]
            q_grad += mm_tn(normed[part, i].reshape(256, D), back)
            grad = mm_nt(back, wq[...]) + jnp.where(inside, unfold[at, :], 0.0)
            unit, scale = norm_parts(x[part, i].astype(jnp.float32).reshape(256, D))
            gain_grad += jnp.sum(grad * unit, axis=0, keepdims=True)
            total = mgrad[part, i].reshape(256, D) + norm_back(grad, gains[pl.ds(0, 1), :], unit, scale)
            ig[i] = total.astype(jnp.bfloat16).reshape(4, 64, D)
    stage[pl.ds(2304, D), :] = q_grad
    stage[pl.ds(2560, 1), :] = gain_grad
    stage[pl.ds(2561, 1), :] = srg_grad
    stage[pl.ds(2562, 126), :] = jnp.zeros((126, D), jnp.float32)
    split_pack(place, stage, send_out, keep_out)


def call(kernel, scalars, arrays, outs, scratch, flops=0, name=None, vmem=24):
    spec = pl.BlockSpec(memory_space=VMEM)
    return pl.pallas_call(
        kernel,
        out_shape=[jax.ShapeDtypeStruct(shape, kind) for shape, kind in outs],
        in_specs=[pl.BlockSpec(memory_space=pltpu.SMEM)] * len(scalars) + [spec] * len(arrays),
        out_specs=[spec] * len(outs),
        scratch_shapes=scratch,
        compiler_params=pltpu.CompilerParams(vmem_limit_bytes=vmem * 2**20),
        cost_estimate=pl.CostEstimate(flops=flops, bytes_accessed=4 * 2**20, transcendentals=0),
        name=name,
    )(*scalars, *arrays)


BF, F32 = jnp.bfloat16, jnp.float32
JOINT = (16, 2, 64, D)
CHUNK = (2, 4, 64, D)
PACK1, PACK2 = 2176, 2688
FC, TB = 512, 1024
SCORE_SCALE = HEAD_DIM ** (-0.5)


def attend(place, chunks, gains, wq, wsr, wkv, wout):
    return call(
        attend_kernel,
        (place,),
        (*chunks, gains, wq, wsr, wkv, wout),
        [
            (JOINT, BF), (JOINT, BF), (JOINT, BF), (JOINT, F32), (JOINT, BF), (JOINT, F32),
            ((128, 2048), BF), ((128, D), F32), ((128, 2 * D), BF),
        ],
        [VMEM((2048, D), F32)],
        flops=10**9, name="attend",
    )


def feed(place, middle, chunks, gains, wfc1, taps, wfc2):
    return call(
        feed_kernel,
        (place,),
        (middle, *chunks, gains, wfc1, taps, wfc2),
        [(CHUNK, BF)] * 4 + [((2048, D), F32), ((PACK1 // 2, D), BF), ((PACK1 // 2, D), BF)],
        [
            VMEM((2048, D), BF), VMEM((2048, D), BF), VMEM((D, 2048), BF), VMEM((2048, D), F32),
            VMEM((1152, 3 * D), BF), VMEM((1152, 3 * D), BF), VMEM((4, 3 * D, FF), BF),
            VMEM((4, 1024, 3 * D), BF), VMEM((4, 3 * D, 1024), BF), VMEM((4, 1024, FF), BF), VMEM((2048, FC), BF),
            VMEM((2048, D), F32), VMEM((4, 1152, 3 * D), F32), VMEM((PACK1, D), F32),
        ],
        flops=16 * 10**9, name="feed", vmem=44,
    )


def back(place, kept, mgrad, gains, wq, wsr, wkv, wout):
    x, normed, query, prob, att, _, pat, pooled, kv = kept
    return call(
        back_kernel,
        (place,),
        (x, normed, query, prob, att, mgrad, pat, pooled, kv, gains, wq, wsr, wkv, wout),
        [(CHUNK, BF)] * 4 + [((PACK2 // 2, D), BF), ((PACK2 // 2, D), BF)],
        [
            VMEM((PACK2, D), F32), VMEM((1024, D), BF), VMEM((1024, D), BF), VMEM((1024, D), BF),
            VMEM((2048, D), BF), VMEM((2048, D), F32),
        ],
        flops=2 * 10**9, name="back",
    )


def over_rows(value, k):
    return lax.ppermute(value, "rows", [(i, i ^ k) for i in range(4)])


def over_four(value, k, phase):
    plane, line = (k >> 1) * 16 + (k & 1), 2 * k
    pairs = [(i, i ^ (plane if (i >> 3) & 1 == phase else line)) for i in range(32)]
    return lax.ppermute(value, ("rows", "batch"), pairs)


def plus(*values):
    return sum(v.astype(F32) for v in values).astype(BF)


def plane_parts(packs):
    halves_in = [plus(keep, over_rows(send, 1)) for send, keep in packs]
    return [
        jnp.concatenate([h[k * (h.shape[0] // 4) : (k + 1) * (h.shape[0] // 4)] for h in halves_in])
        for k in range(4)
    ]


def first_sum(parts):
    got = {k: over_four(parts[k], k, 0) for k in (3, 2, 1)}
    return plus(parts[0], got[1], got[2], got[3])


def second_sum(mine, got):
    got = [g.astype(F32) for g in got]
    return ((mine.astype(F32) + got[0]) + (got[1] + got[2])).astype(BF)


def to_four(value, phase):
    got = {k: over_four(value, k, phase) for k in (3, 2, 1)}
    return got[1], got[2], got[3]


def finish_kernel(place, *refs):
    pieces, (q, sr, kv, out, fc1, fc2, dw, ln1, ln2, srg, stage1, stage2, sems) = refs[:8], refs[8:]
    rows1, rows2 = PACK1 // 8, PACK2 // 8
    for j, piece in enumerate(pieces):
        core, first = (place[1], place[2]) if j < 4 else (1 - place[1], place[3])
        spot = core * 4 + (first ^ (j % 4))
        stage1[pl.ds(pl.multiple_of(spot * rows1, 16), rows1), :] = piece[pl.ds(0, rows1), :].astype(F32)
        stage2[pl.ds(pl.multiple_of(spot * rows2, 16), rows2), :] = piece[pl.ds(rows1, rows2), :].astype(F32)
    moves = [
        (stage2.at[pl.ds(0, 2048)], sr),
        (stage1.at[pl.ds(FF, FF)], fc2),
        *((stage1.at[pl.ds(j * D, D)], fc1.at[:, pl.ds(j * D, D)]) for j in range(8)),
        *((stage2.at[pl.ds(2048 + j * D, D)], kv.at[:, pl.ds(j * D, D)]) for j in range(2)),
        (stage2.at[pl.ds(2304, D)], q),
        (stage2.at[pl.ds(2432, D)], out),
    ]
    copies = [pltpu.make_async_copy(a, b, sems.at[n]) for n, (a, b) in enumerate(moves)]
    for copy in copies:
        copy.start()
    for tap in range(9):
        for j in range(8):
            dw[tap // 3, pl.ds(tap % 3, 1), pl.ds(j * D, D)] = stage1[pl.ds(2 * FF + tap * 8 + j, 1), :]
    ln2[...] = stage1[pl.ds(2 * FF + 72, 1), :].reshape(D)
    ln1[...] = stage2[pl.ds(2560, 1), :].reshape(D)
    srg[...] = stage2[pl.ds(2561, 1), :].reshape(D)
    for copy in copies:
        copy.wait()


def finish(place, pieces):
    far, near = pl.BlockSpec(memory_space=pl.ANY), pl.BlockSpec(memory_space=VMEM)
    shapes = [(D, D), (2048, D), (D, 2 * D), (D, D), (D, FF), (FF, D), (3, 3, FF), (D,), (D,), (D,)]
    return pl.pallas_call(
        finish_kernel,
        out_shape=[jax.ShapeDtypeStruct(shape, F32) for shape in shapes],
        in_specs=[pl.BlockSpec(memory_space=pltpu.SMEM)] + [near] * 8,
        out_specs=[far] * 6 + [near] * 4,
        scratch_shapes=[VMEM((PACK1, D), F32), VMEM((PACK2, D), F32), pltpu.SemaphoreType.DMA((14,))],
        compiler_params=pltpu.CompilerParams(vmem_limit_bytes=12 * 2**20),
        name="finish",
    )(place, *pieces)


def gather_kernel(place, part0, part1, part2, part3, out, sems):
    copies = [
        pltpu.make_async_copy(part, out.at[pl.ds(2 * (place[0] ^ k), 2)], sems.at[k])
        for k, part in enumerate((part0, part1, part2, part3))
    ]
    for copy in copies:
        copy.start()
    for copy in copies:
        copy.wait()


def gather_rows(place, parts, shape):
    far = pl.BlockSpec(memory_space=pl.ANY)
    return pl.pallas_call(
        gather_kernel,
        out_shape=jax.ShapeDtypeStruct(shape, BF),
        in_specs=[pl.BlockSpec(memory_space=pltpu.SMEM)] + [pl.BlockSpec(memory_space=VMEM)] * 4,
        out_specs=far,
        scratch_shapes=[pltpu.SemaphoreType.DMA((4,))],
        compiler_params=pltpu.CompilerParams(vmem_limit_bytes=4 * 2**20),
        name="gather_rows",
    )(place, *parts)


def image_shards(
    tokens, valid_rows, valid_cols, ln1_gain, q_weight, sr_weight, sr_gain, kv_weight, out_weight,
    ln2_gain, fc1_weight, dw_weight, fc2_weight, cotangent,
):
    me, lane = lax.axis_index("rows"), lax.axis_index("batch")
    core = me & 1
    plane, line = (me >> 1) * 2 + (lane & 1), lane >> 1
    first, second = jnp.where(core == 0, plane, line), jnp.where(core == 0, line, plane)
    sizes = [lax.dynamic_slice_in_dim(v, 2 * me, 2) for v in (valid_rows, valid_cols)]
    place = jnp.concatenate([jnp.stack([me, core, first, second]), *sizes]).astype(jnp.int32)

    def spread(source):
        near = {
            k: over_rows(lax.dynamic_slice_in_dim(source, 2 * (me ^ k), 2, 0), k) for k in (3, 2, 1)
        }
        return source, near[1], near[2], near[3]

    def returned(parts):
        near = {k: over_rows(parts[k], k) for k in (3, 2, 1)}
        return parts[0], near[1], near[2], near[3]

    gains = jnp.stack([ln1_gain, sr_gain, ln2_gain])
    row0, row1, row2 = dw_weight.astype(F32)
    taps = jnp.concatenate(
        [row0, 0.5 * (row0 + row1 + row2), 0.5 * (row0 - row1 + row2), row2, jnp.zeros((4, FF), F32)]
    )
    token_parts = spread(tokens)
    cotangent, _ = lax.optimization_barrier((cotangent, token_parts[3]))
    kept = attend(
        place, token_parts, gains, q_weight, sr_weight, kv_weight, out_weight
    )
    *block_parts, mgrad, send1, keep1 = feed(
        place, kept[5].reshape(2048, D), spread(cotangent), gains, fc1_weight, taps, fc2_weight
    )
    *input_parts, send2, keep2 = back(
        place, kept, mgrad.reshape(JOINT), gains, q_weight, sr_weight, kv_weight, out_weight
    )
    parts = plane_parts([(send1, keep1), (send2, keep2)])
    parts, block_parts = lax.optimization_barrier((parts, returned(block_parts)))
    mine = first_sum(parts)
    got, block_out, input_parts = lax.optimization_barrier(
        (to_four(mine, 1), gather_rows(place, block_parts, tokens.shape), returned(input_parts))
    )
    total = second_sum(mine, got)
    got, input_grad = lax.optimization_barrier(
        (to_four(total, 0), gather_rows(place, input_parts, tokens.shape))
    )
    pieces = [total, *got]
    pieces += [over_rows(piece, 1) for piece in pieces]
    q, sr, kv, out, fc1, fc2, dw, ln1_sum, ln2_sum, srg_sum = finish(place, pieces)
    return block_out, input_grad, ln1_sum, q, sr, srg_sum, kv, out, ln2_sum, fc1, dw, fc2


def shards(*arrays):
    tokens = arrays[0]
    fits = (
        lax.axis_size("rows") == 4
        and lax.axis_size("batch") == 8
        and tokens.shape == (8, 4, 64, D)
    )
    return image_shards(*arrays) if fits else row_shards(*arrays)


def solution(mesh):
    placed = (
        P("batch", "rows", None, None),
        P("batch"),
        P("batch"),
        P(),
        P(),
        P(),
        P(),
        P(),
        P(),
        P(),
        P(),
        P(),
        P(),
        P("batch", "rows", None, None),
    )
    return jax.shard_map(
        shards,
        mesh=mesh,
        in_specs=placed,
        out_specs=(
            P("batch", "rows", None, None),
            P("batch", "rows", None, None),
            P(),
            P(),
            P(),
            P(),
            P(),
            P(),
            P(),
            P(),
            P(),
            P(),
        ),
        check_vma=False,
    )
```

```python
import functools

import jax
import jax.numpy as jnp
from jax import lax
from jax.experimental import pallas as pl
from jax.experimental.pallas import tpu as pltpu
from jax.sharding import PartitionSpec as P

D = 128
FF = 1024
HEADS = 2
POOL = 4
HEAD_DIM = 64


EPS = 1e-06
NEG = -1e30


def padded_2(value, sides, width):
    for axis, dim in sides:
        size, length = (lax.axis_size(axis), value.shape[dim])
        up = [(i, (i + 1) % size) for i in range(size - 1)]
        down = [(j, i) for i, j in up]
        last = lax.slice_in_dim(value, length - width, length, axis=dim)
        first = lax.slice_in_dim(value, 0, width, axis=dim)
        before = lax.ppermute(last, axis, up)
        after = lax.ppermute(first, axis, down)
        value = jnp.concatenate([before, value, after], axis=dim)
    return value


def layer_norm(source, gain):
    centered = source - jnp.mean(source, axis=-1, keepdims=True)
    spread = jnp.mean(centered * centered, axis=-1, keepdims=True)
    return centered * lax.rsqrt(spread + EPS) * gain


def activate(source):
    return jax.nn.gelu(source, approximate=False)


def outer_product(left, right):
    return lax.dot_general(
        left.reshape(-1, left.shape[-1]),
        right.reshape(-1, right.shape[-1]),
        (((0,), (0,)), ((), ())),
        preferred_element_type=jnp.float32,
    )


def back_product(grad, weight):
    return lax.dot_general(
        grad, weight, (((grad.ndim - 1,), (1,)), ((), ())), preferred_element_type=jnp.float32
    )


def pad_columns(source):
    return jnp.pad(source, ((0, 0), (0, 0), (1, 1), (0, 0)))


def depth_conv(padded, kernel, count, columns):
    summed = jnp.zeros((padded.shape[0], count, columns, padded.shape[3]), jnp.float32)
    for offset_row in range(3):
        for offset_col in range(3):
            summed = (
                summed
                + padded[:, offset_row : offset_row + count, offset_col : offset_col + columns]
                * kernel[offset_row, offset_col]
            )
    return summed


def row_shards(
    tokens,
    valid_rows,
    valid_cols,
    ln1_gain,
    q_weight,
    sr_weight,
    sr_gain,
    kv_weight,
    out_weight,
    ln2_gain,
    fc1_weight,
    dw_weight,
    fc2_weight,
    cotangent,
):
    images = tokens.shape[0]
    columns = tokens.shape[2]
    groups = lax.axis_size("rows")
    score_scale = HEAD_DIM ** (-0.5)
    first_row = lax.axis_index("rows") * POOL
    ids = first_row + jnp.arange(POOL, dtype=jnp.int32)
    inside = (
        (ids[None, :, None] >= 0)
        & (ids[None, :, None] < valid_rows[:, None, None])
        & (jnp.arange(columns)[None, None, :] < valid_cols[:, None, None])
    )
    inside_float = inside.astype(jnp.float32)[..., None]
    key_live = (
        (jnp.arange(groups)[None, :, None] * POOL < valid_rows[:, None, None])
        & (jnp.arange(columns // POOL)[None, None, :] * POOL < valid_cols[:, None, None])
    ).reshape(images, -1)
    picture = tokens.astype(jnp.float32)
    normed, ln1_back = jax.vjp(layer_norm, picture, ln1_gain)
    normed_low = normed.astype(jnp.bfloat16)
    queries = jnp.dot(normed_low, q_weight, preferred_element_type=jnp.float32).astype(jnp.bfloat16)
    masked = jnp.where(inside[..., None], normed_low, 0)
    patches = (
        masked.reshape(images, POOL, columns // POOL, POOL, D)
        .transpose(0, 2, 1, 3, 4)
        .reshape(images, columns // POOL, POOL * POOL * D)
    )
    pooled = jnp.dot(patches, sr_weight, preferred_element_type=jnp.float32)
    reduced, sr_back = jax.vjp(layer_norm, pooled, sr_gain)
    reduced_low = reduced.astype(jnp.bfloat16)
    key_value = jnp.dot(reduced_low, kv_weight, preferred_element_type=jnp.float32).astype(
        jnp.bfloat16
    )
    gathered = lax.all_gather(key_value[:, None], "rows", axis=1, tiled=True).reshape(
        images, -1, 2 * D
    )
    key_part = gathered[..., :D].reshape(images, -1, HEADS, HEAD_DIM)
    value_part = gathered[..., D:].reshape(images, -1, HEADS, HEAD_DIM)
    head_queries = queries.reshape(images, -1, HEADS, HEAD_DIM)
    scores = (
        jnp.einsum("inhe,iphe->ihnp", head_queries, key_part, preferred_element_type=jnp.float32)
        * score_scale
    )
    scores = jnp.where(key_live[:, None, None, :], scores, NEG)
    probabilities = jax.nn.softmax(scores, axis=-1)
    probs_low = probabilities.astype(jnp.bfloat16)
    attended = jnp.einsum(
        "ihnp,iphe->inhe", probs_low, value_part, preferred_element_type=jnp.float32
    ).reshape(images, POOL, columns, D)
    attended_low = (attended * inside_float).astype(jnp.bfloat16)
    middle = picture + jnp.dot(attended_low, out_weight, preferred_element_type=jnp.float32)
    normed2, ln2_back = jax.vjp(layer_norm, middle, ln2_gain)
    normed2_low = normed2.astype(jnp.bfloat16)
    kernel = dw_weight.astype(jnp.float32)
    hidden_shape = (images, POOL, columns, FF)
    hidden = jnp.where(
        inside[..., None],
        jnp.dot(normed2_low, fc1_weight, preferred_element_type=jnp.float32).astype(jnp.bfloat16),
        0,
    )
    padded = pad_columns(padded_2(hidden, (("rows", 1),), 1))
    convolved = depth_conv(padded, kernel, POOL, columns)
    active, gelu_back = jax.vjp(activate, convolved)
    active_low = active.astype(jnp.bfloat16)
    block_out = (
        middle + jnp.dot(active_low, fc2_weight, preferred_element_type=jnp.float32) * inside_float
    ).astype(jnp.bfloat16)
    branch_grad = jnp.where(inside[..., None], cotangent, 0)
    fc2_grad = outer_product(active_low, branch_grad)
    active_grad = back_product(branch_grad, fc2_weight)
    (conv_grad,) = gelu_back(active_grad)
    conv_low = conv_grad.astype(jnp.bfloat16)
    grad_padded = pad_columns(padded_2(conv_low, (("rows", 1),), 1))
    hidden_grad = jnp.zeros(hidden_shape, jnp.float32)
    for offset_row in range(3):
        for offset_col in range(3):
            hidden_grad = (
                hidden_grad
                + grad_padded[
                    :,
                    2 - offset_row : 2 - offset_row + POOL,
                    2 - offset_col : 2 - offset_col + columns,
                ]
                * kernel[offset_row, offset_col]
            )
    dw_grad = jnp.stack(
        [
            jnp.stack(
                [
                    jnp.sum(
                        padded[:, offset_row : offset_row + POOL, offset_col : offset_col + columns]
                        * conv_low.astype(jnp.float32),
                        axis=(0, 1, 2),
                    )
                    for offset_col in range(3)
                ]
            )
            for offset_row in range(3)
        ]
    )
    hidden_low_grad = jnp.where(inside[..., None], hidden_grad, 0.0).astype(jnp.bfloat16)
    fc1_grad = outer_product(normed2_low, hidden_low_grad)
    normed2_grad = back_product(hidden_low_grad, fc1_weight)
    middle_back, ln2_gain_grad = ln2_back(normed2_grad)
    middle_grad = cotangent.astype(jnp.float32) + middle_back
    branch_low = middle_grad.astype(jnp.bfloat16)
    out_grad = outer_product(attended_low, branch_low)
    attended_grad = (
        jnp.where(inside[..., None], back_product(branch_low, out_weight), 0.0)
        .astype(jnp.bfloat16)
        .reshape(images, -1, HEADS, HEAD_DIM)
    )
    value_grad = jnp.einsum(
        "ihnp,inhe->iphe", probs_low, attended_grad, preferred_element_type=jnp.float32
    )
    prob_grad = jnp.einsum(
        "inhe,iphe->ihnp", attended_grad, value_part, preferred_element_type=jnp.float32
    )
    score_grad = (
        probabilities
        * (prob_grad - jnp.sum(probabilities * prob_grad, axis=-1, keepdims=True))
        * score_scale
    ).astype(jnp.bfloat16)
    query_grad = (
        jnp.einsum("ihnp,iphe->inhe", score_grad, key_part, preferred_element_type=jnp.float32)
        .astype(jnp.bfloat16)
        .reshape(images, POOL, columns, D)
    )
    key_grad = jnp.einsum(
        "ihnp,inhe->iphe", score_grad, head_queries, preferred_element_type=jnp.float32
    )
    pair_partial = jnp.concatenate(
        [key_grad.reshape(images, -1, D), value_grad.reshape(images, -1, D)], axis=-1
    ).reshape(images, groups, columns // POOL, 2 * D)
    pair_owned = lax.psum_scatter(pair_partial, "rows", scatter_dimension=1, tiled=True)
    pair_low = pair_owned[:, 0].astype(jnp.bfloat16)
    pair_weight_grad = outer_product(reduced_low, pair_low)
    reduced_grad = back_product(pair_low, kv_weight)
    pooled_grad, sr_gain_grad = sr_back(reduced_grad)
    pooled_low = pooled_grad.astype(jnp.bfloat16)
    sr_grad = outer_product(patches, pooled_low)
    patch_grad = (
        back_product(pooled_low, sr_weight)
        .reshape(images, columns // POOL, POOL, POOL, D)
        .transpose(0, 2, 1, 3, 4)
        .reshape(images, POOL, columns, D)
    )
    normed_grad = back_product(query_grad, q_weight) + jnp.where(inside[..., None], patch_grad, 0.0)
    q_grad = outer_product(normed_low, query_grad)
    picture_back, ln1_gain_grad = ln1_back(normed_grad)
    input_grad = (middle_grad + picture_back).astype(jnp.bfloat16)
    ln1_sum, q_sum, sr_sum, srg_sum, pair_sum, out_sum, ln2_sum, fc1_sum, dw_sum, fc2_sum = (
        lax.psum(
            (
                ln1_gain_grad,
                q_grad,
                sr_grad,
                sr_gain_grad,
                pair_weight_grad,
                out_grad,
                ln2_gain_grad,
                fc1_grad,
                dw_grad,
                fc2_grad,
            ),
            ("rows", "batch"),
        )
    )
    return (
        block_out,
        input_grad,
        ln1_sum,
        q_sum,
        sr_sum,
        srg_sum,
        pair_sum,
        out_sum,
        ln2_sum,
        fc1_sum,
        dw_sum,
        fc2_sum,
    )


VMEM = pltpu.VMEM
NT = (((1,), (1,)), ((), ()))
TN = (((0,), (0,)), ((), ()))


def mm(left, right):
    return jnp.dot(left, right, preferred_element_type=jnp.float32)


def mm_nt(left, right):
    return lax.dot_general(left, right, NT, preferred_element_type=jnp.float32)


def mm_tn(left, right):
    return lax.dot_general(left, right, TN, preferred_element_type=jnp.float32)


def norm_parts(source):
    centered = source - jnp.mean(source, axis=-1, keepdims=True)
    scale = lax.rsqrt(jnp.mean(centered * centered, axis=-1, keepdims=True) + EPS)
    return centered * scale, scale


def norm_back(grad, gain, unit, scale):
    scaled = grad * gain
    inner = jnp.mean(scaled * unit, axis=-1, keepdims=True)
    return scale * (scaled - jnp.mean(scaled, axis=-1, keepdims=True) - unit * inner)


def inside_mask(place, shape, image, row):
    at = [lax.broadcasted_iota(jnp.int32, shape, d) for d in range(len(shape) - 1)]
    first = image(at) == 0
    rows, cols = (jnp.where(first, place[n], place[n + 1]) for n in (4, 6))
    return ((row(at) < rows) & (at[-1] < cols)).reshape(-1, D)


def image_mask(place):
    return inside_mask(place, (2, 16, 64, D), lambda at: at[0], lambda at: at[1])


def halves(shape):
    return lax.broadcasted_iota(jnp.int32, shape, len(shape) - 1) < HEAD_DIM


def block_pair(source):
    left = halves(source.shape)
    zero = jnp.zeros_like(source)
    return jnp.concatenate([jnp.where(left, source, zero), jnp.where(left, zero, source)], axis=0)


def half_reduce(reducer, value, empty):
    left = halves(value.shape)
    first = reducer(jnp.where(left, value, empty), axis=-1, keepdims=True)
    second = reducer(jnp.where(left, empty, value), axis=-1, keepdims=True)
    return jnp.where(left, first, second)


def attend_kernel(
    place, own, near1, near2, near3, gains, wq, wsr, wkv, wout,
    x_out, normed_out, q_out, prob_out, att_out, mid_out, pat_out, pooled_out, kv_out, masked,
):
    me = place[0]
    for k, chunk in enumerate((own, near1, near2, near3)):
        for i in range(2):
            raw = own[2 * me + i] if k == 0 else chunk[i]
            x_out[pl.ds(pl.multiple_of(i * 1024 + (me ^ k) * 256, 256), 256), :] = raw.reshape(256, D)
    picture = x_out[...].astype(jnp.float32)
    unit, _ = norm_parts(picture)
    normed = (unit * gains[pl.ds(0, 1), :]).astype(jnp.bfloat16)
    normed_out[...] = normed
    inside = image_mask(place)
    masked[...] = jnp.where(inside, normed.astype(jnp.float32), 0.0)
    query = mm(normed, wq[...]).astype(jnp.bfloat16)
    q_out[...] = query
    for i in range(2):
        for a in range(4):
            for u in range(4):
                for t in range(4):
                    piece = masked[pl.ds(i * 1024 + (4 * a + u) * 64 + t, 16, stride=4), :]
                    pat_out[pl.ds(i * 64 + a * 16, 16), pl.ds((u * 4 + t) * D, D)] = piece.astype(
                        jnp.bfloat16
                    )
    pooled = mm(pat_out[...], wsr[...])
    pooled_out[...] = pooled
    unit, _ = norm_parts(pooled)
    pairs = mm((unit * gains[pl.ds(1, 1), :]).astype(jnp.bfloat16), wkv[...]).astype(jnp.bfloat16)
    kv_out[...] = pairs
    lane = lax.broadcasted_iota(jnp.int32, (1024, D), 1) % 64
    scores, values = [], []
    for i in range(2):
        live = ((lane // 16) * 4 < place[4 + i]) & ((lane % 16) * 4 < place[6 + i])
        keys = block_pair(pairs[i * 64 : i * 64 + 64, :D].astype(jnp.float32)).astype(jnp.bfloat16)
        values.append(block_pair(pairs[i * 64 : i * 64 + 64, D:].astype(jnp.float32)).astype(jnp.bfloat16))
        here = mm_nt(query[i * 1024 : (i + 1) * 1024], keys)
        scores.append(jnp.where(live, here * SCORE_SCALE, NEG))
    scores = jnp.concatenate(scores, axis=0)
    weights = jnp.exp(scores - half_reduce(jnp.max, scores, -jnp.inf))
    probs = weights / half_reduce(jnp.sum, weights, 0.0)
    prob_out[...] = probs
    low = probs.astype(jnp.bfloat16)
    mixed = jnp.concatenate([mm(low[i * 1024 : (i + 1) * 1024], values[i]) for i in range(2)], axis=0)
    mixed = jnp.where(inside, mixed, 0.0).astype(jnp.bfloat16)
    att_out[...] = mixed
    mid_out[...] = picture + mm(mixed, wout[...])


def gelu_parts(x):
    density = jnp.exp(x * x * -0.5) * 0.3989422804014327
    phi = 0.5 + 0.5 * lax.erf(x * 0.7071067811865476)
    return x * phi, phi + x * density


def feed_kernel(
    place, mid, cot, cot1, cot2, cot3, gains, wfc1, taps, wfc2,
    bo0, bo1, bo2, bo3, mg_out, send_out, keep_out,
    cj, br, br_t, mask, even, odd, mix, pairs, pairs_t, cg, act, acc, back, stage, result,
):
    me = place[0]
    edge = jnp.zeros((64, 3 * D), jnp.bfloat16)
    for i in range(2):
        even[pl.ds(i * 576 + 512, 64), :] = edge
        odd[pl.ds(i * 576, 64), :] = edge
    col = lax.broadcasted_iota(jnp.int32, (2048, D), 0) % 64
    for k, chunk in enumerate((cot, cot1, cot2, cot3)):
        for i in range(2):
            raw = cot[2 * me + i] if k == 0 else chunk[i]
            for r in range(4):
                at = (r % 2) * 1024 + i * 512 + (me ^ k) * 128 + (r // 2) * 64
                cj[pl.ds(pl.multiple_of(at, 64), 64), :] = raw[r]
    inside = inside_mask(place, (2, 2, 8, 64, D), lambda at: at[1], lambda at: 2 * at[2] + at[0])
    mask[...] = jnp.where(inside, 1.0, 0.0)
    fc1_wide = wfc1[...].astype(jnp.float32)
    for k in range(4):
        for s in range(3):
            mix[k, pl.ds(s * D, D), :] = (fc1_wide * taps[pl.ds(3 * k + s, 1), :]).astype(jnp.bfloat16)
    for c in range(8):
        stage[pl.ds(c * (PACK1 // 8) + 2 * D, 16), :] = jnp.zeros((16, D), jnp.float32)
    branch = cj[...].astype(jnp.float32) * mask[...]
    br[...] = branch.astype(jnp.bfloat16)
    br_t[...] = branch.T.astype(jnp.bfloat16)

    def by_parity():
        return jnp.concatenate([mid[:, :, e].reshape(1024, D) for e in range(2)], axis=0)

    unit, _ = norm_parts(by_parity())
    normed = ((unit * gains[pl.ds(2, 1), :]).astype(jnp.bfloat16)).astype(jnp.float32) * mask[...]
    before = jnp.where(col == 0, 0.0, pltpu.roll(normed, 1, 0))
    after = jnp.where(col == 63, 0.0, pltpu.roll(normed, 2047, 0))
    for s, value in enumerate((before, normed, after)):
        value = value.astype(jnp.bfloat16)
        for e, side in enumerate((even, odd)):
            for i in range(2):
                at = e * 1024 + i * 512
                side[pl.ds(i * 576 + e * 64, 512), pl.ds(s * D, D)] = value[at : at + 512]
    for i in range(2):
        ev, ev_next = (even[pl.ds(i * 576 + h * 64, 512), :].astype(jnp.float32) for h in (0, 1))
        od_last, od = (odd[pl.ds(i * 576 + h * 64, 512), :].astype(jnp.float32) for h in (0, 1))
        for k, value in enumerate((od_last - od, ev + od, od - ev, ev - ev_next)):
            here = pl.ds(i * 512, 512)
            pairs[k, here, :] = value.astype(jnp.bfloat16)
            for s in range(3):
                pairs_t[k, pl.ds(s * D, D), here] = value[:, s * D : (s + 1) * D].T.astype(jnp.bfloat16)
    for f in range(FF // FC):
        chan = pl.ds(f * FC, FC)
        for b in range(1024 // TB):
            part = pl.ds(b * TB, TB)
            m0, m1, m2, m3 = (mm(pairs[k, part, :], mix[k, :, chan]) for k in range(4))
            grads = []
            for e, conv in enumerate((m0 + (m1 + m2), (m1 - m2) - m3)):
                here = pl.ds(e * 1024 + b * TB, TB)
                value, slope = gelu_parts(conv)
                low = value.astype(jnp.bfloat16)
                act[here, :] = low
                grads.append(mm_nt(br[here, :], wfc2[chan, :]) * slope)
                if f == 0:
                    acc[here, :] = mm(low, wfc2[chan, :])
                else:
                    acc[here, :] += mm(low, wfc2[chan, :])
            for k, value in enumerate((grads[0], grads[0] + grads[1], grads[0] - grads[1], grads[1])):
                cg[k, part, chan] = value.astype(jnp.bfloat16)
        fc2_grad = mm(br_t[...], act[...])
        fc2_grad = fc2_grad.T
        for j in range(FC // D):
            stage[pl.ds((f * (FC // D) + j) * (PACK1 // 8) + D, D), :] = fc2_grad[j * D : (j + 1) * D]
        fc1_grad = jnp.zeros((D, FC), jnp.float32)
        tap_grads = []
        for k in range(4):
            outer = mm(pairs_t[k], cg[k, :, chan])
            for s in range(3):
                here = outer[s * D : (s + 1) * D]
                if k == 3:
                    here = -here
                fc1_grad += here * taps[pl.ds(3 * k + s, 1), chan]
                tap_grads.append(jnp.sum(here * wfc1[:, chan].astype(jnp.float32), axis=0, keepdims=True))
        for s in range(3):
            half_sum = 0.5 * (tap_grads[3 + s] + tap_grads[6 + s])
            half_gap = 0.5 * (tap_grads[3 + s] - tap_grads[6 + s])
            for p, value in enumerate((tap_grads[s] + half_sum, half_gap, half_sum + tap_grads[9 + s])):
                for j in range(FC // D):
                    at = (f * (FC // D) + j) * (PACK1 // 8) + 2 * D + 3 * p + s
                    stage[pl.ds(at, 1), :] = value[:, j * D : (j + 1) * D]
        for j in range(FC // D):
            stage[pl.ds((f * (FC // D) + j) * (PACK1 // 8), D), :] = fc1_grad[:, j * D : (j + 1) * D]
    for i in range(2):
        back[0, pl.ds(i * 576 + 512, 64), :] = jnp.zeros((64, 3 * D), jnp.float32)
        back[3, pl.ds(i * 576, 64), :] = jnp.zeros((64, 3 * D), jnp.float32)
    for k in range(4):
        spread = mm_nt(cg[k], mix[k])
        for i in range(2):
            back[k, pl.ds(i * 576 + (64 if k == 3 else 0), 512), :] = spread[i * 512 : (i + 1) * 512]
    spread = []
    for e in range(2):
        for i in range(2):
            here, later = pl.ds(i * 576, 512), pl.ds(i * 576 + 64, 512)
            if e == 0:
                spread.append(back[1, here, :] - back[2, here, :] + (back[3, here, :] - back[3, later, :]))
            else:
                spread.append(back[1, here, :] + back[2, here, :] + (back[0, later, :] - back[0, here, :]))
    spread = jnp.concatenate(spread, axis=0)
    after = jnp.where(col == 63, 0.0, pltpu.roll(spread[:, :D], 2047, 0))
    before = jnp.where(col == 0, 0.0, pltpu.roll(spread[:, 2 * D :], 1, 0))
    normed_grad = (spread[:, D : 2 * D] + before + after) * mask[...]
    middle = by_parity()
    unit, scale = norm_parts(middle)
    gain_grad = jnp.sum(normed_grad * unit, axis=0, keepdims=True)
    total = cj[...].astype(jnp.float32) + norm_back(normed_grad, gains[pl.ds(2, 1), :], unit, scale)
    final = (middle + acc[...] * mask[...]).astype(jnp.bfloat16)
    for e in range(2):
        mg_out[:, :, e] = total[e * 1024 : (e + 1) * 1024].reshape(2, 8, 64, D)
        result[:, :, e] = final[e * 1024 : (e + 1) * 1024].reshape(2, 8, 64, D)
    for k, bo in enumerate((bo0, bo1, bo2, bo3)):
        for i in range(2):
            bo[i] = result[i, pl.ds((me ^ k) * 2, 2)].reshape(4, 64, D)
    stage[pl.ds(2 * D + 9, 1), :] = gain_grad
    split_pack(place, stage, send_out, keep_out)


def split_pack(place, stage, send_out, keep_out):
    rows = stage.shape[0] // 8
    for k in range(4):
        at = pl.ds(k * rows, rows)
        for out, core, first in ((send_out, 1 - place[1], place[3]), (keep_out, place[1], place[2])):
            start = pl.multiple_of((core * 4 + (first ^ k)) * rows, 16)
            out[at, :] = stage[pl.ds(start, rows), :].astype(jnp.bfloat16)


def back_kernel(
    place, normed, query, prob, att, mgrad, pat, pooled, kv,
    gains, wq, wsr, wkv, wout,
    query_grad, pooled_out, send_out, keep_out,
    stage,
):
    inside = image_mask(place)
    low = mgrad[...].astype(jnp.bfloat16)
    out_grad = mm_tn(att[...], low)
    mixed = jnp.where(inside, mm_nt(low, wout[...]), 0.0).astype(jnp.bfloat16)
    keys, values = (
        [
            block_pair(kv[pl.ds(i * 64, 64), pl.ds(n * D, D)].astype(jnp.float32)).astype(jnp.bfloat16)
            for i in range(2)
        ]
        for n in range(2)
    )
    parts = [slice(i * 1024, (i + 1) * 1024) for i in range(2)]
    weights = prob[...]
    back = jnp.concatenate([mm_nt(mixed[parts[i]], values[i]) for i in range(2)], axis=0)
    back = weights * (back - half_reduce(jnp.sum, weights * back, 0.0)) * SCORE_SCALE
    back = back.astype(jnp.bfloat16)
    grads = jnp.concatenate([mm(back[parts[i]], keys[i]) for i in range(2)], axis=0).astype(jnp.bfloat16)
    query_grad[...] = grads
    weights = weights.astype(jnp.bfloat16)
    left = halves((64, D))
    key_rows = []
    for i in range(2):
        value_full = mm_tn(weights[parts[i]], mixed[parts[i]])
        key_full = mm_tn(back[parts[i]], query[pl.ds(i * 1024, 1024), :])
        key_rows.append(
            jnp.concatenate(
                [
                    jnp.where(left, key_full[:64], key_full[64:]),
                    jnp.where(left, value_full[:64], value_full[64:]),
                ],
                axis=1,
            )
        )
    pair = jnp.concatenate(key_rows, axis=0).astype(jnp.bfloat16)
    unit, scale = norm_parts(pooled[...])
    reduced = (unit * gains[pl.ds(1, 1), :]).astype(jnp.bfloat16)
    kv_grad = mm_tn(reduced, pair)
    reduced_grad = mm_nt(pair, wkv[...])
    srg_grad = jnp.sum(reduced_grad * unit, axis=0, keepdims=True)
    pooled_low = norm_back(reduced_grad, gains[pl.ds(1, 1), :], unit, scale).astype(jnp.bfloat16)
    pooled_out[...] = pooled_low
    sr_grad = mm_tn(pat[...], pooled_low)
    each = PACK2 // 8
    for c in range(8):
        stage[pl.ds(c * each, 256), :] = sr_grad[c * 256 : (c + 1) * 256]
    for c in range(8):
        side, row = c // 4, (c % 4) * 32
        stage[pl.ds(c * each + 256, 32), :] = kv_grad[row : row + 32, side * D : (side + 1) * D]
        stage[pl.ds(c * each + 304, 16), :] = out_grad[c * 16 : (c + 1) * 16]
        stage[pl.ds(c * each + 320, 16), :] = jnp.zeros((16, D), jnp.float32)
    q_grad = mm_tn(normed[...], grads)
    weighted = q_grad * wq[...].astype(jnp.float32)
    for c in range(16):
        at = slice(c * D, (c + 1) * D)
        weighted += sr_grad[at] * wsr[pl.ds(c * D, D), :].astype(jnp.float32)
    high = weighted.astype(jnp.bfloat16)
    low = (weighted - high.astype(jnp.float32)).astype(jnp.bfloat16)
    ones = jnp.ones((16, D), jnp.bfloat16)
    gain_grad = (mm_nt(ones, high) + mm_nt(ones, low))[0:1] / gains[pl.ds(0, 1), :]
    for c in range(8):
        stage[pl.ds(c * each + 288, 16), :] = q_grad[c * 16 : (c + 1) * 16]
    stage[pl.ds(320, 1), :] = gain_grad
    stage[pl.ds(321, 1), :] = srg_grad
    split_pack(place, stage, send_out, keep_out)


def input_kernel(
    place, x, query_grad, pooled_low, mgrad, gains, wq, wsr,
    ig0, ig1, ig2, ig3,
    unfold, result,
):
    me = place[0]
    patch_grad = mm_nt(pooled_low[...], wsr[...])
    for i in range(2):
        for a in range(4):
            for u in range(4):
                for t in range(4):
                    unfold[pl.ds(i * 1024 + (4 * a + u) * 64 + t, 16, stride=4), :] = patch_grad[
                        i * 64 + a * 16 : i * 64 + a * 16 + 16, (u * 4 + t) * D : (u * 4 + t + 1) * D
                    ]
    grad = mm_nt(query_grad[...], wq[...]) + jnp.where(image_mask(place), unfold[...], 0.0)
    unit, scale = norm_parts(x[...].astype(jnp.float32))
    total = mgrad[...] + norm_back(grad, gains[pl.ds(0, 1), :], unit, scale)
    result[...] = total.astype(jnp.bfloat16).reshape(2, 16, 64, D)
    for k, ig in enumerate((ig0, ig1, ig2, ig3)):
        for i in range(2):
            ig[i] = result[i, pl.ds((me ^ k) * 4, 4)]


def call(kernel, scalars, arrays, outs, scratch, flops=0, name=None, vmem=24):
    spec = pl.BlockSpec(memory_space=VMEM)
    return pl.pallas_call(
        kernel,
        out_shape=[jax.ShapeDtypeStruct(shape, kind) for shape, kind in outs],
        in_specs=[pl.BlockSpec(memory_space=pltpu.SMEM)] * len(scalars) + [spec] * len(arrays),
        out_specs=[spec] * len(outs),
        scratch_shapes=scratch,
        compiler_params=pltpu.CompilerParams(vmem_limit_bytes=vmem * 2**20),
        cost_estimate=pl.CostEstimate(flops=flops, bytes_accessed=4 * 2**20, transcendentals=0),
        name=name,
    )(*scalars, *arrays)


BF, F32 = jnp.bfloat16, jnp.float32
FLAT = (2048, D)
SPLIT = (2, 8, 2, 64, D)
CHUNK = (2, 4, 64, D)
PACK1, PACK2 = 2176, 2688
FC, TB = 512, 1024
SCORE_SCALE = HEAD_DIM ** (-0.5)


def attend(place, chunks, gains, wq, wsr, wkv, wout):
    return call(
        attend_kernel,
        (place,),
        (*chunks, gains, wq, wsr, wkv, wout),
        [
            (FLAT, BF), (FLAT, BF), (FLAT, BF), (FLAT, F32), (FLAT, BF), (FLAT, F32),
            ((128, 2048), BF), ((128, D), F32), ((128, 2 * D), BF),
        ],
        [VMEM((2048, D), F32)],
        flops=10**9, name="attend",
    )


def feed(place, middle, chunks, gains, wfc1, taps, wfc2):
    return call(
        feed_kernel,
        (place,),
        (middle, *chunks, gains, wfc1, taps, wfc2),
        [(CHUNK, BF)] * 4 + [(SPLIT, F32), ((PACK1 // 2, D), BF), ((PACK1 // 2, D), BF)],
        [
            VMEM((2048, D), BF), VMEM((2048, D), BF), VMEM((D, 2048), BF), VMEM((2048, D), F32),
            VMEM((1152, 3 * D), BF), VMEM((1152, 3 * D), BF), VMEM((4, 3 * D, FF), BF),
            VMEM((4, 1024, 3 * D), BF), VMEM((4, 3 * D, 1024), BF), VMEM((4, 1024, FF), BF), VMEM((2048, FC), BF),
            VMEM((2048, D), F32), VMEM((4, 1152, 3 * D), F32), VMEM((PACK1, D), F32), VMEM(SPLIT, BF),
        ],
        flops=16 * 10**9, name="feed", vmem=44,
    )


def back(place, kept, mgrad, gains, wq, wsr, wkv, wout):
    _, normed, query, prob, att, _, pat, pooled, kv = kept
    return call(
        back_kernel,
        (place,),
        (normed, query, prob, att, mgrad, pat, pooled, kv, gains, wq, wsr, wkv, wout),
        [(FLAT, BF), ((128, D), BF), ((PACK2 // 2, D), BF), ((PACK2 // 2, D), BF)],
        [VMEM((PACK2, D), F32)],
        flops=2 * 10**9, name="back",
    )


def input_gradient(place, x, query_grad, pooled_low, mgrad, gains, wq, wsr):
    return call(
        input_kernel,
        (place,),
        (x, query_grad, pooled_low, mgrad, gains, wq, wsr),
        [(CHUNK, BF)] * 4,
        [VMEM((2048, D), F32), VMEM((2, 16, 64, D), BF)],
        flops=10**9, name="input_gradient",
    )


def over_rows(value, k):
    return lax.ppermute(value, "rows", [(i, i ^ k) for i in range(4)])


def over_four(value, k, phase):
    plane, line = (k >> 1) * 16 + (k & 1), 2 * k
    pairs = [(i, i ^ (plane if (i >> 3) & 1 == phase else line)) for i in range(32)]
    return lax.ppermute(value, ("rows", "batch"), pairs)


def plus(*values):
    return sum(v.astype(F32) for v in values).astype(BF)


def plane_parts(packs):
    halves_in = [plus(keep, over_rows(send, 1)) for send, keep in packs]
    return [
        jnp.concatenate([h[k * (h.shape[0] // 4) : (k + 1) * (h.shape[0] // 4)] for h in halves_in])
        for k in range(4)
    ]


def to_four(values, phase):
    return [over_four(values[k], k, phase) for k in (1, 2, 3)]


def finish_kernel(half, place, *refs):
    pieces, refs = refs[: 4 * (half + 1)], refs[4 * (half + 1) :]
    if half:
        refs = refs[6:]
    (q, sr, kv, out, fc1, fc2), refs = refs[:6], refs[6:]
    stage, small_dw, small_ln1, small_ln2, small_srg, sems = refs[-6:]
    copies = []

    def move(source, target):
        copies.append(pltpu.make_async_copy(source, target, sems.at[len(copies)]))
        copies[-1].start()

    def chunk_of(j):
        core, first = (place[1], place[2]) if j < 4 else (1 - place[1], place[3])
        return core * 4 + (first ^ (j % 4))

    for k in range(4):
        c = chunk_of(4 * half + k)
        stage[k] = pieces[4 * half + k][...].astype(F32)
        chan = pl.ds(pl.multiple_of(c * D, D), D)
        move(stage.at[k, pl.ds(0, D)], fc1.at[:, chan])
        move(stage.at[k, pl.ds(D, D)], fc2.at[chan])
        move(stage.at[k, pl.ds(272, 256)], sr.at[pl.ds(pl.multiple_of(c * 256, 256), 256)])
        row = pl.ds(pl.multiple_of((c % 4) * 32, 32), 32)
        move(stage.at[k, pl.ds(528, 32)], kv.at[row, pl.ds(pl.multiple_of((c // 4) * D, D), D)])
        row = pl.ds(pl.multiple_of(c * 16, 16), 16)
        move(stage.at[k, pl.ds(560, 16)], q.at[row])
        move(stage.at[k, pl.ds(576, 16)], out.at[row])
    if half:
        sums = [jnp.zeros((1, D), F32)] * 3
        for j, piece in enumerate(pieces):
            chan = pl.ds(pl.multiple_of(chunk_of(j) * D, D), D)
            small = piece[pl.ds(256, 16), :].astype(F32)
            for tap in range(9):
                small_dw[tap // 3, pl.ds(tap % 3, 1), chan] = small[tap : tap + 1]
            last = piece[pl.ds(592, 16), :].astype(F32)
            rows = (last[0:1], small[9:10], last[1:2])
            sums = [total + row for total, row in zip(sums, rows)]
        move(small_dw, refs[0])
        for ref, small, total in zip(refs[1:4], (small_ln1, small_ln2, small_srg), sums):
            small[...] = total.reshape(D)
            move(small, ref)
    for copy in copies:
        copy.wait()


def finish(place, pieces, earlier=()):
    far, near = pl.BlockSpec(memory_space=pl.ANY), pl.BlockSpec(memory_space=VMEM)
    half = 1 if earlier else 0
    shapes = [((D, D), F32), ((2048, D), F32), ((D, 2 * D), F32), ((D, D), F32), ((D, FF), F32), ((FF, D), F32)]
    specs, n = [far] * 6, len(shapes)
    if half:
        shapes += [((3, 3, FF), F32), ((D,), F32), ((D,), F32), ((D,), F32)]
        specs += [far] * 4
    before = 1 + len(pieces)
    return pl.pallas_call(
        functools.partial(finish_kernel, half),
        out_shape=[jax.ShapeDtypeStruct(*each) for each in shapes],
        in_specs=[pl.BlockSpec(memory_space=pltpu.SMEM)] + [near] * (before - 1) + [far] * len(earlier),
        out_specs=specs,
        scratch_shapes=[
            VMEM((4, 608, D), F32), VMEM((3, 3, FF), F32), VMEM((D,), F32), VMEM((D,), F32), VMEM((D,), F32),
            pltpu.SemaphoreType.DMA((28,)),
        ],
        input_output_aliases={before + i: i for i in range(n)} if half else {},
        compiler_params=pltpu.CompilerParams(vmem_limit_bytes=8 * 2**20),
        cost_estimate=pl.CostEstimate(flops=0, bytes_accessed=4 * 2**20, transcendentals=0),
        name="finish",
    )(place, *pieces, *earlier)


def gather_kernel(place, part0, part1, part2, part3, out, sems):
    copies = [
        pltpu.make_async_copy(part, out.at[pl.ds(2 * (place[0] ^ k), 2)], sems.at[k])
        for k, part in enumerate((part0, part1, part2, part3))
    ]
    for copy in copies:
        copy.start()
    for copy in copies:
        copy.wait()


def gather_rows(place, parts, shape):
    far = pl.BlockSpec(memory_space=pl.ANY)
    return pl.pallas_call(
        gather_kernel,
        out_shape=jax.ShapeDtypeStruct(shape, BF),
        in_specs=[pl.BlockSpec(memory_space=pltpu.SMEM)] + [pl.BlockSpec(memory_space=VMEM)] * 4,
        out_specs=far,
        scratch_shapes=[pltpu.SemaphoreType.DMA((4,))],
        compiler_params=pltpu.CompilerParams(vmem_limit_bytes=4 * 2**20),
        name="gather_rows",
    )(place, *parts)


def image_shards(
    tokens, valid_rows, valid_cols, ln1_gain, q_weight, sr_weight, sr_gain, kv_weight, out_weight,
    ln2_gain, fc1_weight, dw_weight, fc2_weight, cotangent,
):
    me, lane = lax.axis_index("rows"), lax.axis_index("batch")
    core = me & 1
    plane, line = (me >> 1) * 2 + (lane & 1), lane >> 1
    first, second = jnp.where(core == 0, plane, line), jnp.where(core == 0, line, plane)
    sizes = [lax.dynamic_slice_in_dim(v, 2 * me, 2) for v in (valid_rows, valid_cols)]
    place = jnp.concatenate([jnp.stack([me, core, first, second]), *sizes]).astype(jnp.int32)

    def spread(source):
        near = {
            k: over_rows(lax.dynamic_slice_in_dim(source, 2 * (me ^ k), 2, 0), k) for k in (3, 2, 1)
        }
        return source, near[1], near[2], near[3]

    def returned(parts):
        near = {k: over_rows(parts[k], k) for k in (3, 2, 1)}
        return [parts[0], near[1], near[2], near[3]]

    gains = jnp.stack([ln1_gain, sr_gain, ln2_gain])
    row0, row1, row2 = dw_weight.astype(F32)
    taps = jnp.concatenate(
        [row0, 0.5 * (row0 + row1 + row2), 0.5 * (row0 - row1 + row2), row2, jnp.zeros((4, FF), F32)]
    )
    token_parts = spread(tokens)
    cotangent, _ = lax.optimization_barrier((cotangent, token_parts[1]))
    kept = attend(
        place, token_parts, gains, q_weight, sr_weight, kv_weight, out_weight
    )
    *block_parts, mgrad, send1, keep1 = feed(
        place, kept[5].reshape(SPLIT), spread(cotangent), gains, fc1_weight, taps, fc2_weight
    )
    mgrad = mgrad.reshape(FLAT)
    query_grad, pooled_low, send2, keep2 = back(
        place, kept, mgrad, gains, q_weight, sr_weight, kv_weight, out_weight
    )
    parts = plane_parts([(send1, keep1), (send2, keep2)])
    block = returned(block_parts)
    parts, block[2] = lax.optimization_barrier((parts, block[2]))
    inputs = input_gradient(place, kept[0], query_grad, pooled_low, mgrad, gains, q_weight, sr_weight)
    mine, inputs = lax.optimization_barrier((plus(parts[0], *to_four(parts, 0)), list(inputs)))
    inputs = returned(inputs)
    got = [g.astype(F32) for g in to_four([mine] * 4, 1)]
    got, block_out = lax.optimization_barrier((got, gather_rows(place, block, tokens.shape)))
    got, block[3] = lax.optimization_barrier((got, block[3]))
    total = ((mine.astype(F32) + got[0]) + (got[1] + got[2])).astype(BF)
    got = to_four([total] * 4, 0)
    got, inputs[2], inputs[3] = lax.optimization_barrier((got, inputs[2], inputs[3]))
    got, input_grad = lax.optimization_barrier((got, gather_rows(place, inputs, tokens.shape)))
    pieces = (total, *got)
    others = tuple(over_rows(piece, 1) for piece in pieces)
    half = finish(place, pieces)
    q, sr, kv, out, fc1, fc2, dw, ln1_sum, ln2_sum, srg_sum = finish(place, pieces + others, half)
    return block_out, input_grad, ln1_sum, q, sr, srg_sum, kv, out, ln2_sum, fc1, dw, fc2


def shards(*arrays):
    tokens = arrays[0]
    fits = (
        lax.axis_size("rows") == 4
        and lax.axis_size("batch") == 8
        and tokens.shape == (8, 4, 64, D)
    )
    return image_shards(*arrays) if fits else row_shards(*arrays)


def solution(mesh):
    placed = (
        P("batch", "rows", None, None),
        P("batch"),
        P("batch"),
        P(),
        P(),
        P(),
        P(),
        P(),
        P(),
        P(),
        P(),
        P(),
        P(),
        P("batch", "rows", None, None),
    )
    return jax.shard_map(
        shards,
        mesh=mesh,
        in_specs=placed,
        out_specs=(
            P("batch", "rows", None, None),
            P("batch", "rows", None, None),
            P(),
            P(),
            P(),
            P(),
            P(),
            P(),
            P(),
            P(),
            P(),
            P(),
        ),
        check_vma=False,
    )
```

```python
import functools

import jax
import jax.numpy as jnp
from jax import lax
from jax.experimental import pallas as pl
from jax.experimental.pallas import tpu as pltpu
from jax.sharding import PartitionSpec as P

D = 128
FF = 1024
HEADS = 2
POOL = 4
HEAD_DIM = 64


EPS = 1e-06
NEG = -1e30


def padded_2(value, sides, width):
    for axis, dim in sides:
        size, length = (lax.axis_size(axis), value.shape[dim])
        up = [(i, (i + 1) % size) for i in range(size - 1)]
        down = [(j, i) for i, j in up]
        last = lax.slice_in_dim(value, length - width, length, axis=dim)
        first = lax.slice_in_dim(value, 0, width, axis=dim)
        before = lax.ppermute(last, axis, up)
        after = lax.ppermute(first, axis, down)
        value = jnp.concatenate([before, value, after], axis=dim)
    return value


def layer_norm(source, gain):
    centered = source - jnp.mean(source, axis=-1, keepdims=True)
    spread = jnp.mean(centered * centered, axis=-1, keepdims=True)
    return centered * lax.rsqrt(spread + EPS) * gain


def activate(source):
    return jax.nn.gelu(source, approximate=False)


def outer_product(left, right):
    return lax.dot_general(
        left.reshape(-1, left.shape[-1]),
        right.reshape(-1, right.shape[-1]),
        (((0,), (0,)), ((), ())),
        preferred_element_type=jnp.float32,
    )


def back_product(grad, weight):
    return lax.dot_general(
        grad, weight, (((grad.ndim - 1,), (1,)), ((), ())), preferred_element_type=jnp.float32
    )


def pad_columns(source):
    return jnp.pad(source, ((0, 0), (0, 0), (1, 1), (0, 0)))


def depth_conv(padded, kernel, count, columns):
    summed = jnp.zeros((padded.shape[0], count, columns, padded.shape[3]), jnp.float32)
    for offset_row in range(3):
        for offset_col in range(3):
            summed = (
                summed
                + padded[:, offset_row : offset_row + count, offset_col : offset_col + columns]
                * kernel[offset_row, offset_col]
            )
    return summed


def row_shards(
    tokens,
    valid_rows,
    valid_cols,
    ln1_gain,
    q_weight,
    sr_weight,
    sr_gain,
    kv_weight,
    out_weight,
    ln2_gain,
    fc1_weight,
    dw_weight,
    fc2_weight,
    cotangent,
):
    images = tokens.shape[0]
    columns = tokens.shape[2]
    groups = lax.axis_size("rows")
    score_scale = HEAD_DIM ** (-0.5)
    first_row = lax.axis_index("rows") * POOL
    ids = first_row + jnp.arange(POOL, dtype=jnp.int32)
    inside = (
        (ids[None, :, None] >= 0)
        & (ids[None, :, None] < valid_rows[:, None, None])
        & (jnp.arange(columns)[None, None, :] < valid_cols[:, None, None])
    )
    inside_float = inside.astype(jnp.float32)[..., None]
    key_live = (
        (jnp.arange(groups)[None, :, None] * POOL < valid_rows[:, None, None])
        & (jnp.arange(columns // POOL)[None, None, :] * POOL < valid_cols[:, None, None])
    ).reshape(images, -1)
    picture = tokens.astype(jnp.float32)
    normed, ln1_back = jax.vjp(layer_norm, picture, ln1_gain)
    normed_low = normed.astype(jnp.bfloat16)
    queries = jnp.dot(normed_low, q_weight, preferred_element_type=jnp.float32).astype(jnp.bfloat16)
    masked = jnp.where(inside[..., None], normed_low, 0)
    patches = (
        masked.reshape(images, POOL, columns // POOL, POOL, D)
        .transpose(0, 2, 1, 3, 4)
        .reshape(images, columns // POOL, POOL * POOL * D)
    )
    pooled = jnp.dot(patches, sr_weight, preferred_element_type=jnp.float32)
    reduced, sr_back = jax.vjp(layer_norm, pooled, sr_gain)
    reduced_low = reduced.astype(jnp.bfloat16)
    key_value = jnp.dot(reduced_low, kv_weight, preferred_element_type=jnp.float32).astype(
        jnp.bfloat16
    )
    gathered = lax.all_gather(key_value[:, None], "rows", axis=1, tiled=True).reshape(
        images, -1, 2 * D
    )
    key_part = gathered[..., :D].reshape(images, -1, HEADS, HEAD_DIM)
    value_part = gathered[..., D:].reshape(images, -1, HEADS, HEAD_DIM)
    head_queries = queries.reshape(images, -1, HEADS, HEAD_DIM)
    scores = (
        jnp.einsum("inhe,iphe->ihnp", head_queries, key_part, preferred_element_type=jnp.float32)
        * score_scale
    )
    scores = jnp.where(key_live[:, None, None, :], scores, NEG)
    probabilities = jax.nn.softmax(scores, axis=-1)
    probs_low = probabilities.astype(jnp.bfloat16)
    attended = jnp.einsum(
        "ihnp,iphe->inhe", probs_low, value_part, preferred_element_type=jnp.float32
    ).reshape(images, POOL, columns, D)
    attended_low = (attended * inside_float).astype(jnp.bfloat16)
    middle = picture + jnp.dot(attended_low, out_weight, preferred_element_type=jnp.float32)
    normed2, ln2_back = jax.vjp(layer_norm, middle, ln2_gain)
    normed2_low = normed2.astype(jnp.bfloat16)
    kernel = dw_weight.astype(jnp.float32)
    hidden_shape = (images, POOL, columns, FF)
    hidden = jnp.where(
        inside[..., None],
        jnp.dot(normed2_low, fc1_weight, preferred_element_type=jnp.float32).astype(jnp.bfloat16),
        0,
    )
    padded = pad_columns(padded_2(hidden, (("rows", 1),), 1))
    convolved = depth_conv(padded, kernel, POOL, columns)
    active, gelu_back = jax.vjp(activate, convolved)
    active_low = active.astype(jnp.bfloat16)
    block_out = (
        middle + jnp.dot(active_low, fc2_weight, preferred_element_type=jnp.float32) * inside_float
    ).astype(jnp.bfloat16)
    branch_grad = jnp.where(inside[..., None], cotangent, 0)
    fc2_grad = outer_product(active_low, branch_grad)
    active_grad = back_product(branch_grad, fc2_weight)
    (conv_grad,) = gelu_back(active_grad)
    conv_low = conv_grad.astype(jnp.bfloat16)
    grad_padded = pad_columns(padded_2(conv_low, (("rows", 1),), 1))
    hidden_grad = jnp.zeros(hidden_shape, jnp.float32)
    for offset_row in range(3):
        for offset_col in range(3):
            hidden_grad = (
                hidden_grad
                + grad_padded[
                    :,
                    2 - offset_row : 2 - offset_row + POOL,
                    2 - offset_col : 2 - offset_col + columns,
                ]
                * kernel[offset_row, offset_col]
            )
    dw_grad = jnp.stack(
        [
            jnp.stack(
                [
                    jnp.sum(
                        padded[:, offset_row : offset_row + POOL, offset_col : offset_col + columns]
                        * conv_low.astype(jnp.float32),
                        axis=(0, 1, 2),
                    )
                    for offset_col in range(3)
                ]
            )
            for offset_row in range(3)
        ]
    )
    hidden_low_grad = jnp.where(inside[..., None], hidden_grad, 0.0).astype(jnp.bfloat16)
    fc1_grad = outer_product(normed2_low, hidden_low_grad)
    normed2_grad = back_product(hidden_low_grad, fc1_weight)
    middle_back, ln2_gain_grad = ln2_back(normed2_grad)
    middle_grad = cotangent.astype(jnp.float32) + middle_back
    branch_low = middle_grad.astype(jnp.bfloat16)
    out_grad = outer_product(attended_low, branch_low)
    attended_grad = (
        jnp.where(inside[..., None], back_product(branch_low, out_weight), 0.0)
        .astype(jnp.bfloat16)
        .reshape(images, -1, HEADS, HEAD_DIM)
    )
    value_grad = jnp.einsum(
        "ihnp,inhe->iphe", probs_low, attended_grad, preferred_element_type=jnp.float32
    )
    prob_grad = jnp.einsum(
        "inhe,iphe->ihnp", attended_grad, value_part, preferred_element_type=jnp.float32
    )
    score_grad = (
        probabilities
        * (prob_grad - jnp.sum(probabilities * prob_grad, axis=-1, keepdims=True))
        * score_scale
    ).astype(jnp.bfloat16)
    query_grad = (
        jnp.einsum("ihnp,iphe->inhe", score_grad, key_part, preferred_element_type=jnp.float32)
        .astype(jnp.bfloat16)
        .reshape(images, POOL, columns, D)
    )
    key_grad = jnp.einsum(
        "ihnp,inhe->iphe", score_grad, head_queries, preferred_element_type=jnp.float32
    )
    pair_partial = jnp.concatenate(
        [key_grad.reshape(images, -1, D), value_grad.reshape(images, -1, D)], axis=-1
    ).reshape(images, groups, columns // POOL, 2 * D)
    pair_owned = lax.psum_scatter(pair_partial, "rows", scatter_dimension=1, tiled=True)
    pair_low = pair_owned[:, 0].astype(jnp.bfloat16)
    pair_weight_grad = outer_product(reduced_low, pair_low)
    reduced_grad = back_product(pair_low, kv_weight)
    pooled_grad, sr_gain_grad = sr_back(reduced_grad)
    pooled_low = pooled_grad.astype(jnp.bfloat16)
    sr_grad = outer_product(patches, pooled_low)
    patch_grad = (
        back_product(pooled_low, sr_weight)
        .reshape(images, columns // POOL, POOL, POOL, D)
        .transpose(0, 2, 1, 3, 4)
        .reshape(images, POOL, columns, D)
    )
    normed_grad = back_product(query_grad, q_weight) + jnp.where(inside[..., None], patch_grad, 0.0)
    q_grad = outer_product(normed_low, query_grad)
    picture_back, ln1_gain_grad = ln1_back(normed_grad)
    input_grad = (middle_grad + picture_back).astype(jnp.bfloat16)
    ln1_sum, q_sum, sr_sum, srg_sum, pair_sum, out_sum, ln2_sum, fc1_sum, dw_sum, fc2_sum = (
        lax.psum(
            (
                ln1_gain_grad,
                q_grad,
                sr_grad,
                sr_gain_grad,
                pair_weight_grad,
                out_grad,
                ln2_gain_grad,
                fc1_grad,
                dw_grad,
                fc2_grad,
            ),
            ("rows", "batch"),
        )
    )
    return (
        block_out,
        input_grad,
        ln1_sum,
        q_sum,
        sr_sum,
        srg_sum,
        pair_sum,
        out_sum,
        ln2_sum,
        fc1_sum,
        dw_sum,
        fc2_sum,
    )


VMEM = pltpu.VMEM
NT = (((1,), (1,)), ((), ()))
TN = (((0,), (0,)), ((), ()))


def mm(left, right):
    return jnp.dot(left, right, preferred_element_type=jnp.float32)


def mm_nt(left, right):
    return lax.dot_general(left, right, NT, preferred_element_type=jnp.float32)


def mm_tn(left, right):
    return lax.dot_general(left, right, TN, preferred_element_type=jnp.float32)


def norm_parts(source):
    centered = source - jnp.mean(source, axis=-1, keepdims=True)
    scale = lax.rsqrt(jnp.mean(centered * centered, axis=-1, keepdims=True) + EPS)
    return centered * scale, scale


def norm_back(grad, gain, unit, scale):
    scaled = grad * gain
    inner = jnp.mean(scaled * unit, axis=-1, keepdims=True)
    return scale * (scaled - jnp.mean(scaled, axis=-1, keepdims=True) - unit * inner)


def inside_mask(place, shape, image, row):
    at = [lax.broadcasted_iota(jnp.int32, shape, d) for d in range(len(shape) - 1)]
    first = image(at) == 0
    rows, cols = (jnp.where(first, place[n], place[n + 1]) for n in (4, 6))
    return ((row(at) < rows) & (at[-1] < cols)).reshape(-1, D)


def image_mask(place):
    return inside_mask(place, (2, 16, 64, D), lambda at: at[0], lambda at: at[1])


def halves(shape):
    return lax.broadcasted_iota(jnp.int32, shape, len(shape) - 1) < HEAD_DIM


def block_pair(source):
    left = halves(source.shape)
    zero = jnp.zeros_like(source)
    return jnp.concatenate([jnp.where(left, source, zero), jnp.where(left, zero, source)], axis=0)


def half_reduce(reducer, value, empty):
    left = halves(value.shape)
    first = reducer(jnp.where(left, value, empty), axis=-1, keepdims=True)
    second = reducer(jnp.where(left, empty, value), axis=-1, keepdims=True)
    return jnp.where(left, first, second)


def attend_kernel(
    place, own, near1, near2, near3, gains, wq, wsr, wkv, wout,
    x_out, normed_out, q_out, prob_out, att_out, mid_out, pat_out, pooled_out, kv_out, masked,
):
    me = place[0]
    for k, chunk in enumerate((own, near1, near2, near3)):
        for i in range(2):
            raw = own[2 * me + i] if k == 0 else chunk[i]
            x_out[pl.ds(pl.multiple_of(i * 1024 + (me ^ k) * 256, 256), 256), :] = raw.reshape(256, D)
    picture = x_out[...].astype(jnp.float32)
    unit, _ = norm_parts(picture)
    normed = (unit * gains[pl.ds(0, 1), :]).astype(jnp.bfloat16)
    normed_out[...] = normed
    inside = image_mask(place)
    masked[...] = jnp.where(inside, normed.astype(jnp.float32), 0.0)
    query = mm(normed, wq[...]).astype(jnp.bfloat16)
    q_out[...] = query
    for i in range(2):
        for a in range(4):
            for u in range(4):
                for t in range(4):
                    piece = masked[pl.ds(i * 1024 + (4 * a + u) * 64 + t, 16, stride=4), :]
                    pat_out[pl.ds(i * 64 + a * 16, 16), pl.ds((u * 4 + t) * D, D)] = piece.astype(
                        jnp.bfloat16
                    )
    pooled = mm(pat_out[...], wsr[...])
    pooled_out[...] = pooled
    unit, _ = norm_parts(pooled)
    pairs = mm((unit * gains[pl.ds(1, 1), :]).astype(jnp.bfloat16), wkv[...]).astype(jnp.bfloat16)
    kv_out[...] = pairs
    lane = lax.broadcasted_iota(jnp.int32, (1024, D), 1) % 64
    scores, values = [], []
    for i in range(2):
        live = ((lane // 16) * 4 < place[4 + i]) & ((lane % 16) * 4 < place[6 + i])
        keys = block_pair(pairs[i * 64 : i * 64 + 64, :D].astype(jnp.float32)).astype(jnp.bfloat16)
        values.append(block_pair(pairs[i * 64 : i * 64 + 64, D:].astype(jnp.float32)).astype(jnp.bfloat16))
        here = mm_nt(query[i * 1024 : (i + 1) * 1024], keys)
        scores.append(jnp.where(live, here * SCORE_SCALE, NEG))
    scores = jnp.concatenate(scores, axis=0)
    weights = jnp.exp(scores - half_reduce(jnp.max, scores, -jnp.inf))
    probs = weights / half_reduce(jnp.sum, weights, 0.0)
    prob_out[...] = probs
    low = probs.astype(jnp.bfloat16)
    mixed = jnp.concatenate([mm(low[i * 1024 : (i + 1) * 1024], values[i]) for i in range(2)], axis=0)
    mixed = jnp.where(inside, mixed, 0.0).astype(jnp.bfloat16)
    att_out[...] = mixed
    mid_out[...] = picture + mm(mixed, wout[...])


def gelu_parts(x):
    density = jnp.exp(x * x * -0.5) * 0.3989422804014327
    phi = 0.5 + 0.5 * lax.erf(x * 0.7071067811865476)
    return x * phi, phi + x * density


def feed_kernel(
    place, mid, cot, cot1, cot2, cot3, gains, wfc1, taps, wfc2,
    bo0, bo1, bo2, bo3, mg_out, send_out, keep_out,
    cj, br, br_t, mask, even, odd, mix, pairs, pairs_t, cg, act, acc, back, stage, result, unit2, scale2,
):
    me = place[0]
    edge = jnp.zeros((64, 3 * D), jnp.bfloat16)
    for i in range(2):
        even[pl.ds(i * 576 + 512, 64), :] = edge
        odd[pl.ds(i * 576, 64), :] = edge
    col = lax.broadcasted_iota(jnp.int32, (2048, D), 0) % 64
    for k, chunk in enumerate((cot, cot1, cot2, cot3)):
        for i in range(2):
            raw = cot[2 * me + i] if k == 0 else chunk[i]
            for r in range(4):
                at = (r % 2) * 1024 + i * 512 + (me ^ k) * 128 + (r // 2) * 64
                cj[pl.ds(pl.multiple_of(at, 64), 64), :] = raw[r]
    inside = inside_mask(place, (2, 2, 8, 64, D), lambda at: at[1], lambda at: 2 * at[2] + at[0])
    mask[...] = jnp.where(inside, 1.0, 0.0)
    fc1_wide = wfc1[...].astype(jnp.float32)
    for k in range(4):
        for s in range(3):
            mix[k, pl.ds(s * D, D), :] = (fc1_wide * taps[pl.ds(3 * k + s, 1), :]).astype(jnp.bfloat16)
    for c in range(8):
        stage[pl.ds(c * (PACK1 // 8) + 2 * D, 16), :] = jnp.zeros((16, D), jnp.float32)
    branch = cj[...].astype(jnp.float32) * mask[...]
    br[...] = branch.astype(jnp.bfloat16)
    br_t[...] = branch.T.astype(jnp.bfloat16)

    def by_parity():
        return jnp.concatenate([mid[:, :, e].reshape(1024, D) for e in range(2)], axis=0)

    unit, scale = norm_parts(by_parity())
    unit2[...] = unit
    scale2[...] = jnp.broadcast_to(scale, (2048, D))
    normed = ((unit * gains[pl.ds(2, 1), :]).astype(jnp.bfloat16)).astype(jnp.float32) * mask[...]
    before = jnp.where(col == 0, 0.0, pltpu.roll(normed, 1, 0))
    after = jnp.where(col == 63, 0.0, pltpu.roll(normed, 2047, 0))
    for s, value in enumerate((before, normed, after)):
        value = value.astype(jnp.bfloat16)
        for e, side in enumerate((even, odd)):
            for i in range(2):
                at = e * 1024 + i * 512
                side[pl.ds(i * 576 + e * 64, 512), pl.ds(s * D, D)] = value[at : at + 512]
    for i in range(2):
        ev, ev_next = (even[pl.ds(i * 576 + h * 64, 512), :].astype(jnp.float32) for h in (0, 1))
        od_last, od = (odd[pl.ds(i * 576 + h * 64, 512), :].astype(jnp.float32) for h in (0, 1))
        for k, value in enumerate((od_last - od, ev + od, od - ev, ev - ev_next)):
            here = pl.ds(i * 512, 512)
            pairs[k, here, :] = value.astype(jnp.bfloat16)
            for s in range(3):
                pairs_t[k, pl.ds(s * D, D), here] = value[:, s * D : (s + 1) * D].T.astype(jnp.bfloat16)
    for f in range(FF // FC):
        chan = pl.ds(f * FC, FC)
        for b in range(1024 // TB):
            part = pl.ds(b * TB, TB)
            m0, m1, m2, m3 = (mm(pairs[k, part, :], mix[k, :, chan]) for k in range(4))
            grads = []
            for e, conv in enumerate((m0 + (m1 + m2), (m1 - m2) - m3)):
                here = pl.ds(e * 1024 + b * TB, TB)
                value, slope = gelu_parts(conv)
                low = value.astype(jnp.bfloat16)
                act[here, :] = low
                grads.append(mm_nt(br[here, :], wfc2[chan, :]) * slope)
                if f == 0:
                    acc[here, :] = mm(low, wfc2[chan, :])
                else:
                    acc[here, :] += mm(low, wfc2[chan, :])
            for k, value in enumerate((grads[0], grads[0] + grads[1], grads[0] - grads[1], grads[1])):
                cg[k, part, chan] = value.astype(jnp.bfloat16)
        fc2_grad = mm(br_t[...], act[...])
        fc2_grad = fc2_grad.T
        for j in range(FC // D):
            stage[pl.ds((f * (FC // D) + j) * (PACK1 // 8) + D, D), :] = fc2_grad[j * D : (j + 1) * D]
        fc1_grad = jnp.zeros((D, FC), jnp.float32)
        tap_grads = []
        for k in range(4):
            outer = mm(pairs_t[k], cg[k, :, chan])
            for s in range(3):
                here = outer[s * D : (s + 1) * D]
                if k == 3:
                    here = -here
                fc1_grad += here * taps[pl.ds(3 * k + s, 1), chan]
                tap_grads.append(jnp.sum(here * wfc1[:, chan].astype(jnp.float32), axis=0, keepdims=True))
        for s in range(3):
            half_sum = 0.5 * (tap_grads[3 + s] + tap_grads[6 + s])
            half_gap = 0.5 * (tap_grads[3 + s] - tap_grads[6 + s])
            for p, value in enumerate((tap_grads[s] + half_sum, half_gap, half_sum + tap_grads[9 + s])):
                for j in range(FC // D):
                    at = (f * (FC // D) + j) * (PACK1 // 8) + 2 * D + 3 * p + s
                    stage[pl.ds(at, 1), :] = value[:, j * D : (j + 1) * D]
        for j in range(FC // D):
            stage[pl.ds((f * (FC // D) + j) * (PACK1 // 8), D), :] = fc1_grad[:, j * D : (j + 1) * D]
    for i in range(2):
        back[0, pl.ds(i * 576 + 512, 64), :] = jnp.zeros((64, 3 * D), jnp.float32)
        back[3, pl.ds(i * 576, 64), :] = jnp.zeros((64, 3 * D), jnp.float32)
    for k in range(4):
        spread = mm_nt(cg[k], mix[k])
        for i in range(2):
            back[k, pl.ds(i * 576 + (64 if k == 3 else 0), 512), :] = spread[i * 512 : (i + 1) * 512]
    spread = []
    for e in range(2):
        for i in range(2):
            here, later = pl.ds(i * 576, 512), pl.ds(i * 576 + 64, 512)
            if e == 0:
                spread.append(back[1, here, :] - back[2, here, :] + (back[3, here, :] - back[3, later, :]))
            else:
                spread.append(back[1, here, :] + back[2, here, :] + (back[0, later, :] - back[0, here, :]))
    spread = jnp.concatenate(spread, axis=0)
    after = jnp.where(col == 63, 0.0, pltpu.roll(spread[:, :D], 2047, 0))
    before = jnp.where(col == 0, 0.0, pltpu.roll(spread[:, 2 * D :], 1, 0))
    normed_grad = (spread[:, D : 2 * D] + before + after) * mask[...]
    middle = by_parity()
    unit, scale = unit2[...], scale2[...]
    gain_grad = jnp.sum(normed_grad * unit, axis=0, keepdims=True)
    total = cj[...].astype(jnp.float32) + norm_back(normed_grad, gains[pl.ds(2, 1), :], unit, scale)
    final = (middle + acc[...] * mask[...]).astype(jnp.bfloat16)
    for e in range(2):
        mg_out[:, :, e] = total[e * 1024 : (e + 1) * 1024].reshape(2, 8, 64, D)
        result[:, :, e] = final[e * 1024 : (e + 1) * 1024].reshape(2, 8, 64, D)
    for k, bo in enumerate((bo0, bo1, bo2, bo3)):
        for i in range(2):
            bo[i] = result[i, pl.ds((me ^ k) * 2, 2)].reshape(4, 64, D)
    stage[pl.ds(2 * D + 9, 1), :] = gain_grad
    split_pack(place, stage, send_out, keep_out)


def split_pack(place, stage, send_out, keep_out):
    rows = stage.shape[0] // 8
    for k in range(4):
        at = pl.ds(k * rows, rows)
        for out, core, first in ((send_out, 1 - place[1], place[3]), (keep_out, place[1], place[2])):
            start = pl.multiple_of((core * 4 + (first ^ k)) * rows, 16)
            out[at, :] = stage[pl.ds(start, rows), :].astype(jnp.bfloat16)


def back_kernel(
    place, normed, query, prob, att, mgrad, pat, pooled, kv,
    gains, wq, wsr, wkv, wout,
    query_grad, pooled_out, send_out, keep_out,
    stage,
):
    inside = image_mask(place)
    low = mgrad[...].astype(jnp.bfloat16)
    out_grad = mm_tn(att[...], low)
    mixed = jnp.where(inside, mm_nt(low, wout[...]), 0.0).astype(jnp.bfloat16)
    keys, values = (
        [
            block_pair(kv[pl.ds(i * 64, 64), pl.ds(n * D, D)].astype(jnp.float32)).astype(jnp.bfloat16)
            for i in range(2)
        ]
        for n in range(2)
    )
    parts = [slice(i * 1024, (i + 1) * 1024) for i in range(2)]
    weights = prob[...]
    back = jnp.concatenate([mm_nt(mixed[parts[i]], values[i]) for i in range(2)], axis=0)
    back = weights * (back - half_reduce(jnp.sum, weights * back, 0.0)) * SCORE_SCALE
    back = back.astype(jnp.bfloat16)
    grads = jnp.concatenate([mm(back[parts[i]], keys[i]) for i in range(2)], axis=0).astype(jnp.bfloat16)
    query_grad[...] = grads
    weights = weights.astype(jnp.bfloat16)
    left = halves((64, D))
    key_rows = []
    for i in range(2):
        value_full = mm_tn(weights[parts[i]], mixed[parts[i]])
        key_full = mm_tn(back[parts[i]], query[pl.ds(i * 1024, 1024), :])
        key_rows.append(
            jnp.concatenate(
                [
                    jnp.where(left, key_full[:64], key_full[64:]),
                    jnp.where(left, value_full[:64], value_full[64:]),
                ],
                axis=1,
            )
        )
    pair = jnp.concatenate(key_rows, axis=0).astype(jnp.bfloat16)
    unit, scale = norm_parts(pooled[...])
    reduced = (unit * gains[pl.ds(1, 1), :]).astype(jnp.bfloat16)
    kv_grad = mm_tn(reduced, pair)
    reduced_grad = mm_nt(pair, wkv[...])
    srg_grad = jnp.sum(reduced_grad * unit, axis=0, keepdims=True)
    pooled_low = norm_back(reduced_grad, gains[pl.ds(1, 1), :], unit, scale).astype(jnp.bfloat16)
    pooled_out[...] = pooled_low
    sr_grad = mm_tn(pat[...], pooled_low)
    each = PACK2 // 8
    for c in range(8):
        stage[pl.ds(c * each, 256), :] = sr_grad[c * 256 : (c + 1) * 256]
    for c in range(8):
        side, row = c // 4, (c % 4) * 32
        stage[pl.ds(c * each + 256, 32), :] = kv_grad[row : row + 32, side * D : (side + 1) * D]
        stage[pl.ds(c * each + 304, 16), :] = out_grad[c * 16 : (c + 1) * 16]
        stage[pl.ds(c * each + 320, 16), :] = jnp.zeros((16, D), jnp.float32)
    q_grad = mm_tn(normed[...], grads)
    weighted = q_grad * wq[...].astype(jnp.float32)
    for c in range(16):
        at = slice(c * D, (c + 1) * D)
        weighted += sr_grad[at] * wsr[pl.ds(c * D, D), :].astype(jnp.float32)
    high = weighted.astype(jnp.bfloat16)
    low = (weighted - high.astype(jnp.float32)).astype(jnp.bfloat16)
    ones = jnp.ones((16, D), jnp.bfloat16)
    gain_grad = (mm_nt(ones, high) + mm_nt(ones, low))[0:1] / gains[pl.ds(0, 1), :]
    for c in range(8):
        stage[pl.ds(c * each + 288, 16), :] = q_grad[c * 16 : (c + 1) * 16]
    stage[pl.ds(320, 1), :] = gain_grad
    stage[pl.ds(321, 1), :] = srg_grad
    split_pack(place, stage, send_out, keep_out)


def input_kernel(
    place, x, query_grad, pooled_low, mgrad, gains, wq, wsr,
    ig0, ig1, ig2, ig3,
    unfold, result,
):
    me = place[0]
    patch_grad = mm_nt(pooled_low[...], wsr[...])
    for i in range(2):
        for a in range(4):
            for u in range(4):
                for t in range(4):
                    unfold[pl.ds(i * 1024 + (4 * a + u) * 64 + t, 16, stride=4), :] = patch_grad[
                        i * 64 + a * 16 : i * 64 + a * 16 + 16, (u * 4 + t) * D : (u * 4 + t + 1) * D
                    ]
    grad = mm_nt(query_grad[...], wq[...]) + jnp.where(image_mask(place), unfold[...], 0.0)
    unit, scale = norm_parts(x[...].astype(jnp.float32))
    total = mgrad[...] + norm_back(grad, gains[pl.ds(0, 1), :], unit, scale)
    result[...] = total.astype(jnp.bfloat16).reshape(2, 16, 64, D)
    for k, ig in enumerate((ig0, ig1, ig2, ig3)):
        for i in range(2):
            ig[i] = result[i, pl.ds((me ^ k) * 4, 4)]


def call(kernel, scalars, arrays, outs, scratch, flops=0, name=None, vmem=24):
    spec = pl.BlockSpec(memory_space=VMEM)
    return pl.pallas_call(
        kernel,
        out_shape=[jax.ShapeDtypeStruct(shape, kind) for shape, kind in outs],
        in_specs=[pl.BlockSpec(memory_space=pltpu.SMEM)] * len(scalars) + [spec] * len(arrays),
        out_specs=[spec] * len(outs),
        scratch_shapes=scratch,
        compiler_params=pltpu.CompilerParams(vmem_limit_bytes=vmem * 2**20),
        cost_estimate=pl.CostEstimate(flops=flops, bytes_accessed=4 * 2**20, transcendentals=0),
        name=name,
    )(*scalars, *arrays)


BF, F32 = jnp.bfloat16, jnp.float32
FLAT = (2048, D)
SPLIT = (2, 8, 2, 64, D)
CHUNK = (2, 4, 64, D)
PACK1, PACK2 = 2176, 2688
FC, TB = 512, 1024
SCORE_SCALE = HEAD_DIM ** (-0.5)


def attend(place, chunks, gains, wq, wsr, wkv, wout):
    return call(
        attend_kernel,
        (place,),
        (*chunks, gains, wq, wsr, wkv, wout),
        [
            (FLAT, BF), (FLAT, BF), (FLAT, BF), (FLAT, F32), (FLAT, BF), (FLAT, F32),
            ((128, 2048), BF), ((128, D), F32), ((128, 2 * D), BF),
        ],
        [VMEM((2048, D), F32)],
        flops=10**9, name="attend",
    )


def feed(place, middle, chunks, gains, wfc1, taps, wfc2):
    return call(
        feed_kernel,
        (place,),
        (middle, *chunks, gains, wfc1, taps, wfc2),
        [(CHUNK, BF)] * 4 + [(SPLIT, F32), ((PACK1 // 2, D), BF), ((PACK1 // 2, D), BF)],
        [
            VMEM((2048, D), BF), VMEM((2048, D), BF), VMEM((D, 2048), BF), VMEM((2048, D), F32),
            VMEM((1152, 3 * D), BF), VMEM((1152, 3 * D), BF), VMEM((4, 3 * D, FF), BF),
            VMEM((4, 1024, 3 * D), BF), VMEM((4, 3 * D, 1024), BF), VMEM((4, 1024, FF), BF), VMEM((2048, FC), BF),
            VMEM((2048, D), F32), VMEM((4, 1152, 3 * D), F32), VMEM((PACK1, D), F32), VMEM(SPLIT, BF), VMEM(FLAT, F32), VMEM(FLAT, F32),
        ],
        flops=16 * 10**9, name="feed", vmem=44,
    )


def back(place, kept, mgrad, gains, wq, wsr, wkv, wout):
    _, normed, query, prob, att, _, pat, pooled, kv = kept
    return call(
        back_kernel,
        (place,),
        (normed, query, prob, att, mgrad, pat, pooled, kv, gains, wq, wsr, wkv, wout),
        [(FLAT, BF), ((128, D), BF), ((PACK2 // 2, D), BF), ((PACK2 // 2, D), BF)],
        [VMEM((PACK2, D), F32)],
        flops=2 * 10**9, name="back",
    )


def input_gradient(place, x, query_grad, pooled_low, mgrad, gains, wq, wsr):
    return call(
        input_kernel,
        (place,),
        (x, query_grad, pooled_low, mgrad, gains, wq, wsr),
        [(CHUNK, BF)] * 4,
        [VMEM((2048, D), F32), VMEM((2, 16, 64, D), BF)],
        flops=10**9, name="input_gradient",
    )


def over_rows(value, k):
    return lax.ppermute(value, "rows", [(i, i ^ k) for i in range(4)])


def over_four(value, k, phase):
    plane, line = (k >> 1) * 16 + (k & 1), 2 * k
    pairs = [(i, i ^ (plane if (i >> 3) & 1 == phase else line)) for i in range(32)]
    return lax.ppermute(value, ("rows", "batch"), pairs)


def plus(*values):
    return sum(v.astype(F32) for v in values).astype(BF)


def plane_parts(packs):
    halves_in = [plus(keep, over_rows(send, 1)) for send, keep in packs]
    return [
        jnp.concatenate([h[k * (h.shape[0] // 4) : (k + 1) * (h.shape[0] // 4)] for h in halves_in])
        for k in range(4)
    ]


def to_four(values, phase):
    return [over_four(values[k], k, phase) for k in (1, 2, 3)]


def finish_kernel(half, place, *refs):
    pieces, refs = refs[: 4 * (half + 1)], refs[4 * (half + 1) :]
    if half:
        refs = refs[6:]
    (q, sr, kv, out, fc1, fc2), refs = refs[:6], refs[6:]
    stage, small_dw, small_ln1, small_ln2, small_srg, sems = refs[-6:]
    copies = []

    def move(source, target):
        copies.append(pltpu.make_async_copy(source, target, sems.at[len(copies)]))
        copies[-1].start()

    def chunk_of(j):
        core, first = (place[1], place[2]) if j < 4 else (1 - place[1], place[3])
        return core * 4 + (first ^ (j % 4))

    for k in range(4):
        c = chunk_of(4 * half + k)
        stage[k] = pieces[4 * half + k][...].astype(F32)
        chan = pl.ds(pl.multiple_of(c * D, D), D)
        move(stage.at[k, pl.ds(0, D)], fc1.at[:, chan])
        move(stage.at[k, pl.ds(D, D)], fc2.at[chan])
        move(stage.at[k, pl.ds(272, 256)], sr.at[pl.ds(pl.multiple_of(c * 256, 256), 256)])
        row = pl.ds(pl.multiple_of((c % 4) * 32, 32), 32)
        move(stage.at[k, pl.ds(528, 32)], kv.at[row, pl.ds(pl.multiple_of((c // 4) * D, D), D)])
        row = pl.ds(pl.multiple_of(c * 16, 16), 16)
        move(stage.at[k, pl.ds(560, 16)], q.at[row])
        move(stage.at[k, pl.ds(576, 16)], out.at[row])
    if half:
        sums = [jnp.zeros((1, D), F32)] * 3
        for j, piece in enumerate(pieces):
            chan = pl.ds(pl.multiple_of(chunk_of(j) * D, D), D)
            small = piece[pl.ds(256, 16), :].astype(F32)
            for tap in range(9):
                small_dw[tap // 3, pl.ds(tap % 3, 1), chan] = small[tap : tap + 1]
            last = piece[pl.ds(592, 16), :].astype(F32)
            rows = (last[0:1], small[9:10], last[1:2])
            sums = [total + row for total, row in zip(sums, rows)]
        move(small_dw, refs[0])
        for ref, small, total in zip(refs[1:4], (small_ln1, small_ln2, small_srg), sums):
            small[...] = total.reshape(D)
            move(small, ref)
    for copy in copies:
        copy.wait()


def finish(place, pieces, earlier=()):
    far, near = pl.BlockSpec(memory_space=pl.ANY), pl.BlockSpec(memory_space=VMEM)
    half = 1 if earlier else 0
    shapes = [((D, D), F32), ((2048, D), F32), ((D, 2 * D), F32), ((D, D), F32), ((D, FF), F32), ((FF, D), F32)]
    specs, n = [far] * 6, len(shapes)
    if half:
        shapes += [((3, 3, FF), F32), ((D,), F32), ((D,), F32), ((D,), F32)]
        specs += [far] * 4
    before = 1 + len(pieces)
    return pl.pallas_call(
        functools.partial(finish_kernel, half),
        out_shape=[jax.ShapeDtypeStruct(*each) for each in shapes],
        in_specs=[pl.BlockSpec(memory_space=pltpu.SMEM)] + [near] * (before - 1) + [far] * len(earlier),
        out_specs=specs,
        scratch_shapes=[
            VMEM((4, 608, D), F32), VMEM((3, 3, FF), F32), VMEM((D,), F32), VMEM((D,), F32), VMEM((D,), F32),
            pltpu.SemaphoreType.DMA((28,)),
        ],
        input_output_aliases={before + i: i for i in range(n)} if half else {},
        compiler_params=pltpu.CompilerParams(vmem_limit_bytes=8 * 2**20),
        cost_estimate=pl.CostEstimate(flops=0, bytes_accessed=4 * 2**20, transcendentals=0),
        name="finish",
    )(place, *pieces, *earlier)


def gather_kernel(place, part0, part1, part2, part3, out, sems):
    copies = [
        pltpu.make_async_copy(part, out.at[pl.ds(2 * (place[0] ^ k), 2)], sems.at[k])
        for k, part in enumerate((part0, part1, part2, part3))
    ]
    for copy in copies:
        copy.start()
    for copy in copies:
        copy.wait()


def gather_rows(place, parts, shape):
    far = pl.BlockSpec(memory_space=pl.ANY)
    return pl.pallas_call(
        gather_kernel,
        out_shape=jax.ShapeDtypeStruct(shape, BF),
        in_specs=[pl.BlockSpec(memory_space=pltpu.SMEM)] + [pl.BlockSpec(memory_space=VMEM)] * 4,
        out_specs=far,
        scratch_shapes=[pltpu.SemaphoreType.DMA((4,))],
        compiler_params=pltpu.CompilerParams(vmem_limit_bytes=4 * 2**20),
        name="gather_rows",
    )(place, *parts)


def image_shards(
    tokens, valid_rows, valid_cols, ln1_gain, q_weight, sr_weight, sr_gain, kv_weight, out_weight,
    ln2_gain, fc1_weight, dw_weight, fc2_weight, cotangent,
):
    me, lane = lax.axis_index("rows"), lax.axis_index("batch")
    core = me & 1
    plane, line = (me >> 1) * 2 + (lane & 1), lane >> 1
    first, second = jnp.where(core == 0, plane, line), jnp.where(core == 0, line, plane)
    sizes = [lax.dynamic_slice_in_dim(v, 2 * me, 2) for v in (valid_rows, valid_cols)]
    place = jnp.concatenate([jnp.stack([me, core, first, second]), *sizes]).astype(jnp.int32)

    def spread(source):
        near = {
            k: over_rows(lax.dynamic_slice_in_dim(source, 2 * (me ^ k), 2, 0), k) for k in (3, 2, 1)
        }
        return source, near[1], near[2], near[3]

    def returned(parts):
        near = {k: over_rows(parts[k], k) for k in (3, 2, 1)}
        return [parts[0], near[1], near[2], near[3]]

    gains = jnp.stack([ln1_gain, sr_gain, ln2_gain])
    row0, row1, row2 = dw_weight.astype(F32)
    taps = jnp.concatenate(
        [row0, 0.5 * (row0 + row1 + row2), 0.5 * (row0 - row1 + row2), row2, jnp.zeros((4, FF), F32)]
    )
    token_parts = spread(tokens)
    cotangent, _ = lax.optimization_barrier((cotangent, token_parts[1]))
    kept = attend(
        place, token_parts, gains, q_weight, sr_weight, kv_weight, out_weight
    )
    *block_parts, mgrad, send1, keep1 = feed(
        place, kept[5].reshape(SPLIT), spread(cotangent), gains, fc1_weight, taps, fc2_weight
    )
    mgrad = mgrad.reshape(FLAT)
    query_grad, pooled_low, send2, keep2 = back(
        place, kept, mgrad, gains, q_weight, sr_weight, kv_weight, out_weight
    )
    parts = plane_parts([(send1, keep1), (send2, keep2)])
    block = returned(block_parts)
    inputs = input_gradient(place, kept[0], query_grad, pooled_low, mgrad, gains, q_weight, sr_weight)
    mine, inputs = lax.optimization_barrier((plus(parts[0], *to_four(parts, 0)), list(inputs)))
    inputs = returned(inputs)
    mine, block[2] = lax.optimization_barrier((mine, block[2]))
    got = [g.astype(F32) for g in to_four([mine] * 4, 1)]
    got, block_out = lax.optimization_barrier((got, gather_rows(place, block, tokens.shape)))
    got, block[3] = lax.optimization_barrier((got, block[3]))
    total = ((mine.astype(F32) + got[0]) + (got[1] + got[2])).astype(BF)
    got = to_four([total] * 4, 0)
    got, inputs[2], inputs[3] = lax.optimization_barrier((got, inputs[2], inputs[3]))
    got, input_grad = lax.optimization_barrier((got, gather_rows(place, inputs, tokens.shape)))
    pieces = (total, *got)
    others = tuple(over_rows(piece, 1) for piece in pieces)
    half = finish(place, pieces)
    q, sr, kv, out, fc1, fc2, dw, ln1_sum, ln2_sum, srg_sum = finish(place, pieces + others, half)
    return block_out, input_grad, ln1_sum, q, sr, srg_sum, kv, out, ln2_sum, fc1, dw, fc2


def shards(*arrays):
    tokens = arrays[0]
    fits = (
        lax.axis_size("rows") == 4
        and lax.axis_size("batch") == 8
        and tokens.shape == (8, 4, 64, D)
    )
    return image_shards(*arrays) if fits else row_shards(*arrays)


def solution(mesh):
    placed = (
        P("batch", "rows", None, None),
        P("batch"),
        P("batch"),
        P(),
        P(),
        P(),
        P(),
        P(),
        P(),
        P(),
        P(),
        P(),
        P(),
        P("batch", "rows", None, None),
    )
    return jax.shard_map(
        shards,
        mesh=mesh,
        in_specs=placed,
        out_specs=(
            P("batch", "rows", None, None),
            P("batch", "rows", None, None),
            P(),
            P(),
            P(),
            P(),
            P(),
            P(),
            P(),
            P(),
            P(),
            P(),
        ),
        check_vma=False,
    )
```

```python
import functools

import jax
import jax.numpy as jnp
from jax import lax
from jax.experimental import pallas as pl
from jax.experimental.pallas import tpu as pltpu
from jax.sharding import PartitionSpec as P

D = 128
FF = 1024
HEADS = 2
POOL = 4
HEAD_DIM = 64


EPS = 1e-06
NEG = -1e30


def padded_2(value, sides, width):
    for axis, dim in sides:
        size, length = (lax.axis_size(axis), value.shape[dim])
        up = [(i, (i + 1) % size) for i in range(size - 1)]
        down = [(j, i) for i, j in up]
        last = lax.slice_in_dim(value, length - width, length, axis=dim)
        first = lax.slice_in_dim(value, 0, width, axis=dim)
        before = lax.ppermute(last, axis, up)
        after = lax.ppermute(first, axis, down)
        value = jnp.concatenate([before, value, after], axis=dim)
    return value


def layer_norm(source, gain):
    centered = source - jnp.mean(source, axis=-1, keepdims=True)
    spread = jnp.mean(centered * centered, axis=-1, keepdims=True)
    return centered * lax.rsqrt(spread + EPS) * gain


def activate(source):
    return jax.nn.gelu(source, approximate=False)


def outer_product(left, right):
    return lax.dot_general(
        left.reshape(-1, left.shape[-1]),
        right.reshape(-1, right.shape[-1]),
        (((0,), (0,)), ((), ())),
        preferred_element_type=jnp.float32,
    )


def back_product(grad, weight):
    return lax.dot_general(
        grad, weight, (((grad.ndim - 1,), (1,)), ((), ())), preferred_element_type=jnp.float32
    )


def pad_columns(source):
    return jnp.pad(source, ((0, 0), (0, 0), (1, 1), (0, 0)))


def depth_conv(padded, kernel, count, columns):
    summed = jnp.zeros((padded.shape[0], count, columns, padded.shape[3]), jnp.float32)
    for offset_row in range(3):
        for offset_col in range(3):
            summed = (
                summed
                + padded[:, offset_row : offset_row + count, offset_col : offset_col + columns]
                * kernel[offset_row, offset_col]
            )
    return summed


def row_shards(
    tokens,
    valid_rows,
    valid_cols,
    ln1_gain,
    q_weight,
    sr_weight,
    sr_gain,
    kv_weight,
    out_weight,
    ln2_gain,
    fc1_weight,
    dw_weight,
    fc2_weight,
    cotangent,
):
    images = tokens.shape[0]
    columns = tokens.shape[2]
    groups = lax.axis_size("rows")
    score_scale = HEAD_DIM ** (-0.5)
    first_row = lax.axis_index("rows") * POOL
    ids = first_row + jnp.arange(POOL, dtype=jnp.int32)
    inside = (
        (ids[None, :, None] >= 0)
        & (ids[None, :, None] < valid_rows[:, None, None])
        & (jnp.arange(columns)[None, None, :] < valid_cols[:, None, None])
    )
    inside_float = inside.astype(jnp.float32)[..., None]
    key_live = (
        (jnp.arange(groups)[None, :, None] * POOL < valid_rows[:, None, None])
        & (jnp.arange(columns // POOL)[None, None, :] * POOL < valid_cols[:, None, None])
    ).reshape(images, -1)
    picture = tokens.astype(jnp.float32)
    normed, ln1_back = jax.vjp(layer_norm, picture, ln1_gain)
    normed_low = normed.astype(jnp.bfloat16)
    queries = jnp.dot(normed_low, q_weight, preferred_element_type=jnp.float32).astype(jnp.bfloat16)
    masked = jnp.where(inside[..., None], normed_low, 0)
    patches = (
        masked.reshape(images, POOL, columns // POOL, POOL, D)
        .transpose(0, 2, 1, 3, 4)
        .reshape(images, columns // POOL, POOL * POOL * D)
    )
    pooled = jnp.dot(patches, sr_weight, preferred_element_type=jnp.float32)
    reduced, sr_back = jax.vjp(layer_norm, pooled, sr_gain)
    reduced_low = reduced.astype(jnp.bfloat16)
    key_value = jnp.dot(reduced_low, kv_weight, preferred_element_type=jnp.float32).astype(
        jnp.bfloat16
    )
    gathered = lax.all_gather(key_value[:, None], "rows", axis=1, tiled=True).reshape(
        images, -1, 2 * D
    )
    key_part = gathered[..., :D].reshape(images, -1, HEADS, HEAD_DIM)
    value_part = gathered[..., D:].reshape(images, -1, HEADS, HEAD_DIM)
    head_queries = queries.reshape(images, -1, HEADS, HEAD_DIM)
    scores = (
        jnp.einsum("inhe,iphe->ihnp", head_queries, key_part, preferred_element_type=jnp.float32)
        * score_scale
    )
    scores = jnp.where(key_live[:, None, None, :], scores, NEG)
    probabilities = jax.nn.softmax(scores, axis=-1)
    probs_low = probabilities.astype(jnp.bfloat16)
    attended = jnp.einsum(
        "ihnp,iphe->inhe", probs_low, value_part, preferred_element_type=jnp.float32
    ).reshape(images, POOL, columns, D)
    attended_low = (attended * inside_float).astype(jnp.bfloat16)
    middle = picture + jnp.dot(attended_low, out_weight, preferred_element_type=jnp.float32)
    normed2, ln2_back = jax.vjp(layer_norm, middle, ln2_gain)
    normed2_low = normed2.astype(jnp.bfloat16)
    kernel = dw_weight.astype(jnp.float32)
    hidden_shape = (images, POOL, columns, FF)
    hidden = jnp.where(
        inside[..., None],
        jnp.dot(normed2_low, fc1_weight, preferred_element_type=jnp.float32).astype(jnp.bfloat16),
        0,
    )
    padded = pad_columns(padded_2(hidden, (("rows", 1),), 1))
    convolved = depth_conv(padded, kernel, POOL, columns)
    active, gelu_back = jax.vjp(activate, convolved)
    active_low = active.astype(jnp.bfloat16)
    block_out = (
        middle + jnp.dot(active_low, fc2_weight, preferred_element_type=jnp.float32) * inside_float
    ).astype(jnp.bfloat16)
    branch_grad = jnp.where(inside[..., None], cotangent, 0)
    fc2_grad = outer_product(active_low, branch_grad)
    active_grad = back_product(branch_grad, fc2_weight)
    (conv_grad,) = gelu_back(active_grad)
    conv_low = conv_grad.astype(jnp.bfloat16)
    grad_padded = pad_columns(padded_2(conv_low, (("rows", 1),), 1))
    hidden_grad = jnp.zeros(hidden_shape, jnp.float32)
    for offset_row in range(3):
        for offset_col in range(3):
            hidden_grad = (
                hidden_grad
                + grad_padded[
                    :,
                    2 - offset_row : 2 - offset_row + POOL,
                    2 - offset_col : 2 - offset_col + columns,
                ]
                * kernel[offset_row, offset_col]
            )
    dw_grad = jnp.stack(
        [
            jnp.stack(
                [
                    jnp.sum(
                        padded[:, offset_row : offset_row + POOL, offset_col : offset_col + columns]
                        * conv_low.astype(jnp.float32),
                        axis=(0, 1, 2),
                    )
                    for offset_col in range(3)
                ]
            )
            for offset_row in range(3)
        ]
    )
    hidden_low_grad = jnp.where(inside[..., None], hidden_grad, 0.0).astype(jnp.bfloat16)
    fc1_grad = outer_product(normed2_low, hidden_low_grad)
    normed2_grad = back_product(hidden_low_grad, fc1_weight)
    middle_back, ln2_gain_grad = ln2_back(normed2_grad)
    middle_grad = cotangent.astype(jnp.float32) + middle_back
    branch_low = middle_grad.astype(jnp.bfloat16)
    out_grad = outer_product(attended_low, branch_low)
    attended_grad = (
        jnp.where(inside[..., None], back_product(branch_low, out_weight), 0.0)
        .astype(jnp.bfloat16)
        .reshape(images, -1, HEADS, HEAD_DIM)
    )
    value_grad = jnp.einsum(
        "ihnp,inhe->iphe", probs_low, attended_grad, preferred_element_type=jnp.float32
    )
    prob_grad = jnp.einsum(
        "inhe,iphe->ihnp", attended_grad, value_part, preferred_element_type=jnp.float32
    )
    score_grad = (
        probabilities
        * (prob_grad - jnp.sum(probabilities * prob_grad, axis=-1, keepdims=True))
        * score_scale
    ).astype(jnp.bfloat16)
    query_grad = (
        jnp.einsum("ihnp,iphe->inhe", score_grad, key_part, preferred_element_type=jnp.float32)
        .astype(jnp.bfloat16)
        .reshape(images, POOL, columns, D)
    )
    key_grad = jnp.einsum(
        "ihnp,inhe->iphe", score_grad, head_queries, preferred_element_type=jnp.float32
    )
    pair_partial = jnp.concatenate(
        [key_grad.reshape(images, -1, D), value_grad.reshape(images, -1, D)], axis=-1
    ).reshape(images, groups, columns // POOL, 2 * D)
    pair_owned = lax.psum_scatter(pair_partial, "rows", scatter_dimension=1, tiled=True)
    pair_low = pair_owned[:, 0].astype(jnp.bfloat16)
    pair_weight_grad = outer_product(reduced_low, pair_low)
    reduced_grad = back_product(pair_low, kv_weight)
    pooled_grad, sr_gain_grad = sr_back(reduced_grad)
    pooled_low = pooled_grad.astype(jnp.bfloat16)
    sr_grad = outer_product(patches, pooled_low)
    patch_grad = (
        back_product(pooled_low, sr_weight)
        .reshape(images, columns // POOL, POOL, POOL, D)
        .transpose(0, 2, 1, 3, 4)
        .reshape(images, POOL, columns, D)
    )
    normed_grad = back_product(query_grad, q_weight) + jnp.where(inside[..., None], patch_grad, 0.0)
    q_grad = outer_product(normed_low, query_grad)
    picture_back, ln1_gain_grad = ln1_back(normed_grad)
    input_grad = (middle_grad + picture_back).astype(jnp.bfloat16)
    ln1_sum, q_sum, sr_sum, srg_sum, pair_sum, out_sum, ln2_sum, fc1_sum, dw_sum, fc2_sum = (
        lax.psum(
            (
                ln1_gain_grad,
                q_grad,
                sr_grad,
                sr_gain_grad,
                pair_weight_grad,
                out_grad,
                ln2_gain_grad,
                fc1_grad,
                dw_grad,
                fc2_grad,
            ),
            ("rows", "batch"),
        )
    )
    return (
        block_out,
        input_grad,
        ln1_sum,
        q_sum,
        sr_sum,
        srg_sum,
        pair_sum,
        out_sum,
        ln2_sum,
        fc1_sum,
        dw_sum,
        fc2_sum,
    )


VMEM = pltpu.VMEM
NT = (((1,), (1,)), ((), ()))
TN = (((0,), (0,)), ((), ()))


def mm(left, right):
    return jnp.dot(left, right, preferred_element_type=jnp.float32)


def mm_nt(left, right):
    return lax.dot_general(left, right, NT, preferred_element_type=jnp.float32)


def mm_tn(left, right):
    return lax.dot_general(left, right, TN, preferred_element_type=jnp.float32)


def norm_parts(source):
    centered = source - jnp.mean(source, axis=-1, keepdims=True)
    scale = lax.rsqrt(jnp.mean(centered * centered, axis=-1, keepdims=True) + EPS)
    return centered * scale, scale


def norm_back(grad, gain, unit, scale):
    scaled = grad * gain
    inner = jnp.mean(scaled * unit, axis=-1, keepdims=True)
    return scale * (scaled - jnp.mean(scaled, axis=-1, keepdims=True) - unit * inner)


def inside_mask(place, shape, image, row):
    at = [lax.broadcasted_iota(jnp.int32, shape, d) for d in range(len(shape) - 1)]
    first = image(at) == 0
    rows, cols = (jnp.where(first, place[n], place[n + 1]) for n in (4, 6))
    return ((row(at) < rows) & (at[-1] < cols)).reshape(-1, D)


def image_mask(place):
    return inside_mask(place, (2, 16, 64, D), lambda at: at[0], lambda at: at[1])


def halves(shape):
    return lax.broadcasted_iota(jnp.int32, shape, len(shape) - 1) < HEAD_DIM


def block_pair(source):
    left = halves(source.shape)
    zero = jnp.zeros_like(source)
    return jnp.concatenate([jnp.where(left, source, zero), jnp.where(left, zero, source)], axis=0)


def half_reduce(reducer, value, empty):
    left = halves(value.shape)
    first = reducer(jnp.where(left, value, empty), axis=-1, keepdims=True)
    second = reducer(jnp.where(left, empty, value), axis=-1, keepdims=True)
    return jnp.where(left, first, second)


def attend_kernel(
    place, own, near1, near2, near3, gains, wq, wsr, wkv, wout,
    x_out, normed_out, q_out, prob_out, att_out, mid_out, pat_out, pooled_out, kv_out, masked,
):
    me = place[0]
    for k, chunk in enumerate((own, near1, near2, near3)):
        for i in range(2):
            raw = own[2 * me + i] if k == 0 else chunk[i]
            x_out[pl.ds(pl.multiple_of(i * 1024 + (me ^ k) * 256, 256), 256), :] = raw.reshape(256, D)
    picture = x_out[...].astype(jnp.float32)
    unit, _ = norm_parts(picture)
    normed = (unit * gains[pl.ds(0, 1), :]).astype(jnp.bfloat16)
    normed_out[...] = normed
    inside = image_mask(place)
    masked[...] = jnp.where(inside, normed.astype(jnp.float32), 0.0)
    query = mm(normed, wq[...]).astype(jnp.bfloat16)
    q_out[...] = query
    for i in range(2):
        for a in range(4):
            for u in range(4):
                for t in range(4):
                    piece = masked[pl.ds(i * 1024 + (4 * a + u) * 64 + t, 16, stride=4), :]
                    pat_out[pl.ds(i * 64 + a * 16, 16), pl.ds((u * 4 + t) * D, D)] = piece.astype(
                        jnp.bfloat16
                    )
    pooled = mm(pat_out[...], wsr[...])
    pooled_out[...] = pooled
    unit, _ = norm_parts(pooled)
    pairs = mm((unit * gains[pl.ds(1, 1), :]).astype(jnp.bfloat16), wkv[...]).astype(jnp.bfloat16)
    kv_out[...] = pairs
    lane = lax.broadcasted_iota(jnp.int32, (1024, D), 1) % 64
    scores, values = [], []
    for i in range(2):
        live = ((lane // 16) * 4 < place[4 + i]) & ((lane % 16) * 4 < place[6 + i])
        keys = block_pair(pairs[i * 64 : i * 64 + 64, :D].astype(jnp.float32)).astype(jnp.bfloat16)
        values.append(block_pair(pairs[i * 64 : i * 64 + 64, D:].astype(jnp.float32)).astype(jnp.bfloat16))
        here = mm_nt(query[i * 1024 : (i + 1) * 1024], keys)
        scores.append(jnp.where(live, here * SCORE_SCALE, NEG))
    scores = jnp.concatenate(scores, axis=0)
    weights = jnp.exp(scores - half_reduce(jnp.max, scores, -jnp.inf))
    probs = weights / half_reduce(jnp.sum, weights, 0.0)
    prob_out[...] = probs
    low = probs.astype(jnp.bfloat16)
    mixed = jnp.concatenate([mm(low[i * 1024 : (i + 1) * 1024], values[i]) for i in range(2)], axis=0)
    mixed = jnp.where(inside, mixed, 0.0).astype(jnp.bfloat16)
    att_out[...] = mixed
    mid_out[...] = picture + mm(mixed, wout[...])


def gelu_parts(x):
    density = jnp.exp(x * x * -0.5) * 0.3989422804014327
    phi = 0.5 + 0.5 * lax.erf(x * 0.7071067811865476)
    return x * phi, phi + x * density


def feed_kernel(
    place, mid, cot, cot1, cot2, cot3, gains, wfc1, taps, wfc2,
    bo0, bo1, bo2, bo3, mg_out, send_out, keep_out,
    cj, br, br_t, mask, even, odd, mix, pairs, pairs_t, cg, act, acc, back, stage, result, unit2, scale2,
):
    me = place[0]
    edge = jnp.zeros((64, 3 * D), jnp.bfloat16)
    for i in range(2):
        even[pl.ds(i * 576 + 512, 64), :] = edge
        odd[pl.ds(i * 576, 64), :] = edge
    col = lax.broadcasted_iota(jnp.int32, (2048, D), 0) % 64
    for k, chunk in enumerate((cot, cot1, cot2, cot3)):
        for i in range(2):
            raw = cot[2 * me + i] if k == 0 else chunk[i]
            for r in range(4):
                at = (r % 2) * 1024 + i * 512 + (me ^ k) * 128 + (r // 2) * 64
                cj[pl.ds(pl.multiple_of(at, 64), 64), :] = raw[r]
    inside = inside_mask(place, (2, 2, 8, 64, D), lambda at: at[1], lambda at: 2 * at[2] + at[0])
    mask[...] = jnp.where(inside, 1.0, 0.0)
    fc1_wide = wfc1[...].astype(jnp.float32)
    for k in range(4):
        for s in range(3):
            mix[k, pl.ds(s * D, D), :] = (fc1_wide * taps[pl.ds(3 * k + s, 1), :]).astype(jnp.bfloat16)
    for c in range(8):
        stage[pl.ds(c * (PACK1 // 8) + 2 * D, 16), :] = jnp.zeros((16, D), jnp.float32)
    branch = cj[...].astype(jnp.float32) * mask[...]
    br[...] = branch.astype(jnp.bfloat16)
    br_t[...] = branch.T.astype(jnp.bfloat16)

    def by_parity():
        return jnp.concatenate([mid[:, :, e].reshape(1024, D) for e in range(2)], axis=0)

    unit, scale = norm_parts(by_parity())
    unit2[...] = unit
    scale2[...] = jnp.broadcast_to(scale, (2048, D))
    normed = ((unit * gains[pl.ds(2, 1), :]).astype(jnp.bfloat16)).astype(jnp.float32) * mask[...]
    before = jnp.where(col == 0, 0.0, pltpu.roll(normed, 1, 0))
    after = jnp.where(col == 63, 0.0, pltpu.roll(normed, 2047, 0))
    for s, value in enumerate((before, normed, after)):
        value = value.astype(jnp.bfloat16)
        for e, side in enumerate((even, odd)):
            for i in range(2):
                at = e * 1024 + i * 512
                side[pl.ds(i * 576 + e * 64, 512), pl.ds(s * D, D)] = value[at : at + 512]
    for i in range(2):
        ev, ev_next = (even[pl.ds(i * 576 + h * 64, 512), :].astype(jnp.float32) for h in (0, 1))
        od_last, od = (odd[pl.ds(i * 576 + h * 64, 512), :].astype(jnp.float32) for h in (0, 1))
        for k, value in enumerate((od_last - od, ev + od, od - ev, ev - ev_next)):
            here = pl.ds(i * 512, 512)
            pairs[k, here, :] = value.astype(jnp.bfloat16)
            for s in range(3):
                pairs_t[k, pl.ds(s * D, D), here] = value[:, s * D : (s + 1) * D].T.astype(jnp.bfloat16)
    for f in range(FF // FC):
        chan = pl.ds(f * FC, FC)
        for b in range(1024 // TB):
            part = pl.ds(b * TB, TB)
            m0, m1, m2, m3 = (mm(pairs[k, part, :], mix[k, :, chan]) for k in range(4))
            grads = []
            for e, conv in enumerate((m0 + (m1 + m2), (m1 - m2) - m3)):
                here = pl.ds(e * 1024 + b * TB, TB)
                value, slope = gelu_parts(conv)
                low = value.astype(jnp.bfloat16)
                act[here, :] = low
                grads.append(mm_nt(br[here, :], wfc2[chan, :]) * slope)
                if f == 0:
                    acc[here, :] = mm(low, wfc2[chan, :])
                else:
                    acc[here, :] += mm(low, wfc2[chan, :])
            for k, value in enumerate((grads[0], grads[0] + grads[1], grads[0] - grads[1], grads[1])):
                cg[k, part, chan] = value.astype(jnp.bfloat16)
        fc2_grad = mm(br_t[...], act[...])
        fc2_grad = fc2_grad.T
        for j in range(FC // D):
            stage[pl.ds((f * (FC // D) + j) * (PACK1 // 8) + D, D), :] = fc2_grad[j * D : (j + 1) * D]
        fc1_grad = jnp.zeros((D, FC), jnp.float32)
        tap_grads = []
        for k in range(4):
            outer = mm(pairs_t[k], cg[k, :, chan])
            for s in range(3):
                here = outer[s * D : (s + 1) * D]
                if k == 3:
                    here = -here
                fc1_grad += here * taps[pl.ds(3 * k + s, 1), chan]
                tap_grads.append(jnp.sum(here * wfc1[:, chan].astype(jnp.float32), axis=0, keepdims=True))
        for s in range(3):
            half_sum = 0.5 * (tap_grads[3 + s] + tap_grads[6 + s])
            half_gap = 0.5 * (tap_grads[3 + s] - tap_grads[6 + s])
            for p, value in enumerate((tap_grads[s] + half_sum, half_gap, half_sum + tap_grads[9 + s])):
                for j in range(FC // D):
                    at = (f * (FC // D) + j) * (PACK1 // 8) + 2 * D + 3 * p + s
                    stage[pl.ds(at, 1), :] = value[:, j * D : (j + 1) * D]
        for j in range(FC // D):
            stage[pl.ds((f * (FC // D) + j) * (PACK1 // 8), D), :] = fc1_grad[:, j * D : (j + 1) * D]
    for i in range(2):
        back[0, pl.ds(i * 576 + 512, 64), :] = jnp.zeros((64, 3 * D), jnp.float32)
        back[3, pl.ds(i * 576, 64), :] = jnp.zeros((64, 3 * D), jnp.float32)
    for k in range(4):
        spread = mm_nt(cg[k], mix[k])
        for i in range(2):
            back[k, pl.ds(i * 576 + (64 if k == 3 else 0), 512), :] = spread[i * 512 : (i + 1) * 512]
    spread = []
    for e in range(2):
        for i in range(2):
            here, later = pl.ds(i * 576, 512), pl.ds(i * 576 + 64, 512)
            if e == 0:
                spread.append(back[1, here, :] - back[2, here, :] + (back[3, here, :] - back[3, later, :]))
            else:
                spread.append(back[1, here, :] + back[2, here, :] + (back[0, later, :] - back[0, here, :]))
    spread = jnp.concatenate(spread, axis=0)
    after = jnp.where(col == 63, 0.0, pltpu.roll(spread[:, :D], 2047, 0))
    before = jnp.where(col == 0, 0.0, pltpu.roll(spread[:, 2 * D :], 1, 0))
    normed_grad = (spread[:, D : 2 * D] + before + after) * mask[...]
    middle = by_parity()
    unit, scale = unit2[...], scale2[...]
    gain_grad = jnp.sum(normed_grad * unit, axis=0, keepdims=True)
    total = cj[...].astype(jnp.float32) + norm_back(normed_grad, gains[pl.ds(2, 1), :], unit, scale)
    final = (middle + acc[...] * mask[...]).astype(jnp.bfloat16)
    for e in range(2):
        mg_out[:, :, e] = total[e * 1024 : (e + 1) * 1024].reshape(2, 8, 64, D)
        result[:, :, e] = final[e * 1024 : (e + 1) * 1024].reshape(2, 8, 64, D)
    for k, bo in enumerate((bo0, bo1, bo2, bo3)):
        for i in range(2):
            bo[i] = result[i, pl.ds((me ^ k) * 2, 2)].reshape(4, 64, D)
    stage[pl.ds(2 * D + 9, 1), :] = gain_grad
    split_pack(place, stage, send_out, keep_out)


def split_pack(place, stage, send_out, keep_out):
    rows = stage.shape[0] // 8
    for k in range(4):
        at = pl.ds(k * rows, rows)
        for out, core, first in ((send_out, 1 - place[1], place[3]), (keep_out, place[1], place[2])):
            start = pl.multiple_of((core * 4 + (first ^ k)) * rows, 16)
            out[at, :] = stage[pl.ds(start, rows), :].astype(jnp.bfloat16)


def back_kernel(
    place, normed, query, prob, att, mgrad, pat, pooled, kv,
    gains, wq, wsr, wkv, wout,
    query_grad, pooled_out, send_out, keep_out,
    stage,
):
    inside = image_mask(place)
    low = mgrad[...].astype(jnp.bfloat16)
    out_grad = mm_tn(att[...], low)
    mixed = jnp.where(inside, mm_nt(low, wout[...]), 0.0).astype(jnp.bfloat16)
    keys, values = (
        [
            block_pair(kv[pl.ds(i * 64, 64), pl.ds(n * D, D)].astype(jnp.float32)).astype(jnp.bfloat16)
            for i in range(2)
        ]
        for n in range(2)
    )
    parts = [slice(i * 1024, (i + 1) * 1024) for i in range(2)]
    weights = prob[...]
    back = jnp.concatenate([mm_nt(mixed[parts[i]], values[i]) for i in range(2)], axis=0)
    back = weights * (back - half_reduce(jnp.sum, weights * back, 0.0)) * SCORE_SCALE
    back = back.astype(jnp.bfloat16)
    grads = jnp.concatenate([mm(back[parts[i]], keys[i]) for i in range(2)], axis=0).astype(jnp.bfloat16)
    query_grad[...] = grads
    weights = weights.astype(jnp.bfloat16)
    left = halves((64, D))
    key_rows = []
    for i in range(2):
        value_full = mm_tn(weights[parts[i]], mixed[parts[i]])
        key_full = mm_tn(back[parts[i]], query[pl.ds(i * 1024, 1024), :])
        key_rows.append(
            jnp.concatenate(
                [
                    jnp.where(left, key_full[:64], key_full[64:]),
                    jnp.where(left, value_full[:64], value_full[64:]),
                ],
                axis=1,
            )
        )
    pair = jnp.concatenate(key_rows, axis=0).astype(jnp.bfloat16)
    unit, scale = norm_parts(pooled[...])
    reduced = (unit * gains[pl.ds(1, 1), :]).astype(jnp.bfloat16)
    kv_grad = mm_tn(reduced, pair)
    reduced_grad = mm_nt(pair, wkv[...])
    srg_grad = jnp.sum(reduced_grad * unit, axis=0, keepdims=True)
    pooled_low = norm_back(reduced_grad, gains[pl.ds(1, 1), :], unit, scale).astype(jnp.bfloat16)
    pooled_out[...] = pooled_low
    sr_grad = mm_tn(pat[...], pooled_low)
    each = PACK2 // 8
    for c in range(8):
        stage[pl.ds(c * each, 256), :] = sr_grad[c * 256 : (c + 1) * 256]
    for c in range(8):
        side, row = c // 4, (c % 4) * 32
        stage[pl.ds(c * each + 256, 32), :] = kv_grad[row : row + 32, side * D : (side + 1) * D]
        stage[pl.ds(c * each + 304, 16), :] = out_grad[c * 16 : (c + 1) * 16]
        stage[pl.ds(c * each + 320, 16), :] = jnp.zeros((16, D), jnp.float32)
    q_grad = mm_tn(normed[...], grads)
    weighted = q_grad * wq[...].astype(jnp.float32)
    for c in range(16):
        at = slice(c * D, (c + 1) * D)
        weighted += sr_grad[at] * wsr[pl.ds(c * D, D), :].astype(jnp.float32)
    high = weighted.astype(jnp.bfloat16)
    low = (weighted - high.astype(jnp.float32)).astype(jnp.bfloat16)
    ones = jnp.ones((16, D), jnp.bfloat16)
    gain_grad = (mm_nt(ones, high) + mm_nt(ones, low))[0:1] / gains[pl.ds(0, 1), :]
    for c in range(8):
        stage[pl.ds(c * each + 288, 16), :] = q_grad[c * 16 : (c + 1) * 16]
    stage[pl.ds(320, 1), :] = gain_grad
    stage[pl.ds(321, 1), :] = srg_grad
    split_pack(place, stage, send_out, keep_out)


def input_kernel(
    place, x, query_grad, pooled_low, mgrad, gains, wq, wsr,
    ig0, ig1, ig2, ig3,
    unfold, result,
):
    me = place[0]
    patch_grad = mm_nt(pooled_low[...], wsr[...])
    for i in range(2):
        for a in range(4):
            for u in range(4):
                for t in range(4):
                    unfold[pl.ds(i * 1024 + (4 * a + u) * 64 + t, 16, stride=4), :] = patch_grad[
                        i * 64 + a * 16 : i * 64 + a * 16 + 16, (u * 4 + t) * D : (u * 4 + t + 1) * D
                    ]
    grad = mm_nt(query_grad[...], wq[...]) + jnp.where(image_mask(place), unfold[...], 0.0)
    unit, scale = norm_parts(x[...].astype(jnp.float32))
    total = mgrad[...] + norm_back(grad, gains[pl.ds(0, 1), :], unit, scale)
    result[...] = total.astype(jnp.bfloat16).reshape(2, 16, 64, D)
    for k, ig in enumerate((ig0, ig1, ig2, ig3)):
        for i in range(2):
            ig[i] = result[i, pl.ds((me ^ k) * 4, 4)]


def call(kernel, scalars, arrays, outs, scratch, flops=0, name=None, vmem=24):
    spec = pl.BlockSpec(memory_space=VMEM)
    return pl.pallas_call(
        kernel,
        out_shape=[jax.ShapeDtypeStruct(shape, kind) for shape, kind in outs],
        in_specs=[pl.BlockSpec(memory_space=pltpu.SMEM)] * len(scalars) + [spec] * len(arrays),
        out_specs=[spec] * len(outs),
        scratch_shapes=scratch,
        compiler_params=pltpu.CompilerParams(vmem_limit_bytes=vmem * 2**20),
        cost_estimate=pl.CostEstimate(flops=flops, bytes_accessed=4 * 2**20, transcendentals=0),
        name=name,
    )(*scalars, *arrays)


BF, F32 = jnp.bfloat16, jnp.float32
FLAT = (2048, D)
SPLIT = (2, 8, 2, 64, D)
CHUNK = (2, 4, 64, D)
PACK1, PACK2 = 2176, 2688
FC, TB = 512, 1024
SCORE_SCALE = HEAD_DIM ** (-0.5)


def attend(place, chunks, gains, wq, wsr, wkv, wout):
    return call(
        attend_kernel,
        (place,),
        (*chunks, gains, wq, wsr, wkv, wout),
        [
            (FLAT, BF), (FLAT, BF), (FLAT, BF), (FLAT, F32), (FLAT, BF), (FLAT, F32),
            ((128, 2048), BF), ((128, D), F32), ((128, 2 * D), BF),
        ],
        [VMEM((2048, D), F32)],
        flops=10**9, name="attend",
    )


def feed(place, middle, chunks, gains, wfc1, taps, wfc2):
    return call(
        feed_kernel,
        (place,),
        (middle, *chunks, gains, wfc1, taps, wfc2),
        [(CHUNK, BF)] * 4 + [(SPLIT, F32), ((PACK1 // 2, D), BF), ((PACK1 // 2, D), BF)],
        [
            VMEM((2048, D), BF), VMEM((2048, D), BF), VMEM((D, 2048), BF), VMEM((2048, D), F32),
            VMEM((1152, 3 * D), BF), VMEM((1152, 3 * D), BF), VMEM((4, 3 * D, FF), BF),
            VMEM((4, 1024, 3 * D), BF), VMEM((4, 3 * D, 1024), BF), VMEM((4, 1024, FF), BF), VMEM((2048, FC), BF),
            VMEM((2048, D), F32), VMEM((4, 1152, 3 * D), F32), VMEM((PACK1, D), F32), VMEM(SPLIT, BF), VMEM(FLAT, F32), VMEM(FLAT, F32),
        ],
        flops=16 * 10**9, name="feed", vmem=44,
    )


def back(place, kept, mgrad, gains, wq, wsr, wkv, wout):
    _, normed, query, prob, att, _, pat, pooled, kv = kept
    return call(
        back_kernel,
        (place,),
        (normed, query, prob, att, mgrad, pat, pooled, kv, gains, wq, wsr, wkv, wout),
        [(FLAT, BF), ((128, D), BF), ((PACK2 // 2, D), BF), ((PACK2 // 2, D), BF)],
        [VMEM((PACK2, D), F32)],
        flops=2 * 10**9, name="back",
    )


def input_gradient(place, x, query_grad, pooled_low, mgrad, gains, wq, wsr):
    return call(
        input_kernel,
        (place,),
        (x, query_grad, pooled_low, mgrad, gains, wq, wsr),
        [(CHUNK, BF)] * 4,
        [VMEM((2048, D), F32), VMEM((2, 16, 64, D), BF)],
        flops=10**9, name="input_gradient",
    )


def over_rows(value, k):
    return lax.ppermute(value, "rows", [(i, i ^ k) for i in range(4)])


def over_four(value, k, phase):
    plane, line = (k >> 1) * 16 + (k & 1), 2 * k
    pairs = [(i, i ^ (plane if (i >> 3) & 1 == phase else line)) for i in range(32)]
    return lax.ppermute(value, ("rows", "batch"), pairs)


def plus(*values):
    return sum(v.astype(F32) for v in values).astype(BF)


def plane_parts(packs):
    halves_in = [plus(keep, over_rows(send, 1)) for send, keep in packs]
    return [
        jnp.concatenate([h[k * (h.shape[0] // 4) : (k + 1) * (h.shape[0] // 4)] for h in halves_in])
        for k in range(4)
    ]


def to_four(values, phase):
    return [over_four(values[k], k, phase) for k in (1, 2, 3)]


def finish_kernel(half, place, *refs):
    pieces, refs = refs[: 4 * (half + 1)], refs[4 * (half + 1) :]
    if half:
        refs = refs[6:]
    else:
        grads, refs = refs[:4], refs[4:]
    (q, sr, kv, out, fc1, fc2), refs = refs[:6], refs[6:]
    stage, small_dw, small_ln1, small_ln2, small_srg, sems = refs[-6:]
    copies = []

    def move(source, target):
        copies.append(pltpu.make_async_copy(source, target, sems.at[len(copies)]))
        copies[-1].start()

    def chunk_of(j):
        core, first = (place[1], place[2]) if j < 4 else (1 - place[1], place[3])
        return core * 4 + (first ^ (j % 4))

    if not half:
        for k in range(4):
            move(grads[k], refs[0].at[pl.ds(2 * (place[0] ^ k), 2)])
    for k in range(4):
        c = chunk_of(4 * half + k)
        stage[k] = pieces[4 * half + k][...].astype(F32)
        chan = pl.ds(pl.multiple_of(c * D, D), D)
        move(stage.at[k, pl.ds(0, D)], fc1.at[:, chan])
        move(stage.at[k, pl.ds(D, D)], fc2.at[chan])
        move(stage.at[k, pl.ds(272, 256)], sr.at[pl.ds(pl.multiple_of(c * 256, 256), 256)])
        row = pl.ds(pl.multiple_of((c % 4) * 32, 32), 32)
        move(stage.at[k, pl.ds(528, 32)], kv.at[row, pl.ds(pl.multiple_of((c // 4) * D, D), D)])
        row = pl.ds(pl.multiple_of(c * 16, 16), 16)
        move(stage.at[k, pl.ds(560, 16)], q.at[row])
        move(stage.at[k, pl.ds(576, 16)], out.at[row])
    if half:
        sums = [jnp.zeros((1, D), F32)] * 3
        for j, piece in enumerate(pieces):
            chan = pl.ds(pl.multiple_of(chunk_of(j) * D, D), D)
            small = piece[pl.ds(256, 16), :].astype(F32)
            for tap in range(9):
                small_dw[tap // 3, pl.ds(tap % 3, 1), chan] = small[tap : tap + 1]
            last = piece[pl.ds(592, 16), :].astype(F32)
            rows = (last[0:1], small[9:10], last[1:2])
            sums = [total + row for total, row in zip(sums, rows)]
        move(small_dw, refs[0])
        for ref, small, total in zip(refs[1:4], (small_ln1, small_ln2, small_srg), sums):
            small[...] = total.reshape(D)
            move(small, ref)
    for copy in copies:
        copy.wait()


def finish(place, pieces, earlier=(), grads=(), shape=None):
    far, near = pl.BlockSpec(memory_space=pl.ANY), pl.BlockSpec(memory_space=VMEM)
    half = 1 if earlier else 0
    shapes = [((D, D), F32), ((2048, D), F32), ((D, 2 * D), F32), ((D, D), F32), ((D, FF), F32), ((FF, D), F32)]
    specs, n = [far] * 6, len(shapes)
    if half:
        shapes += [((3, 3, FF), F32), ((D,), F32), ((D,), F32), ((D,), F32)]
        specs += [far] * 4
    else:
        shapes += [(shape, BF)]
        specs += [far]
    before = 1 + len(pieces) + len(grads)
    return pl.pallas_call(
        functools.partial(finish_kernel, half),
        out_shape=[jax.ShapeDtypeStruct(*each) for each in shapes],
        in_specs=[pl.BlockSpec(memory_space=pltpu.SMEM)] + [near] * (before - 1) + [far] * len(earlier),
        out_specs=specs,
        scratch_shapes=[
            VMEM((4, 608, D), F32), VMEM((3, 3, FF), F32), VMEM((D,), F32), VMEM((D,), F32), VMEM((D,), F32),
            pltpu.SemaphoreType.DMA((28,)),
        ],
        input_output_aliases={before + i: i for i in range(n)} if half else {},
        compiler_params=pltpu.CompilerParams(vmem_limit_bytes=8 * 2**20),
        cost_estimate=pl.CostEstimate(flops=0, bytes_accessed=4 * 2**20, transcendentals=0),
        name="finish",
    )(place, *pieces, *grads, *earlier)


def gather_kernel(place, part0, part1, part2, part3, out, sems):
    copies = [
        pltpu.make_async_copy(part, out.at[pl.ds(2 * (place[0] ^ k), 2)], sems.at[k])
        for k, part in enumerate((part0, part1, part2, part3))
    ]
    for copy in copies:
        copy.start()
    for copy in copies:
        copy.wait()


def gather_rows(place, parts, shape):
    far = pl.BlockSpec(memory_space=pl.ANY)
    return pl.pallas_call(
        gather_kernel,
        out_shape=jax.ShapeDtypeStruct(shape, BF),
        in_specs=[pl.BlockSpec(memory_space=pltpu.SMEM)] + [pl.BlockSpec(memory_space=VMEM)] * 4,
        out_specs=far,
        scratch_shapes=[pltpu.SemaphoreType.DMA((4,))],
        compiler_params=pltpu.CompilerParams(vmem_limit_bytes=4 * 2**20),
        name="gather_rows",
    )(place, *parts)


def image_shards(
    tokens, valid_rows, valid_cols, ln1_gain, q_weight, sr_weight, sr_gain, kv_weight, out_weight,
    ln2_gain, fc1_weight, dw_weight, fc2_weight, cotangent,
):
    me, lane = lax.axis_index("rows"), lax.axis_index("batch")
    core = me & 1
    plane, line = (me >> 1) * 2 + (lane & 1), lane >> 1
    first, second = jnp.where(core == 0, plane, line), jnp.where(core == 0, line, plane)
    sizes = [lax.dynamic_slice_in_dim(v, 2 * me, 2) for v in (valid_rows, valid_cols)]
    place = jnp.concatenate([jnp.stack([me, core, first, second]), *sizes]).astype(jnp.int32)

    def spread(source):
        near = {
            k: over_rows(lax.dynamic_slice_in_dim(source, 2 * (me ^ k), 2, 0), k) for k in (3, 2, 1)
        }
        return source, near[1], near[2], near[3]

    def returned(parts):
        near = {k: over_rows(parts[k], k) for k in (3, 2, 1)}
        return [parts[0], near[1], near[2], near[3]]

    gains = jnp.stack([ln1_gain, sr_gain, ln2_gain])
    row0, row1, row2 = dw_weight.astype(F32)
    taps = jnp.concatenate(
        [row0, 0.5 * (row0 + row1 + row2), 0.5 * (row0 - row1 + row2), row2, jnp.zeros((4, FF), F32)]
    )
    token_parts = spread(tokens)
    cotangent, _ = lax.optimization_barrier((cotangent, token_parts[1]))
    kept = attend(
        place, token_parts, gains, q_weight, sr_weight, kv_weight, out_weight
    )
    *block_parts, mgrad, send1, keep1 = feed(
        place, kept[5].reshape(SPLIT), spread(cotangent), gains, fc1_weight, taps, fc2_weight
    )
    mgrad = mgrad.reshape(FLAT)
    query_grad, pooled_low, send2, keep2 = back(
        place, kept, mgrad, gains, q_weight, sr_weight, kv_weight, out_weight
    )
    parts = plane_parts([(send1, keep1), (send2, keep2)])
    block = returned(block_parts)
    inputs = input_gradient(place, kept[0], query_grad, pooled_low, mgrad, gains, q_weight, sr_weight)
    mine, inputs = lax.optimization_barrier((plus(parts[0], *to_four(parts, 0)), list(inputs)))
    inputs = returned(inputs)
    mine, block[2] = lax.optimization_barrier((mine, block[2]))
    got = [g.astype(F32) for g in to_four([mine] * 4, 1)]
    got, block_out = lax.optimization_barrier((got, gather_rows(place, block, tokens.shape)))
    got, inputs[1], inputs[2] = lax.optimization_barrier((got, inputs[1], inputs[2]))
    total = ((mine.astype(F32) + got[0]) + (got[1] + got[2])).astype(BF)
    got = to_four([total] * 4, 0)
    got, inputs[3] = lax.optimization_barrier((got, inputs[3]))
    pieces = (total, *got)
    others = tuple(over_rows(piece, 1) for piece in pieces)
    *half, input_grad = finish(place, pieces, (), inputs, tokens.shape)
    q, sr, kv, out, fc1, fc2, dw, ln1_sum, ln2_sum, srg_sum = finish(place, pieces + others, half)
    return block_out, input_grad, ln1_sum, q, sr, srg_sum, kv, out, ln2_sum, fc1, dw, fc2


def shards(*arrays):
    tokens = arrays[0]
    fits = (
        lax.axis_size("rows") == 4
        and lax.axis_size("batch") == 8
        and tokens.shape == (8, 4, 64, D)
    )
    return image_shards(*arrays) if fits else row_shards(*arrays)


def solution(mesh):
    placed = (
        P("batch", "rows", None, None),
        P("batch"),
        P("batch"),
        P(),
        P(),
        P(),
        P(),
        P(),
        P(),
        P(),
        P(),
        P(),
        P(),
        P("batch", "rows", None, None),
    )
    return jax.shard_map(
        shards,
        mesh=mesh,
        in_specs=placed,
        out_specs=(
            P("batch", "rows", None, None),
            P("batch", "rows", None, None),
            P(),
            P(),
            P(),
            P(),
            P(),
            P(),
            P(),
            P(),
            P(),
            P(),
        ),
        check_vma=False,
    )
```

```python
import functools

import jax
import jax.numpy as jnp
from jax import lax
from jax.experimental import pallas as pl
from jax.experimental.pallas import tpu as pltpu
from jax.sharding import PartitionSpec as P

D = 128
FF = 1024
HEADS = 2
POOL = 4
HEAD_DIM = 64


EPS = 1e-06
NEG = -1e30


def padded_2(value, sides, width):
    for axis, dim in sides:
        size, length = (lax.axis_size(axis), value.shape[dim])
        up = [(i, (i + 1) % size) for i in range(size - 1)]
        down = [(j, i) for i, j in up]
        last = lax.slice_in_dim(value, length - width, length, axis=dim)
        first = lax.slice_in_dim(value, 0, width, axis=dim)
        before = lax.ppermute(last, axis, up)
        after = lax.ppermute(first, axis, down)
        value = jnp.concatenate([before, value, after], axis=dim)
    return value


def layer_norm(source, gain):
    centered = source - jnp.mean(source, axis=-1, keepdims=True)
    spread = jnp.mean(centered * centered, axis=-1, keepdims=True)
    return centered * lax.rsqrt(spread + EPS) * gain


def activate(source):
    return jax.nn.gelu(source, approximate=False)


def outer_product(left, right):
    return lax.dot_general(
        left.reshape(-1, left.shape[-1]),
        right.reshape(-1, right.shape[-1]),
        (((0,), (0,)), ((), ())),
        preferred_element_type=jnp.float32,
    )


def back_product(grad, weight):
    return lax.dot_general(
        grad, weight, (((grad.ndim - 1,), (1,)), ((), ())), preferred_element_type=jnp.float32
    )


def pad_columns(source):
    return jnp.pad(source, ((0, 0), (0, 0), (1, 1), (0, 0)))


def depth_conv(padded, kernel, count, columns):
    summed = jnp.zeros((padded.shape[0], count, columns, padded.shape[3]), jnp.float32)
    for offset_row in range(3):
        for offset_col in range(3):
            summed = (
                summed
                + padded[:, offset_row : offset_row + count, offset_col : offset_col + columns]
                * kernel[offset_row, offset_col]
            )
    return summed


def row_shards(
    tokens,
    valid_rows,
    valid_cols,
    ln1_gain,
    q_weight,
    sr_weight,
    sr_gain,
    kv_weight,
    out_weight,
    ln2_gain,
    fc1_weight,
    dw_weight,
    fc2_weight,
    cotangent,
):
    images = tokens.shape[0]
    columns = tokens.shape[2]
    groups = lax.axis_size("rows")
    score_scale = HEAD_DIM ** (-0.5)
    first_row = lax.axis_index("rows") * POOL
    ids = first_row + jnp.arange(POOL, dtype=jnp.int32)
    inside = (
        (ids[None, :, None] >= 0)
        & (ids[None, :, None] < valid_rows[:, None, None])
        & (jnp.arange(columns)[None, None, :] < valid_cols[:, None, None])
    )
    inside_float = inside.astype(jnp.float32)[..., None]
    key_live = (
        (jnp.arange(groups)[None, :, None] * POOL < valid_rows[:, None, None])
        & (jnp.arange(columns // POOL)[None, None, :] * POOL < valid_cols[:, None, None])
    ).reshape(images, -1)
    picture = tokens.astype(jnp.float32)
    normed, ln1_back = jax.vjp(layer_norm, picture, ln1_gain)
    normed_low = normed.astype(jnp.bfloat16)
    queries = jnp.dot(normed_low, q_weight, preferred_element_type=jnp.float32).astype(jnp.bfloat16)
    masked = jnp.where(inside[..., None], normed_low, 0)
    patches = (
        masked.reshape(images, POOL, columns // POOL, POOL, D)
        .transpose(0, 2, 1, 3, 4)
        .reshape(images, columns // POOL, POOL * POOL * D)
    )
    pooled = jnp.dot(patches, sr_weight, preferred_element_type=jnp.float32)
    reduced, sr_back = jax.vjp(layer_norm, pooled, sr_gain)
    reduced_low = reduced.astype(jnp.bfloat16)
    key_value = jnp.dot(reduced_low, kv_weight, preferred_element_type=jnp.float32).astype(
        jnp.bfloat16
    )
    gathered = lax.all_gather(key_value[:, None], "rows", axis=1, tiled=True).reshape(
        images, -1, 2 * D
    )
    key_part = gathered[..., :D].reshape(images, -1, HEADS, HEAD_DIM)
    value_part = gathered[..., D:].reshape(images, -1, HEADS, HEAD_DIM)
    head_queries = queries.reshape(images, -1, HEADS, HEAD_DIM)
    scores = (
        jnp.einsum("inhe,iphe->ihnp", head_queries, key_part, preferred_element_type=jnp.float32)
        * score_scale
    )
    scores = jnp.where(key_live[:, None, None, :], scores, NEG)
    probabilities = jax.nn.softmax(scores, axis=-1)
    probs_low = probabilities.astype(jnp.bfloat16)
    attended = jnp.einsum(
        "ihnp,iphe->inhe", probs_low, value_part, preferred_element_type=jnp.float32
    ).reshape(images, POOL, columns, D)
    attended_low = (attended * inside_float).astype(jnp.bfloat16)
    middle = picture + jnp.dot(attended_low, out_weight, preferred_element_type=jnp.float32)
    normed2, ln2_back = jax.vjp(layer_norm, middle, ln2_gain)
    normed2_low = normed2.astype(jnp.bfloat16)
    kernel = dw_weight.astype(jnp.float32)
    hidden_shape = (images, POOL, columns, FF)
    hidden = jnp.where(
        inside[..., None],
        jnp.dot(normed2_low, fc1_weight, preferred_element_type=jnp.float32).astype(jnp.bfloat16),
        0,
    )
    padded = pad_columns(padded_2(hidden, (("rows", 1),), 1))
    convolved = depth_conv(padded, kernel, POOL, columns)
    active, gelu_back = jax.vjp(activate, convolved)
    active_low = active.astype(jnp.bfloat16)
    block_out = (
        middle + jnp.dot(active_low, fc2_weight, preferred_element_type=jnp.float32) * inside_float
    ).astype(jnp.bfloat16)
    branch_grad = jnp.where(inside[..., None], cotangent, 0)
    fc2_grad = outer_product(active_low, branch_grad)
    active_grad = back_product(branch_grad, fc2_weight)
    (conv_grad,) = gelu_back(active_grad)
    conv_low = conv_grad.astype(jnp.bfloat16)
    grad_padded = pad_columns(padded_2(conv_low, (("rows", 1),), 1))
    hidden_grad = jnp.zeros(hidden_shape, jnp.float32)
    for offset_row in range(3):
        for offset_col in range(3):
            hidden_grad = (
                hidden_grad
                + grad_padded[
                    :,
                    2 - offset_row : 2 - offset_row + POOL,
                    2 - offset_col : 2 - offset_col + columns,
                ]
                * kernel[offset_row, offset_col]
            )
    dw_grad = jnp.stack(
        [
            jnp.stack(
                [
                    jnp.sum(
                        padded[:, offset_row : offset_row + POOL, offset_col : offset_col + columns]
                        * conv_low.astype(jnp.float32),
                        axis=(0, 1, 2),
                    )
                    for offset_col in range(3)
                ]
            )
            for offset_row in range(3)
        ]
    )
    hidden_low_grad = jnp.where(inside[..., None], hidden_grad, 0.0).astype(jnp.bfloat16)
    fc1_grad = outer_product(normed2_low, hidden_low_grad)
    normed2_grad = back_product(hidden_low_grad, fc1_weight)
    middle_back, ln2_gain_grad = ln2_back(normed2_grad)
    middle_grad = cotangent.astype(jnp.float32) + middle_back
    branch_low = middle_grad.astype(jnp.bfloat16)
    out_grad = outer_product(attended_low, branch_low)
    attended_grad = (
        jnp.where(inside[..., None], back_product(branch_low, out_weight), 0.0)
        .astype(jnp.bfloat16)
        .reshape(images, -1, HEADS, HEAD_DIM)
    )
    value_grad = jnp.einsum(
        "ihnp,inhe->iphe", probs_low, attended_grad, preferred_element_type=jnp.float32
    )
    prob_grad = jnp.einsum(
        "inhe,iphe->ihnp", attended_grad, value_part, preferred_element_type=jnp.float32
    )
    score_grad = (
        probabilities
        * (prob_grad - jnp.sum(probabilities * prob_grad, axis=-1, keepdims=True))
        * score_scale
    ).astype(jnp.bfloat16)
    query_grad = (
        jnp.einsum("ihnp,iphe->inhe", score_grad, key_part, preferred_element_type=jnp.float32)
        .astype(jnp.bfloat16)
        .reshape(images, POOL, columns, D)
    )
    key_grad = jnp.einsum(
        "ihnp,inhe->iphe", score_grad, head_queries, preferred_element_type=jnp.float32
    )
    pair_partial = jnp.concatenate(
        [key_grad.reshape(images, -1, D), value_grad.reshape(images, -1, D)], axis=-1
    ).reshape(images, groups, columns // POOL, 2 * D)
    pair_owned = lax.psum_scatter(pair_partial, "rows", scatter_dimension=1, tiled=True)
    pair_low = pair_owned[:, 0].astype(jnp.bfloat16)
    pair_weight_grad = outer_product(reduced_low, pair_low)
    reduced_grad = back_product(pair_low, kv_weight)
    pooled_grad, sr_gain_grad = sr_back(reduced_grad)
    pooled_low = pooled_grad.astype(jnp.bfloat16)
    sr_grad = outer_product(patches, pooled_low)
    patch_grad = (
        back_product(pooled_low, sr_weight)
        .reshape(images, columns // POOL, POOL, POOL, D)
        .transpose(0, 2, 1, 3, 4)
        .reshape(images, POOL, columns, D)
    )
    normed_grad = back_product(query_grad, q_weight) + jnp.where(inside[..., None], patch_grad, 0.0)
    q_grad = outer_product(normed_low, query_grad)
    picture_back, ln1_gain_grad = ln1_back(normed_grad)
    input_grad = (middle_grad + picture_back).astype(jnp.bfloat16)
    ln1_sum, q_sum, sr_sum, srg_sum, pair_sum, out_sum, ln2_sum, fc1_sum, dw_sum, fc2_sum = (
        lax.psum(
            (
                ln1_gain_grad,
                q_grad,
                sr_grad,
                sr_gain_grad,
                pair_weight_grad,
                out_grad,
                ln2_gain_grad,
                fc1_grad,
                dw_grad,
                fc2_grad,
            ),
            ("rows", "batch"),
        )
    )
    return (
        block_out,
        input_grad,
        ln1_sum,
        q_sum,
        sr_sum,
        srg_sum,
        pair_sum,
        out_sum,
        ln2_sum,
        fc1_sum,
        dw_sum,
        fc2_sum,
    )


VMEM = pltpu.VMEM
NT = (((1,), (1,)), ((), ()))
TN = (((0,), (0,)), ((), ()))


def mm(left, right):
    return jnp.dot(left, right, preferred_element_type=jnp.float32)


def mm_nt(left, right):
    return lax.dot_general(left, right, NT, preferred_element_type=jnp.float32)


def mm_tn(left, right):
    return lax.dot_general(left, right, TN, preferred_element_type=jnp.float32)


def norm_parts(source):
    centered = source - jnp.mean(source, axis=-1, keepdims=True)
    scale = lax.rsqrt(jnp.mean(centered * centered, axis=-1, keepdims=True) + EPS)
    return centered * scale, scale


def norm_back(grad, gain, unit, scale):
    scaled = grad * gain
    inner = jnp.mean(scaled * unit, axis=-1, keepdims=True)
    return scale * (scaled - jnp.mean(scaled, axis=-1, keepdims=True) - unit * inner)


def inside_mask(place, shape, image, row):
    at = [lax.broadcasted_iota(jnp.int32, shape, d) for d in range(len(shape) - 1)]
    first = image(at) == 0
    rows, cols = (jnp.where(first, place[n], place[n + 1]) for n in (4, 6))
    return ((row(at) < rows) & (at[-1] < cols)).reshape(-1, D)


def image_mask(place):
    return inside_mask(place, (2, 16, 64, D), lambda at: at[0], lambda at: at[1])


def halves(shape):
    return lax.broadcasted_iota(jnp.int32, shape, len(shape) - 1) < HEAD_DIM


def block_pair(source):
    left = halves(source.shape)
    zero = jnp.zeros_like(source)
    return jnp.concatenate([jnp.where(left, source, zero), jnp.where(left, zero, source)], axis=0)


def half_reduce(reducer, value, empty):
    left = halves(value.shape)
    first = reducer(jnp.where(left, value, empty), axis=-1, keepdims=True)
    second = reducer(jnp.where(left, empty, value), axis=-1, keepdims=True)
    return jnp.where(left, first, second)


def attend_kernel(
    place, own, near1, near2, near3, gains, wq, wsr, wkv, wout,
    x_out, normed_out, q_out, prob_out, att_out, mid_out, pat_out, pooled_out, kv_out, masked,
):
    me = place[0]
    for k, chunk in enumerate((own, near1, near2, near3)):
        for i in range(2):
            raw = own[2 * me + i] if k == 0 else chunk[i]
            x_out[pl.ds(pl.multiple_of(i * 1024 + (me ^ k) * 256, 256), 256), :] = raw.reshape(256, D)
    picture = x_out[...].astype(jnp.float32)
    unit, _ = norm_parts(picture)
    normed = (unit * gains[pl.ds(0, 1), :]).astype(jnp.bfloat16)
    normed_out[...] = normed
    inside = image_mask(place)
    masked[...] = jnp.where(inside, normed.astype(jnp.float32), 0.0)
    query = mm(normed, wq[...]).astype(jnp.bfloat16)
    q_out[...] = query
    for i in range(2):
        for a in range(4):
            for u in range(4):
                for t in range(4):
                    piece = masked[pl.ds(i * 1024 + (4 * a + u) * 64 + t, 16, stride=4), :]
                    pat_out[pl.ds(i * 64 + a * 16, 16), pl.ds((u * 4 + t) * D, D)] = piece.astype(
                        jnp.bfloat16
                    )
    pooled = mm(pat_out[...], wsr[...])
    pooled_out[...] = pooled
    unit, _ = norm_parts(pooled)
    pairs = mm((unit * gains[pl.ds(1, 1), :]).astype(jnp.bfloat16), wkv[...]).astype(jnp.bfloat16)
    kv_out[...] = pairs
    lane = lax.broadcasted_iota(jnp.int32, (1024, D), 1) % 64
    scores, values = [], []
    for i in range(2):
        live = ((lane // 16) * 4 < place[4 + i]) & ((lane % 16) * 4 < place[6 + i])
        keys = block_pair(pairs[i * 64 : i * 64 + 64, :D].astype(jnp.float32)).astype(jnp.bfloat16)
        values.append(block_pair(pairs[i * 64 : i * 64 + 64, D:].astype(jnp.float32)).astype(jnp.bfloat16))
        here = mm_nt(query[i * 1024 : (i + 1) * 1024], keys)
        scores.append(jnp.where(live, here * SCORE_SCALE, NEG))
    scores = jnp.concatenate(scores, axis=0)
    weights = jnp.exp(scores - half_reduce(jnp.max, scores, -jnp.inf))
    probs = weights / half_reduce(jnp.sum, weights, 0.0)
    prob_out[...] = probs
    low = probs.astype(jnp.bfloat16)
    mixed = jnp.concatenate([mm(low[i * 1024 : (i + 1) * 1024], values[i]) for i in range(2)], axis=0)
    mixed = jnp.where(inside, mixed, 0.0).astype(jnp.bfloat16)
    att_out[...] = mixed
    mid_out[...] = picture + mm(mixed, wout[...])


def gelu_parts(x):
    density = jnp.exp(x * x * -0.5) * 0.3989422804014327
    phi = 0.5 + 0.5 * lax.erf(x * 0.7071067811865476)
    return x * phi, phi + x * density


def feed_kernel(
    place, mid, cot, cot1, cot2, cot3, gains, wfc1, taps, wfc2,
    bo0, bo1, bo2, bo3, mg_out, send_out, keep_out,
    cj, br, br_t, mask, even, odd, mix, pairs, pairs_t, cg, act, acc, back, stage, result, unit2, scale2,
):
    me = place[0]
    edge = jnp.zeros((64, 3 * D), jnp.bfloat16)
    for i in range(2):
        even[pl.ds(i * 576 + 512, 64), :] = edge
        odd[pl.ds(i * 576, 64), :] = edge
    col = lax.broadcasted_iota(jnp.int32, (2048, D), 0) % 64
    for k, chunk in enumerate((cot, cot1, cot2, cot3)):
        for i in range(2):
            raw = cot[2 * me + i] if k == 0 else chunk[i]
            for r in range(4):
                at = (r % 2) * 1024 + i * 512 + (me ^ k) * 128 + (r // 2) * 64
                cj[pl.ds(pl.multiple_of(at, 64), 64), :] = raw[r]
    inside = inside_mask(place, (2, 2, 8, 64, D), lambda at: at[1], lambda at: 2 * at[2] + at[0])
    mask[...] = jnp.where(inside, 1.0, 0.0)
    fc1_wide = wfc1[...].astype(jnp.float32)
    for k in range(4):
        for s in range(3):
            mix[k, pl.ds(s * D, D), :] = (fc1_wide * taps[pl.ds(3 * k + s, 1), :]).astype(jnp.bfloat16)
    for c in range(8):
        stage[pl.ds(c * (PACK1 // 8) + 2 * D, 16), :] = jnp.zeros((16, D), jnp.float32)
    branch = cj[...].astype(jnp.float32) * mask[...]
    br[...] = branch.astype(jnp.bfloat16)
    br_t[...] = branch.T.astype(jnp.bfloat16)

    def by_parity():
        return jnp.concatenate([mid[:, :, e].reshape(1024, D) for e in range(2)], axis=0)

    unit, scale = norm_parts(by_parity())
    unit2[...] = unit
    scale2[...] = jnp.broadcast_to(scale, (2048, D))
    normed = ((unit * gains[pl.ds(2, 1), :]).astype(jnp.bfloat16)).astype(jnp.float32) * mask[...]
    before = jnp.where(col == 0, 0.0, pltpu.roll(normed, 1, 0))
    after = jnp.where(col == 63, 0.0, pltpu.roll(normed, 2047, 0))
    for s, value in enumerate((before, normed, after)):
        value = value.astype(jnp.bfloat16)
        for e, side in enumerate((even, odd)):
            for i in range(2):
                at = e * 1024 + i * 512
                side[pl.ds(i * 576 + e * 64, 512), pl.ds(s * D, D)] = value[at : at + 512]
    for i in range(2):
        ev, ev_next = (even[pl.ds(i * 576 + h * 64, 512), :].astype(jnp.float32) for h in (0, 1))
        od_last, od = (odd[pl.ds(i * 576 + h * 64, 512), :].astype(jnp.float32) for h in (0, 1))
        for k, value in enumerate((od_last - od, ev + od, od - ev, ev - ev_next)):
            here = pl.ds(i * 512, 512)
            pairs[k, here, :] = value.astype(jnp.bfloat16)
            for s in range(3):
                pairs_t[k, pl.ds(s * D, D), here] = value[:, s * D : (s + 1) * D].T.astype(jnp.bfloat16)
    for f in range(FF // FC):
        chan = pl.ds(f * FC, FC)
        for b in range(1024 // TB):
            part = pl.ds(b * TB, TB)
            m0, m1, m2, m3 = (mm(pairs[k, part, :], mix[k, :, chan]) for k in range(4))
            grads = []
            for e, conv in enumerate((m0 + (m1 + m2), (m1 - m2) - m3)):
                here = pl.ds(e * 1024 + b * TB, TB)
                value, slope = gelu_parts(conv)
                low = value.astype(jnp.bfloat16)
                act[here, :] = low
                grads.append(mm_nt(br[here, :], wfc2[chan, :]) * slope)
                if f == 0:
                    acc[here, :] = mm(low, wfc2[chan, :])
                else:
                    acc[here, :] += mm(low, wfc2[chan, :])
            for k, value in enumerate((grads[0], grads[0] + grads[1], grads[0] - grads[1], grads[1])):
                cg[k, part, chan] = value.astype(jnp.bfloat16)
        fc2_grad = mm(br_t[...], act[...])
        fc2_grad = fc2_grad.T
        for j in range(FC // D):
            stage[pl.ds((f * (FC // D) + j) * (PACK1 // 8) + D, D), :] = fc2_grad[j * D : (j + 1) * D]
        fc1_grad = jnp.zeros((D, FC), jnp.float32)
        tap_grads = []
        for k in range(4):
            outer = mm(pairs_t[k], cg[k, :, chan])
            for s in range(3):
                here = outer[s * D : (s + 1) * D]
                if k == 3:
                    here = -here
                fc1_grad += here * taps[pl.ds(3 * k + s, 1), chan]
                tap_grads.append(jnp.sum(here * wfc1[:, chan].astype(jnp.float32), axis=0, keepdims=True))
        for s in range(3):
            half_sum = 0.5 * (tap_grads[3 + s] + tap_grads[6 + s])
            half_gap = 0.5 * (tap_grads[3 + s] - tap_grads[6 + s])
            for p, value in enumerate((tap_grads[s] + half_sum, half_gap, half_sum + tap_grads[9 + s])):
                for j in range(FC // D):
                    at = (f * (FC // D) + j) * (PACK1 // 8) + 2 * D + 3 * p + s
                    stage[pl.ds(at, 1), :] = value[:, j * D : (j + 1) * D]
        for j in range(FC // D):
            stage[pl.ds((f * (FC // D) + j) * (PACK1 // 8), D), :] = fc1_grad[:, j * D : (j + 1) * D]
    for i in range(2):
        back[0, pl.ds(i * 576 + 512, 64), :] = jnp.zeros((64, 3 * D), jnp.float32)
        back[3, pl.ds(i * 576, 64), :] = jnp.zeros((64, 3 * D), jnp.float32)
    for k in range(4):
        spread = mm_nt(cg[k], mix[k])
        for i in range(2):
            back[k, pl.ds(i * 576 + (64 if k == 3 else 0), 512), :] = spread[i * 512 : (i + 1) * 512]
    spread = []
    for e in range(2):
        for i in range(2):
            here, later = pl.ds(i * 576, 512), pl.ds(i * 576 + 64, 512)
            if e == 0:
                spread.append(back[1, here, :] - back[2, here, :] + (back[3, here, :] - back[3, later, :]))
            else:
                spread.append(back[1, here, :] + back[2, here, :] + (back[0, later, :] - back[0, here, :]))
    spread = jnp.concatenate(spread, axis=0)
    after = jnp.where(col == 63, 0.0, pltpu.roll(spread[:, :D], 2047, 0))
    before = jnp.where(col == 0, 0.0, pltpu.roll(spread[:, 2 * D :], 1, 0))
    normed_grad = (spread[:, D : 2 * D] + before + after) * mask[...]
    middle = by_parity()
    unit, scale = unit2[...], scale2[...]
    gain_grad = jnp.sum(normed_grad * unit, axis=0, keepdims=True)
    total = cj[...].astype(jnp.float32) + norm_back(normed_grad, gains[pl.ds(2, 1), :], unit, scale)
    final = (middle + acc[...] * mask[...]).astype(jnp.bfloat16)
    for e in range(2):
        mg_out[:, :, e] = total[e * 1024 : (e + 1) * 1024].reshape(2, 8, 64, D)
        result[:, :, e] = final[e * 1024 : (e + 1) * 1024].reshape(2, 8, 64, D)
    for k, bo in enumerate((bo0, bo1, bo2, bo3)):
        for i in range(2):
            bo[i] = result[i, pl.ds((me ^ k) * 2, 2)].reshape(4, 64, D)
    stage[pl.ds(2 * D + 9, 1), :] = gain_grad
    split_pack(place, stage, send_out, keep_out)


def split_pack(place, stage, send_out, keep_out):
    rows = stage.shape[0] // 8
    for k in range(4):
        at = pl.ds(k * rows, rows)
        for out, core, first in ((send_out, 1 - place[1], place[3]), (keep_out, place[1], place[2])):
            start = pl.multiple_of((core * 4 + (first ^ k)) * rows, 16)
            out[at, :] = stage[pl.ds(start, rows), :].astype(jnp.bfloat16)


def back_kernel(
    place, normed, query, prob, att, mgrad, pat, pooled, kv,
    gains, wq, wsr, wkv, wout,
    query_grad, pooled_out, send_out, keep_out,
    stage,
):
    inside = image_mask(place)
    low = mgrad[...].astype(jnp.bfloat16)
    out_grad = mm_tn(att[...], low)
    mixed = jnp.where(inside, mm_nt(low, wout[...]), 0.0).astype(jnp.bfloat16)
    keys, values = (
        [
            block_pair(kv[pl.ds(i * 64, 64), pl.ds(n * D, D)].astype(jnp.float32)).astype(jnp.bfloat16)
            for i in range(2)
        ]
        for n in range(2)
    )
    parts = [slice(i * 1024, (i + 1) * 1024) for i in range(2)]
    weights = prob[...]
    back = jnp.concatenate([mm_nt(mixed[parts[i]], values[i]) for i in range(2)], axis=0)
    back = weights * (back - half_reduce(jnp.sum, weights * back, 0.0)) * SCORE_SCALE
    back = back.astype(jnp.bfloat16)
    grads = jnp.concatenate([mm(back[parts[i]], keys[i]) for i in range(2)], axis=0).astype(jnp.bfloat16)
    query_grad[...] = grads
    weights = weights.astype(jnp.bfloat16)
    left = halves((64, D))
    key_rows = []
    for i in range(2):
        value_full = mm_tn(weights[parts[i]], mixed[parts[i]])
        key_full = mm_tn(back[parts[i]], query[pl.ds(i * 1024, 1024), :])
        key_rows.append(
            jnp.concatenate(
                [
                    jnp.where(left, key_full[:64], key_full[64:]),
                    jnp.where(left, value_full[:64], value_full[64:]),
                ],
                axis=1,
            )
        )
    pair = jnp.concatenate(key_rows, axis=0).astype(jnp.bfloat16)
    unit, scale = norm_parts(pooled[...])
    reduced = (unit * gains[pl.ds(1, 1), :]).astype(jnp.bfloat16)
    kv_grad = mm_tn(reduced, pair)
    reduced_grad = mm_nt(pair, wkv[...])
    srg_grad = jnp.sum(reduced_grad * unit, axis=0, keepdims=True)
    pooled_low = norm_back(reduced_grad, gains[pl.ds(1, 1), :], unit, scale).astype(jnp.bfloat16)
    pooled_out[...] = pooled_low
    sr_grad = mm_tn(pat[...], pooled_low)
    each = PACK2 // 8
    for c in range(8):
        stage[pl.ds(c * each, 256), :] = sr_grad[c * 256 : (c + 1) * 256]
    for c in range(8):
        side, row = c // 4, (c % 4) * 32
        stage[pl.ds(c * each + 256, 32), :] = kv_grad[row : row + 32, side * D : (side + 1) * D]
        stage[pl.ds(c * each + 304, 16), :] = out_grad[c * 16 : (c + 1) * 16]
        stage[pl.ds(c * each + 320, 16), :] = jnp.zeros((16, D), jnp.float32)
    q_grad = mm_tn(normed[...], grads)
    weighted = q_grad * wq[...].astype(jnp.float32)
    for c in range(16):
        at = slice(c * D, (c + 1) * D)
        weighted += sr_grad[at] * wsr[pl.ds(c * D, D), :].astype(jnp.float32)
    high = weighted.astype(jnp.bfloat16)
    low = (weighted - high.astype(jnp.float32)).astype(jnp.bfloat16)
    ones = jnp.ones((16, D), jnp.bfloat16)
    gain_grad = (mm_nt(ones, high) + mm_nt(ones, low))[0:1] / gains[pl.ds(0, 1), :]
    for c in range(8):
        stage[pl.ds(c * each + 288, 16), :] = q_grad[c * 16 : (c + 1) * 16]
    stage[pl.ds(320, 1), :] = gain_grad
    stage[pl.ds(321, 1), :] = srg_grad
    split_pack(place, stage, send_out, keep_out)


def input_kernel(
    place, x, query_grad, pooled_low, mgrad, gains, wq, wsr,
    ig0, ig1, ig2, ig3,
    unfold, result,
):
    me = place[0]
    patch_grad = mm_nt(pooled_low[...], wsr[...])
    for i in range(2):
        for a in range(4):
            for u in range(4):
                for t in range(4):
                    unfold[pl.ds(i * 1024 + (4 * a + u) * 64 + t, 16, stride=4), :] = patch_grad[
                        i * 64 + a * 16 : i * 64 + a * 16 + 16, (u * 4 + t) * D : (u * 4 + t + 1) * D
                    ]
    grad = mm_nt(query_grad[...], wq[...]) + jnp.where(image_mask(place), unfold[...], 0.0)
    unit, scale = norm_parts(x[...].astype(jnp.float32))
    total = mgrad[...] + norm_back(grad, gains[pl.ds(0, 1), :], unit, scale)
    result[...] = total.astype(jnp.bfloat16).reshape(2, 16, 64, D)
    for k, ig in enumerate((ig0, ig1, ig2, ig3)):
        for i in range(2):
            ig[i] = result[i, pl.ds((me ^ k) * 4, 4)]


def call(kernel, scalars, arrays, outs, scratch, flops=0, name=None, vmem=24):
    spec = pl.BlockSpec(memory_space=VMEM)
    return pl.pallas_call(
        kernel,
        out_shape=[jax.ShapeDtypeStruct(shape, kind) for shape, kind in outs],
        in_specs=[pl.BlockSpec(memory_space=pltpu.SMEM)] * len(scalars) + [spec] * len(arrays),
        out_specs=[spec] * len(outs),
        scratch_shapes=scratch,
        compiler_params=pltpu.CompilerParams(vmem_limit_bytes=vmem * 2**20),
        cost_estimate=pl.CostEstimate(flops=flops, bytes_accessed=4 * 2**20, transcendentals=0),
        name=name,
    )(*scalars, *arrays)


BF, F32 = jnp.bfloat16, jnp.float32
FLAT = (2048, D)
SPLIT = (2, 8, 2, 64, D)
CHUNK = (2, 4, 64, D)
PACK1, PACK2 = 2176, 2688
FC, TB = 512, 1024
SCORE_SCALE = HEAD_DIM ** (-0.5)


def attend(place, chunks, gains, wq, wsr, wkv, wout):
    return call(
        attend_kernel,
        (place,),
        (*chunks, gains, wq, wsr, wkv, wout),
        [
            (FLAT, BF), (FLAT, BF), (FLAT, BF), (FLAT, F32), (FLAT, BF), (FLAT, F32),
            ((128, 2048), BF), ((128, D), F32), ((128, 2 * D), BF),
        ],
        [VMEM((2048, D), F32)],
        flops=10**9, name="attend",
    )


def feed(place, middle, chunks, gains, wfc1, taps, wfc2):
    return call(
        feed_kernel,
        (place,),
        (middle, *chunks, gains, wfc1, taps, wfc2),
        [(CHUNK, BF)] * 4 + [(SPLIT, F32), ((PACK1 // 2, D), BF), ((PACK1 // 2, D), BF)],
        [
            VMEM((2048, D), BF), VMEM((2048, D), BF), VMEM((D, 2048), BF), VMEM((2048, D), F32),
            VMEM((1152, 3 * D), BF), VMEM((1152, 3 * D), BF), VMEM((4, 3 * D, FF), BF),
            VMEM((4, 1024, 3 * D), BF), VMEM((4, 3 * D, 1024), BF), VMEM((4, 1024, FF), BF), VMEM((2048, FC), BF),
            VMEM((2048, D), F32), VMEM((4, 1152, 3 * D), F32), VMEM((PACK1, D), F32), VMEM(SPLIT, BF), VMEM(FLAT, F32), VMEM(FLAT, F32),
        ],
        flops=16 * 10**9, name="feed", vmem=44,
    )


def back(place, kept, mgrad, gains, wq, wsr, wkv, wout):
    _, normed, query, prob, att, _, pat, pooled, kv = kept
    return call(
        back_kernel,
        (place,),
        (normed, query, prob, att, mgrad, pat, pooled, kv, gains, wq, wsr, wkv, wout),
        [(FLAT, BF), ((128, D), BF), ((PACK2 // 2, D), BF), ((PACK2 // 2, D), BF)],
        [VMEM((PACK2, D), F32)],
        flops=2 * 10**9, name="back",
    )


def input_gradient(place, x, query_grad, pooled_low, mgrad, gains, wq, wsr):
    return call(
        input_kernel,
        (place,),
        (x, query_grad, pooled_low, mgrad, gains, wq, wsr),
        [(CHUNK, BF)] * 4,
        [VMEM((2048, D), F32), VMEM((2, 16, 64, D), BF)],
        flops=10**9, name="input_gradient",
    )


def over_rows(value, k):
    return lax.ppermute(value, "rows", [(i, i ^ k) for i in range(4)])


def over_four(value, k, phase):
    if phase == 1:
        k = 4 - k
    plane, line = (k >> 1) * 16 + (k & 1), 2 * k
    pairs = [(i, i ^ (plane if (i >> 3) & 1 == phase else line)) for i in range(32)]
    return lax.ppermute(value, ("rows", "batch"), pairs)


def plus(*values):
    return sum(v.astype(F32) for v in values).astype(BF)


def plane_parts(packs):
    halves_in = [plus(keep, over_rows(send, 1)) for send, keep in packs]
    return [
        jnp.concatenate([h[k * (h.shape[0] // 4) : (k + 1) * (h.shape[0] // 4)] for h in halves_in])
        for k in range(4)
    ]


def to_four(values, phase):
    return [over_four(values[k], k, phase) for k in (1, 2, 3)]


def finish_kernel(half, place, *refs):
    pieces, refs = refs[: 4 * (half + 1)], refs[4 * (half + 1) :]
    if half:
        refs = refs[6:]
    else:
        grads, refs = refs[:4], refs[4:]
    (q, sr, kv, out, fc1, fc2), refs = refs[:6], refs[6:]
    stage, small_dw, small_ln1, small_ln2, small_srg, sems = refs[-6:]
    copies = []

    def move(source, target):
        copies.append(pltpu.make_async_copy(source, target, sems.at[len(copies)]))
        copies[-1].start()

    def chunk_of(j):
        core, first = (place[1], place[2]) if j < 4 else (1 - place[1], place[3])
        return core * 4 + (first ^ (j % 4))

    if not half:
        for k in range(4):
            move(grads[k], refs[0].at[pl.ds(2 * (place[0] ^ k), 2)])
    for k in range(4):
        c = chunk_of(4 * half + k)
        stage[k] = pieces[4 * half + k][...].astype(F32)
        chan = pl.ds(pl.multiple_of(c * D, D), D)
        move(stage.at[k, pl.ds(0, D)], fc1.at[:, chan])
        move(stage.at[k, pl.ds(D, D)], fc2.at[chan])
        move(stage.at[k, pl.ds(272, 256)], sr.at[pl.ds(pl.multiple_of(c * 256, 256), 256)])
        row = pl.ds(pl.multiple_of((c % 4) * 32, 32), 32)
        move(stage.at[k, pl.ds(528, 32)], kv.at[row, pl.ds(pl.multiple_of((c // 4) * D, D), D)])
        row = pl.ds(pl.multiple_of(c * 16, 16), 16)
        move(stage.at[k, pl.ds(560, 16)], q.at[row])
        move(stage.at[k, pl.ds(576, 16)], out.at[row])
    if half:
        sums = [jnp.zeros((1, D), F32)] * 3
        for j, piece in enumerate(pieces):
            chan = pl.ds(pl.multiple_of(chunk_of(j) * D, D), D)
            small = piece[pl.ds(256, 16), :].astype(F32)
            for tap in range(9):
                small_dw[tap // 3, pl.ds(tap % 3, 1), chan] = small[tap : tap + 1]
            last = piece[pl.ds(592, 16), :].astype(F32)
            rows = (last[0:1], small[9:10], last[1:2])
            sums = [total + row for total, row in zip(sums, rows)]
        move(small_dw, refs[0])
        for ref, small, total in zip(refs[1:4], (small_ln1, small_ln2, small_srg), sums):
            small[...] = total.reshape(D)
            move(small, ref)
    for copy in copies:
        copy.wait()


def finish(place, pieces, earlier=(), grads=(), shape=None):
    far, near = pl.BlockSpec(memory_space=pl.ANY), pl.BlockSpec(memory_space=VMEM)
    half = 1 if earlier else 0
    shapes = [((D, D), F32), ((2048, D), F32), ((D, 2 * D), F32), ((D, D), F32), ((D, FF), F32), ((FF, D), F32)]
    specs, n = [far] * 6, len(shapes)
    if half:
        shapes += [((3, 3, FF), F32), ((D,), F32), ((D,), F32), ((D,), F32)]
        specs += [far] * 4
    else:
        shapes += [(shape, BF)]
        specs += [far]
    before = 1 + len(pieces) + len(grads)
    return pl.pallas_call(
        functools.partial(finish_kernel, half),
        out_shape=[jax.ShapeDtypeStruct(*each) for each in shapes],
        in_specs=[pl.BlockSpec(memory_space=pltpu.SMEM)] + [near] * (before - 1) + [far] * len(earlier),
        out_specs=specs,
        scratch_shapes=[
            VMEM((4, 608, D), F32), VMEM((3, 3, FF), F32), VMEM((D,), F32), VMEM((D,), F32), VMEM((D,), F32),
            pltpu.SemaphoreType.DMA((28,)),
        ],
        input_output_aliases={before + i: i for i in range(n)} if half else {},
        compiler_params=pltpu.CompilerParams(vmem_limit_bytes=8 * 2**20),
        cost_estimate=pl.CostEstimate(flops=0, bytes_accessed=4 * 2**20, transcendentals=0),
        name="finish",
    )(place, *pieces, *grads, *earlier)


def gather_kernel(place, part0, part1, part2, part3, out, sems):
    copies = [
        pltpu.make_async_copy(part, out.at[pl.ds(2 * (place[0] ^ k), 2)], sems.at[k])
        for k, part in enumerate((part0, part1, part2, part3))
    ]
    for copy in copies:
        copy.start()
    for copy in copies:
        copy.wait()


def gather_rows(place, parts, shape):
    far = pl.BlockSpec(memory_space=pl.ANY)
    return pl.pallas_call(
        gather_kernel,
        out_shape=jax.ShapeDtypeStruct(shape, BF),
        in_specs=[pl.BlockSpec(memory_space=pltpu.SMEM)] + [pl.BlockSpec(memory_space=VMEM)] * 4,
        out_specs=far,
        scratch_shapes=[pltpu.SemaphoreType.DMA((4,))],
        compiler_params=pltpu.CompilerParams(vmem_limit_bytes=4 * 2**20),
        name="gather_rows",
    )(place, *parts)


def image_shards(
    tokens, valid_rows, valid_cols, ln1_gain, q_weight, sr_weight, sr_gain, kv_weight, out_weight,
    ln2_gain, fc1_weight, dw_weight, fc2_weight, cotangent,
):
    me, lane = lax.axis_index("rows"), lax.axis_index("batch")
    core = me & 1
    plane, line = (me >> 1) * 2 + (lane & 1), lane >> 1
    first, second = jnp.where(core == 0, plane, line), jnp.where(core == 0, line, plane)
    sizes = [lax.dynamic_slice_in_dim(v, 2 * me, 2) for v in (valid_rows, valid_cols)]
    place = jnp.concatenate([jnp.stack([me, core, first, second]), *sizes]).astype(jnp.int32)

    def spread(source):
        near = {
            k: over_rows(lax.dynamic_slice_in_dim(source, 2 * (me ^ k), 2, 0), k) for k in (3, 2, 1)
        }
        return source, near[1], near[2], near[3]

    def returned(parts):
        near = {k: over_rows(parts[k], k) for k in (3, 2, 1)}
        return [parts[0], near[1], near[2], near[3]]

    gains = jnp.stack([ln1_gain, sr_gain, ln2_gain])
    row0, row1, row2 = dw_weight.astype(F32)
    taps = jnp.concatenate(
        [row0, 0.5 * (row0 + row1 + row2), 0.5 * (row0 - row1 + row2), row2, jnp.zeros((4, FF), F32)]
    )
    token_parts = spread(tokens)
    cotangent, _ = lax.optimization_barrier((cotangent, token_parts[1]))
    kept = attend(
        place, token_parts, gains, q_weight, sr_weight, kv_weight, out_weight
    )
    *block_parts, mgrad, send1, keep1 = feed(
        place, kept[5].reshape(SPLIT), spread(cotangent), gains, fc1_weight, taps, fc2_weight
    )
    mgrad = mgrad.reshape(FLAT)
    query_grad, pooled_low, send2, keep2 = back(
        place, kept, mgrad, gains, q_weight, sr_weight, kv_weight, out_weight
    )
    parts = plane_parts([(send1, keep1), (send2, keep2)])
    block = returned(block_parts)
    inputs = input_gradient(place, kept[0], query_grad, pooled_low, mgrad, gains, q_weight, sr_weight)
    mine, inputs = lax.optimization_barrier((plus(parts[0], *to_four(parts, 0)), list(inputs)))
    inputs = returned(inputs)
    mine, block[2] = lax.optimization_barrier((mine, block[2]))
    got = [g.astype(F32) for g in to_four([mine] * 4, 1)]
    got, block_out = lax.optimization_barrier((got, gather_rows(place, block, tokens.shape)))
    got, inputs[1], inputs[2] = lax.optimization_barrier((got, inputs[1], inputs[2]))
    total = ((mine.astype(F32) + got[2]) + (got[1] + got[0])).astype(BF)
    got = to_four([total] * 4, 0)
    got, inputs[3] = lax.optimization_barrier((got, inputs[3]))
    pieces = (total, *got)
    others = tuple(over_rows(piece, 1) for piece in pieces)
    *half, input_grad = finish(place, pieces, (), inputs, tokens.shape)
    q, sr, kv, out, fc1, fc2, dw, ln1_sum, ln2_sum, srg_sum = finish(place, pieces + others, half)
    return block_out, input_grad, ln1_sum, q, sr, srg_sum, kv, out, ln2_sum, fc1, dw, fc2


def shards(*arrays):
    tokens = arrays[0]
    fits = (
        lax.axis_size("rows") == 4
        and lax.axis_size("batch") == 8
        and tokens.shape == (8, 4, 64, D)
    )
    return image_shards(*arrays) if fits else row_shards(*arrays)


def solution(mesh):
    placed = (
        P("batch", "rows", None, None),
        P("batch"),
        P("batch"),
        P(),
        P(),
        P(),
        P(),
        P(),
        P(),
        P(),
        P(),
        P(),
        P(),
        P("batch", "rows", None, None),
    )
    return jax.shard_map(
        shards,
        mesh=mesh,
        in_specs=placed,
        out_specs=(
            P("batch", "rows", None, None),
            P("batch", "rows", None, None),
            P(),
            P(),
            P(),
            P(),
            P(),
            P(),
            P(),
            P(),
            P(),
            P(),
        ),
        check_vma=False,
    )
```
